32 devices in a mesh: fsdp: 16 (over z, y, x), rep: 2 (over core).
Axes of the slice: x: 2, y: 2, z: 4, core: 2. Of those that a mesh axis runs over, the one named last changes fastest.
Arguments:
- frames: bfloat16 [64, 16, 5, 3, 49], P(('fsdp', 'rep')), may hold values from -6 to 6
- features: bfloat16 [64, 16, 49, 2048], P(('fsdp', 'rep')), may hold values from -6 to 6
- seg_counts: int32 [64], P(('fsdp', 'rep')), may hold values from 8 to 16, as said below
- stem_weight: bfloat16 [64, 588], P('fsdp'), may hold values from -0.25 to 0.25
- stem_gain: bfloat16 [64], P('fsdp'), may hold values from 0.5 to 1.5
- stem_shift: bfloat16 [64], P('fsdp'), may hold values from -3 to 3
- lateral: bfloat16 [64, 2048], P('fsdp'), may hold values from -0.75 to 0.75
- reduce_weight: bfloat16 [2048, 512], P('fsdp'), may hold values from -0.125 to 0.125
- gain_one: bfloat16 [512], P('fsdp'), may hold values from 0.5 to 1.5
- shift_one: bfloat16 [512], P('fsdp'), may hold values from -3 to 3
- diff_weight: bfloat16 [2, 4608, 512], P(None, 'fsdp'), may hold values from -0.09375 to 0.09375
- gate_shift: bfloat16 [512], P('fsdp'), may hold values from -3 to 3
- mid_weight: bfloat16 [4608, 512], P('fsdp'), may hold values from -0.09375 to 0.09375
- gain_two: bfloat16 [512], P('fsdp'), may hold values from 0.5 to 1.5
- shift_two: bfloat16 [512], P('fsdp'), may hold values from -3 to 3
- expand_weight: bfloat16 [512, 2048], P('fsdp'), may hold values from -0.25 to 0.25
- gain_three: bfloat16 [2048], P('fsdp'), may hold values from 0.5 to 1.5
- shift_three: bfloat16 [2048], P('fsdp'), may hold values from -3 to 3
- pooled_grad: bfloat16 [64, 49, 2048], P(('fsdp', 'rep')), may hold values from -6 to 6
Outputs:
- pooled: bfloat16 [64, 49, 2048], P(('fsdp', 'rep'))
- features_grad: float32 [64, 16, 49, 2048], P(('fsdp', 'rep'))
- stem_weight_grad: float32 [64, 588], P('fsdp')
- stem_gain_grad: float32 [64], P('fsdp')
- stem_shift_grad: float32 [64], P('fsdp')
- lateral_grad: float32 [64, 2048], P('fsdp')
- reduce_grad: float32 [2048, 512], P('fsdp')
- gain_one_grad: float32 [512], P('fsdp')
- shift_one_grad: float32 [512], P('fsdp')
- diff_grad: float32 [2, 4608, 512], P(None, 'fsdp')
- gate_grad: float32 [512], P('fsdp')
- mid_grad: float32 [4608, 512], P('fsdp')
- gain_two_grad: float32 [512], P('fsdp')
- shift_two_grad: float32 [512], P('fsdp')
- expand_grad: float32 [512, 2048], P('fsdp')
- gain_three_grad: float32 [2048], P('fsdp')
- shift_three_grad: float32 [2048], P('fsdp')
The draws below stay inside these ranges and needn't reach their ends.
Inputs may be any that keep to these rules, and one draw needn't show every extreme that they name: `seg_counts`: each clip has 8 or 16 true segments, both counts occurring in every draw.
All inputs are finite; a program needn't handle non-finite values.
Results may differ from the reference program's by a relative error of at most 0.015.
Values may be sent and summed in bfloat16 or wider, within the bound.
A program may use at most 448 MiB of HBM per device.

```python
import jax
import jax.numpy as jnp
from jax import lax

WIDTH = 2048
MID = 512
STEM = 64
RGB = 3
FRAMES = 5
GRID = 7
SEG = 16
DIFFS = 588
CLIPS = 64


def draw_seg_counts(key, part):
    key = jax.random.fold_in(key, 11)
    halves = jax.random.randint(key, (CLIPS,), 0, 2)
    ranking = jax.random.permutation(jax.random.fold_in(key, 1), CLIPS)
    halves = jnp.where(ranking == 0, 1, jnp.where(ranking == 1, 0, halves))
    return (SEG // 2 * (1 + halves)).astype(jnp.int32)


def level_of(rng, shape, split, least, largest):
    def one(position, shards_of):
        draws = jax.random.uniform(jax.random.fold_in(jax.random.fold_in(rng, 6), position), (shards_of,), jnp.float32, least / len(split), largest / len(split))
        return jnp.repeat(jnp.exp(draws), shape[position] // shards_of).reshape((-1,) + (1,) * (len(shape) - position - 1))

    loudness = one(*split[0])
    for cut in split[1:]:
        loudness = loudness * one(*cut)
    return loudness


def noise(own_key, shape, spread, most, split=(), kind=jnp.bfloat16):
    loudness = level_of(own_key, shape, split, -0.22, 0.18) if split else 1.0
    entries = jax.random.normal(own_key, shape, jnp.float32) * spread * loudness
    return jnp.minimum(jnp.maximum(entries, -most), most).astype(kind)


def setup_inputs(seed: int = 0) -> dict:
    keys = jax.random.split(jax.random.key(seed), 20)
    return {
        "frames": noise(keys[0], (CLIPS, SEG, FRAMES, RGB, GRID * GRID), 1.0, 6.0, ((0, 32),)),
        "features": noise(keys[1], (CLIPS, SEG, GRID * GRID, WIDTH), 1.0, 6.0, ((0, 32),)),
        "seg_counts": draw_seg_counts(jax.random.fold_in(keys[19], 71), 0),
        "stem_weight": noise(keys[3], (STEM, DIFFS), DIFFS ** -0.5, 0.25, ((0, 16),)),
        "stem_gain": jnp.clip(1.0 + 0.1 * jax.random.normal(keys[4], (STEM,), jnp.float32), 0.5, 1.5).astype(jnp.bfloat16),
        "stem_shift": noise(keys[5], (STEM,), 0.5, 3.0, ((0, 16),)),
        "lateral": noise(keys[6], (STEM, WIDTH), STEM ** -0.5, 0.75, ((0, 16),)),
        "reduce_weight": noise(keys[7], (WIDTH, MID), WIDTH ** -0.5, 0.125, ((0, 16),)),
        "gain_one": jnp.clip(1.0 + 0.1 * jax.random.normal(keys[8], (MID,), jnp.float32), 0.5, 1.5).astype(jnp.bfloat16),
        "shift_one": noise(keys[9], (MID,), 0.5, 3.0, ((0, 16),)),
        "diff_weight": noise(keys[10], (2, 9 * MID, MID), (9 * MID) ** -0.5, 0.09375, ((1, 16),)),
        "gate_shift": noise(keys[11], (MID,), 0.5, 3.0, ((0, 16),)),
        "mid_weight": noise(keys[12], (9 * MID, MID), (9 * MID) ** -0.5, 0.09375, ((0, 16),)),
        "gain_two": jnp.clip(1.0 + 0.1 * jax.random.normal(keys[13], (MID,), jnp.float32), 0.5, 1.5).astype(jnp.bfloat16),
        "shift_two": noise(keys[14], (MID,), 0.5, 3.0, ((0, 16),)),
        "expand_weight": noise(keys[15], (MID, WIDTH), MID ** -0.5, 0.25, ((0, 16),)),
        "gain_three": jnp.clip(1.0 + 0.1 * jax.random.normal(keys[16], (WIDTH,), jnp.float32), 0.5, 1.5).astype(jnp.bfloat16),
        "shift_three": noise(keys[17], (WIDTH,), 0.5, 3.0, ((0, 16),)),
        "pooled_grad": noise(keys[18], (CLIPS, GRID * GRID, WIDTH), 1.0, 6.0, ((0, 32),)),
    }


epsilon = 1e-05
highest = lax.Precision.HIGHEST

@jax.custom_vjp
def low(v):
    return lax.optimization_barrier(v.astype(jnp.bfloat16)).astype(jnp.float32)

@jax.custom_vjp
def low_back(v):
    return v

def low_keep(v):
    return (low(v), None)

def low_pass(kept, grad):
    return (grad,)

def back_keep(v):
    return (v, None)

def back_low(kept, grad):
    return (low(grad),)
low.defvjp(low_keep, low_pass)
low_back.defvjp(back_keep, back_low)

def patches(source, half_span, stride):
    batch_rows = source.shape[0]
    channels = source.shape[-1]
    square = source.reshape(batch_rows, GRID, GRID, channels)
    margin = half_span * stride
    padded = jnp.pad(square, ((0, 0), (margin, margin), (margin, margin), (0, 0)))
    pieces = []
    for row_off in range(-half_span, half_span + 1):
        for col_off in range(-half_span, half_span + 1):
            row_start = margin + row_off * stride
            col_start = margin + col_off * stride
            pieces.append(padded[:, row_start:row_start + GRID, col_start:col_start + GRID, :])
    return jnp.concatenate(pieces, axis=-1).reshape(batch_rows, GRID * GRID, -1)

def pool_mean(source):
    batch_rows, pixels, channels = source.shape
    return lax.optimization_barrier(jnp.sum(patches(source, 1, 1).reshape(batch_rows, pixels, 9, channels), axis=2)) / 9.0

def convolve(source, weight, half_span, stride):
    blocks = source.reshape(-1, SEG, source.shape[1], source.shape[2])

    def one_block(piece):
        return jnp.einsum('bpk,kd->bpd', patches(piece, half_span, stride), weight, precision=highest)
    result = lax.map(jax.checkpoint(one_block), blocks)
    return result.reshape(source.shape[0], source.shape[1], -1)

def project(source, weight):
    return jnp.einsum('bpc,cd->bpd', source, weight, precision=highest)

def normalize(values, row_valid, row_total, gain_vec, shift_vec):
    centre = lax.optimization_barrier(jnp.sum(values * row_valid, axis=(0, 1))) / row_total
    centred = values - centre
    variance = lax.optimization_barrier(jnp.sum(centred * centred * row_valid, axis=(0, 1))) / row_total
    return row_valid * (gain_vec * centred * lax.rsqrt(variance + epsilon) + shift_vec)

def reference(frames, features, seg_counts, stem_weight, stem_gain, stem_shift, lateral, reduce_weight, gain_one, shift_one, diff_weight, gate_shift, mid_weight, gain_two, shift_two, expand_weight, gain_three, shift_three, pooled_grad):
    clip_count = features.shape[0]
    slot_total = clip_count * SEG
    pixels = GRID * GRID
    seg_index = lax.broadcasted_iota(jnp.int32, (clip_count, SEG), 1)
    valid_seg = (seg_index < seg_counts[:, None]).astype(jnp.float32)
    pair_valid = valid_seg * jnp.concatenate([valid_seg[:, 1:], jnp.zeros((clip_count, 1), jnp.float32)], axis=1)
    row_valid = jnp.broadcast_to(valid_seg.reshape(slot_total, 1, 1), (slot_total, pixels, 1))
    count_float = seg_counts.astype(jnp.float32)
    row_total = jnp.sum(count_float) * pixels
    moving = frames.astype(jnp.float32)
    motion = (moving[:, :, 1:] - moving[:, :, :-1]) * valid_seg[:, :, None, None, None]
    motion = low(jnp.transpose(motion, (0, 1, 4, 2, 3)).reshape(slot_total, pixels, -1))
    params = (features.astype(jnp.float32), stem_weight.astype(jnp.float32), stem_gain.astype(jnp.float32), stem_shift.astype(jnp.float32), lateral.astype(jnp.float32), reduce_weight.astype(jnp.float32), gain_one.astype(jnp.float32), shift_one.astype(jnp.float32), diff_weight.astype(jnp.float32), gate_shift.astype(jnp.float32), mid_weight.astype(jnp.float32), gain_two.astype(jnp.float32), shift_two.astype(jnp.float32), expand_weight.astype(jnp.float32), gain_three.astype(jnp.float32), shift_three.astype(jnp.float32))

    def forward(weights):
        feature_in, stem_kernel, stem_gains, stem_shifts, lateral_map, reduce_map, gains_one, shifts_one, diff_maps, gate_shifts, mid_map, gains_two, shifts_two, expand_map, gains_three, shifts_three = weights
        stem_pre = low_back(convolve(motion, stem_kernel.T, 3, 1))
        stem_act = jax.nn.gelu(normalize(stem_pre, row_valid, row_total, stem_gains, stem_shifts))
        stem_pool = low(pool_mean(stem_act))
        block_in = feature_in.reshape(slot_total, pixels, WIDTH) + low_back(project(stem_pool, lateral_map))
        block_low = low(block_in)
        reduced = low_back(project(block_low, reduce_map))
        act_one = jax.nn.gelu(normalize(reduced, row_valid, row_total, gains_one, shifts_one))
        act_grid = act_one.reshape(clip_count, SEG, pixels, MID)
        later = jnp.concatenate([act_grid[:, 1:], jnp.zeros((clip_count, 1, pixels, MID), jnp.float32)], axis=1)
        change = low(((later - act_grid) * pair_valid[:, :, None, None]).reshape(slot_total, pixels, MID))
        gate_pre = low_back(convolve(change, diff_maps[0], 1, 1) + convolve(change, diff_maps[1], 1, 2))
        gate = jax.nn.sigmoid(gate_pre + gate_shifts)
        modulated = low(act_one * (1.0 + gate))
        middle = low_back(convolve(modulated, mid_map, 1, 1))
        act_two = low(jax.nn.gelu(normalize(middle, row_valid, row_total, gains_two, shifts_two)))
        expanded = low_back(project(act_two, expand_map))
        block_out = jax.nn.gelu(block_in + normalize(expanded, row_valid, row_total, gains_three, shifts_three))
        summed = lax.optimization_barrier(jnp.sum(block_out.reshape(clip_count, SEG, pixels, WIDTH) * valid_seg[:, :, None, None], axis=1))
        return summed / count_float[:, None, None]
    pooled, pull_back = jax.vjp(forward, params)
    grads, = pull_back(pooled_grad.astype(jnp.float32))
    return (pooled.astype(jnp.bfloat16), grads[0], grads[1], grads[2], grads[3], grads[4], grads[5], grads[6], grads[7], grads[8], grads[9], grads[10], grads[11], grads[12], grads[13], grads[14], grads[15])
```

```python
import functools

import jax
import jax.numpy as jnp
from jax import lax
from jax.experimental import pallas as pl
from jax.experimental.pallas import tpu as pltpu
from jax.sharding import PartitionSpec as P

GRID = 7
PIXELS = GRID * GRID
epsilon = 1e-05
MESH = pl.DeviceIdType.MESH
ANY = pl.BlockSpec(memory_space=pl.ANY)
IN_VMEM = pl.BlockSpec(memory_space=pltpu.VMEM)
VMEM_LIMIT = 60 * 1024 * 1024
bf16 = jnp.bfloat16
f32 = jnp.float32
DMA = pltpu.SemaphoreType.DMA


def factor_three(size):
    best = None
    for b in range(1, size + 1):
        for c in range(1, b + 1):
            if size % (b * c) == 0 and size // (b * c) >= b:
                a = size // (b * c)
                if best is None or a + b + c < sum(best):
                    best = (a, b, c)
    return best


class Place:
    def __init__(self, dims, reps, rep=None):
        self.dims, self.reps = dims, reps
        size_a, size_b, size_c = dims
        self.me = lax.axis_index("fsdp")
        self.rep = lax.axis_index("rep") if rep is None else rep
        ib, ic = (self.me // size_c) % size_b, self.me % size_c
        self.ia = self.me // (size_b * size_c)
        odd = self.rep % 2 if size_b == size_c else 0
        self.stride_u = size_c * (1 - odd) + odd
        self.stride_v = (1 - odd) + size_c * odd
        self.iu = ib * (1 - odd) + ic * odd
        self.iv = ic * (1 - odd) + ib * odd

    def at(self, da, du, dv):
        size_a, size_b, size_c = self.dims
        a = (self.ia + da + size_a) % size_a
        u = (self.iu + du + size_b) % size_b
        v = (self.iv + dv + size_c) % size_c
        return a * (size_b * size_c) + u * self.stride_u + v * self.stride_v

    def greet(self):
        size_a, size_b, size_c = self.dims
        peers = [(self.at(d, 0, 0), self.rep) for d in range(1, size_a)]
        peers += [(self.at(0, d, 0), self.rep) for d in range(1, size_b)]
        peers += [(self.at(0, 0, d), self.rep) for d in range(1, size_c)]
        peers += [(self.me, (self.rep + d) % self.reps) for d in range(1, self.reps)]
        greet(peers)


def greet(peers):
    barrier = pltpu.get_barrier_semaphore()
    for target, rep in peers:
        pl.semaphore_signal(
            barrier, inc=1, device_id={"fsdp": target, "rep": rep}, device_id_type=MESH
        )
    pl.semaphore_wait(barrier, len(peers))


def remote(src, dst, sems, target, rep):
    return pltpu.make_async_remote_copy(
        src_ref=src,
        dst_ref=dst,
        send_sem=sems.at[0],
        recv_sem=sems.at[1],
        device_id={"fsdp": target, "rep": rep},
        device_id_type=MESH,
    )


def columns(width, which):
    start = which * width
    return pl.ds(start if isinstance(start, int) else pl.multiple_of(start, width), width)


def views(refs):
    out = []
    for ref, stacked in refs:
        out += [ref.at[j] for j in range(ref.shape[0])] if stacked else [ref]
    return out


def gather_kernel(dims, reps, stacked, *refs):
    number = len(stacked)
    shards = views(zip(refs[:number], stacked))
    fulls = views(zip(refs[number : 2 * number], stacked))
    own_sem, a_sem, b_sem, c_sem, r_sem = refs[2 * number :]
    count = len(shards)
    size_a, size_b, size_c = dims
    place = Place(dims, reps)
    me, rep = place.me, place.rep
    place.greet()
    waits = []

    def slot(k, index, which):
        return fulls[k].at[index, :, columns(fulls[k].shape[-1] // reps, which)]

    def push(k, da, du, dv, target, target_rep, sems):
        index = place.at(-da, -du, -dv)
        if (da, du, dv) == (0, 0, 0):
            source = shards[k].at[:, columns(shards[k].shape[-1] // reps, rep)]
        else:
            source = slot(k, index, rep)
        copy = remote(source, slot(k, index, rep), sems, target, target_rep)
        copy.start()
        waits.append(copy)

    def landed(k, da, du, dv, which, sems):
        there = slot(k, place.at(-da, -du, -dv), which)
        remote(there, there, sems, me, rep).wait_recv()

    def forward(k, da, du, dv):
        if dv == 0 and du == 0:
            for d in range(1, size_b):
                push(k, da, 0, 0, place.at(0, d, 0), rep, b_sem.at[k, da, d - 1])
        if dv == 0:
            for d in range(1, size_c):
                push(k, da, du, 0, place.at(0, 0, d), rep, c_sem.at[k, da, du, d - 1])
        if (da, du, dv) != (0, 0, 0):
            for d in range(1, reps):
                push(k, da, du, dv, me, (rep + d) % reps, r_sem.at[k, da, du, dv, d - 1])

    local = []
    for k in range(count):
        copy = pltpu.make_async_copy(shards[k], fulls[k].at[me], own_sem.at[k])
        copy.start()
        local.append(copy)
    for k in range(count):
        for d in range(1, size_a):
            push(k, 0, 0, 0, place.at(d, 0, 0), rep, a_sem.at[k, d - 1])
        forward(k, 0, 0, 0)
    for k in range(count):
        for da in range(1, size_a):
            landed(k, da, 0, 0, rep, a_sem.at[k, da - 1])
            forward(k, da, 0, 0)
        for du in range(1, size_b):
            for da in range(size_a):
                landed(k, da, du, 0, rep, b_sem.at[k, da, du - 1])
                forward(k, da, du, 0)
        for dv in range(1, size_c):
            for du in range(size_b):
                for da in range(size_a):
                    landed(k, da, du, dv, rep, c_sem.at[k, da, du, dv - 1])
                    forward(k, da, du, dv)
    for k in range(count):
        for dv in range(size_c):
            for du in range(size_b):
                for da in range(size_a):
                    if (da, du, dv) != (0, 0, 0):
                        for d in range(1, reps):
                            landed(k, da, du, dv, (rep + reps - d) % reps, r_sem.at[k, da, du, dv, d - 1])
    for copy in waits:
        copy.wait_send()
    for copy in local:
        copy.wait()


def gather_all(shards, fsdp, reps, collective_id, name):
    dims = factor_three(fsdp)
    size_a, size_b, size_c = dims
    stacked = [s.ndim == 3 for s in shards]
    count = sum(s.shape[0] if s.ndim == 3 else 1 for s in shards)
    return pl.pallas_call(
        functools.partial(gather_kernel, dims, reps, stacked),
        out_shape=[
            jax.ShapeDtypeStruct(s.shape[:-2] + (fsdp,) + s.shape[-2:], s.dtype) for s in shards
        ],
        in_specs=[ANY] * len(shards),
        out_specs=[ANY] * len(shards),
        scratch_shapes=[
            DMA((count,)),
            DMA((count, max(size_a - 1, 1), 2)),
            DMA((count, size_a, max(size_b - 1, 1), 2)),
            DMA((count, size_a, size_b, max(size_c - 1, 1), 2)),
            DMA((count, size_a, size_b, size_c, max(reps - 1, 1), 2)),
        ],
        compiler_params=pltpu.CompilerParams(
            collective_id=collective_id, has_side_effects=True, vmem_limit_bytes=VMEM_LIMIT
        ),
        name=name,
    )(*shards)


def scatter_kernel(dims, reps, stacked, *refs):
    number = len(stacked)
    partials = views(zip(refs[:number], stacked))
    totals = views(zip(refs[number : 2 * number], stacked))
    count = len(partials)
    rest = refs[2 * number :]
    held, from_rep, from_v, from_u, from_a, share = (rest[i * count : (i + 1) * count] for i in range(6))
    own_sem, r_sem, v_sem, u_sem, a_sem, s_sem = rest[6 * count :]
    size_a, size_b, size_c = dims
    place = Place(dims, reps)
    me, rep = place.me, place.rep
    place.greet()
    waits = []

    def push(source, there, sems, target, target_rep):
        copy = remote(source, there, sems, target, target_rep)
        copy.start()
        waits.append(copy)

    def landed(there, sems):
        remote(there, there, sems, me, rep).wait_recv()

    def order():
        for dv in list(range(1, size_c)) + [0]:
            for du in list(range(1, size_b)) + [0]:
                for da in list(range(1, size_a)) + [0]:
                    yield da, du, dv

    local = {}
    for k in range(count):
        width = partials[k].shape[-1] // reps
        for da, du, dv in order():
            for d in range(1, reps):
                other = (rep + d) % reps
                index = Place(dims, reps, other).at(da, du, dv)
                push(
                    partials[k].at[index, :, columns(width, other)],
                    from_rep[k].at[d - 1, index],
                    r_sem.at[k, da, du, dv, d - 1],
                    me,
                    other,
                )
            index = place.at(da, du, dv)
            copy = pltpu.make_async_copy(
                partials[k].at[index, :, columns(width, rep)],
                held[k].at[index],
                own_sem.at[k, da, du, dv],
            )
            copy.start()
            local[k, da, du, dv] = copy

    for k in range(count):
        for da, du, dv in order():
            index = place.at(da, du, dv)
            local[k, da, du, dv].wait()
            total = held[k][index].astype(f32)
            for d in range(1, reps):
                landed(from_rep[k].at[d - 1, index], r_sem.at[k, da, du, dv, d - 1])
                total = total + from_rep[k][d - 1, index].astype(f32)
            if dv == 0:
                for e in range(1, size_c):
                    landed(from_v[k].at[e - 1, da, du], v_sem.at[k, da, du, e - 1])
                    total = total + from_v[k][e - 1, da, du].astype(f32)
                if du == 0:
                    for e in range(1, size_b):
                        landed(from_u[k].at[e - 1, da], u_sem.at[k, da, e - 1])
                        total = total + from_u[k][e - 1, da].astype(f32)
                    if da == 0:
                        for e in range(1, size_a):
                            landed(from_a[k].at[e - 1], a_sem.at[k, e - 1])
                            total = total + from_a[k][e - 1].astype(f32)
            if (da, du, dv) == (0, 0, 0):
                share[k][rep] = total.astype(bf16)
                for d in range(1, reps):
                    push(share[k].at[rep], share[k].at[rep], s_sem.at[k, d - 1], me, (rep + d) % reps)
                continue
            held[k][index] = total.astype(bf16)
            if dv:
                push(held[k].at[index], from_v[k].at[dv - 1, da, du], v_sem.at[k, da, du, dv - 1], place.at(0, 0, dv), rep)
            elif du:
                push(held[k].at[index], from_u[k].at[du - 1, da], u_sem.at[k, da, du - 1], place.at(0, du, 0), rep)
            else:
                push(held[k].at[index], from_a[k].at[da - 1], a_sem.at[k, da - 1], place.at(da, 0, 0), rep)
    for k in range(count):
        width = partials[k].shape[-1] // reps
        for d in range(1, reps):
            landed(share[k].at[(rep + reps - d) % reps], s_sem.at[k, d - 1])
        for which in range(reps):
            totals[k][:, which * width : (which + 1) * width] = share[k][which].astype(f32)
    for copy in waits:
        copy.wait_send()


def scatter_all(partials, fsdp, reps, collective_id, name):
    dims = factor_three(fsdp)
    size_a, size_b, size_c = dims
    stacked = [p.ndim == 4 for p in partials]
    shapes = []
    for p in partials:
        shapes += [(p.shape[-2], p.shape[-1] // reps)] * (p.shape[0] if p.ndim == 4 else 1)
    count = len(shapes)

    def buffers(*lead):
        return [pltpu.VMEM(lead + shape, bf16) for shape in shapes]

    return pl.pallas_call(
        functools.partial(scatter_kernel, dims, reps, stacked),
        out_shape=[
            jax.ShapeDtypeStruct(p.shape[:-3] + p.shape[-2:], f32) for p in partials
        ],
        in_specs=[ANY] * len(partials),
        out_specs=[IN_VMEM] * len(partials),
        scratch_shapes=buffers(fsdp)
        + buffers(max(reps - 1, 1), fsdp)
        + buffers(max(size_c - 1, 1), size_a, size_b)
        + buffers(max(size_b - 1, 1), size_a)
        + buffers(max(size_a - 1, 1))
        + buffers(reps)
        + [
            DMA((count, size_a, size_b, size_c)),
            DMA((count, size_a, size_b, size_c, max(reps - 1, 1), 2)),
            DMA((count, size_a, size_b, max(size_c - 1, 1), 2)),
            DMA((count, size_a, max(size_b - 1, 1), 2)),
            DMA((count, max(size_a - 1, 1), 2)),
            DMA((count, max(reps - 1, 1), 2)),
        ],
        compiler_params=pltpu.CompilerParams(
            collective_id=collective_id, has_side_effects=True, vmem_limit_bytes=VMEM_LIMIT
        ),
        name=name,
    )(*partials)


def stage_sizes(devices):
    sizes = []
    while devices > 1:
        size = next(s for s in (8, 4, 2, 7, 5, 3, devices) if devices % s == 0)
        sizes.append(size)
        devices //= size
    return sizes


def exchange_kernel(sizes, reps, moments, *refs):
    rows = 3 if moments else 2
    sources, results = refs[:rows], refs[rows : 2 * rows]
    mine, slots, sems = refs[2 * rows], refs[2 * rows + 1 : -1], refs[-1]
    place = lax.axis_index("fsdp") * reps + lax.axis_index("rep")
    stages = []
    stride = 1
    for size in sizes:
        position = (place // stride) % size
        peers = []
        for d in range(1, size):
            target = place + ((position + d) % size - position) * stride
            peers.append((target // reps, target % reps))
        stages.append((size, position, peers))
        stride *= size
    greet([peer for stage in stages for peer in stage[2]])
    current = [source[...] for source in sources]
    waits = []
    for index, (size, position, peers) in enumerate(stages):
        for row, value in enumerate(current):
            mine[index, row : row + 1] = value
        slots[index][position] = mine[index]
        for d, (target, rep) in enumerate(peers, 1):
            copy = remote(mine.at[index], slots[index].at[position], sems.at[index, d - 1], target, rep)
            copy.start()
            waits.append(copy)
        for d, (target, rep) in enumerate(peers, 1):
            there = slots[index].at[(position + size - d) % size]
            remote(there, there, sems.at[index, d - 1], target, rep).wait_recv()
        parts = [[slots[index][j, row : row + 1] for row in range(rows)] for j in range(size)]
        current = [functools.reduce(jnp.add, [part[row] for part in parts]) for row in range(rows)]
        if moments:
            centre = current[0] / current[2]
            squares = current[1]
            for part in parts:
                off = part[0] / part[2] - centre
                squares = squares + part[2] * off * off
            current[1] = squares
    for result, value in zip(results, current):
        result[...] = value
    for copy in waits:
        copy.wait_send()


def exchange(rows, fsdp, reps, moments, collective_id, name):
    sizes = stage_sizes(fsdp * reps)
    width = rows[0].shape[-1]
    return pl.pallas_call(
        functools.partial(exchange_kernel, sizes, reps, moments),
        out_shape=[jax.ShapeDtypeStruct((1, width), f32)] * len(rows),
        in_specs=[IN_VMEM] * len(rows),
        out_specs=[IN_VMEM] * len(rows),
        scratch_shapes=[pltpu.VMEM((len(sizes), 8, width), f32)]
        + [pltpu.VMEM((size, 8, width), f32) for size in sizes]
        + [DMA((len(sizes), max(max(sizes) - 1, 1), 2))],
        compiler_params=pltpu.CompilerParams(
            collective_id=collective_id, has_side_effects=True, vmem_limit_bytes=VMEM_LIMIT
        ),
        name=name,
    )(*[row.reshape(1, width) for row in rows])


ORDER = ("HWNC", "HWIO", "HWNC")


def pad_of(span):
    return ((span, span), (span, span))


def convolve(source, weight, span, stride):
    side = 2 * span + 1
    kernel = weight.reshape(side, side, source.shape[-1], -1)
    return lax.conv_general_dilated(
        source, kernel, (1, 1), pad_of(span * stride), rhs_dilation=(stride, stride),
        dimension_numbers=ORDER, preferred_element_type=f32,
    )


def convolve_back(grads, weight, span, stride):
    side = 2 * span + 1
    kernel = weight.reshape(side, side, -1, grads.shape[-1])[::-1, ::-1]
    return lax.conv_general_dilated(
        grads, kernel, (1, 1), pad_of(span * stride), rhs_dilation=(stride, stride),
        dimension_numbers=("HWNC", "HWOI", "HWNC"), preferred_element_type=f32,
    )


def convolve_terms(source, grads, span, stride, kind):
    return lax.conv_general_dilated(
        source, grads, (stride, stride), pad_of(span * stride),
        dimension_numbers=("HWCN", "HWIO", "HWNC"), preferred_element_type=kind,
    )


def pool_mean(source):
    total = lax.reduce_window(source, 0.0, lax.add, (3, 3, 1, 1), (1, 1, 1, 1), "SAME")
    return total / 9.0


def project(source, weight):
    return jnp.einsum("yxnc,cd->yxnd", source, weight, preferred_element_type=f32)


def project_back(grads, weight):
    return jnp.einsum("yxnd,cd->yxnc", grads, weight, preferred_element_type=f32)


def project_terms(source, grads, kind):
    return jnp.einsum("yxnc,yxnd->cd", source, grads, preferred_element_type=kind)


def gelu_back(pre_act, grads):
    return jax.vjp(jax.nn.gelu, pre_act)[1](grads)[0]


def make_shards(fsdp, reps):
    def shards(
        frames, features, seg_counts, stem_weight, stem_gain, stem_shift, lateral, reduce_weight,
        gain_one, shift_one, diff_weight, gate_shift, mid_weight, gain_two, shift_two,
        expand_weight, gain_three, shift_three, pooled_grad,
    ):
        clip_count, seg_slots, pixels, feature_width = features.shape
        slots = clip_count * seg_slots
        mid_width = reduce_weight.shape[1]
        stem_rows, stem_depth = stem_weight.shape
        stem_width = stem_rows * fsdp

        seg_index = lax.broadcasted_iota(jnp.int32, (clip_count, seg_slots), 1)
        valid_seg = (seg_index < seg_counts[:, None]).astype(f32)
        pair_seg = valid_seg * jnp.concatenate(
            [valid_seg[:, 1:], jnp.zeros((clip_count, 1), f32)], axis=1
        )
        valid = valid_seg.reshape(1, 1, slots, 1)
        pair = pair_seg.reshape(1, 1, slots, 1)
        count_float = seg_counts.astype(f32)
        local_count = jnp.sum(count_float) * pixels

        vectors = [gain_three, shift_three, gain_one, shift_one, gate_shift, gain_two, shift_two, stem_gain, stem_shift]
        row = jnp.concatenate(vectors)
        small = jnp.concatenate(
            [
                lateral,
                jnp.pad(stem_weight, ((0, 0), (0, feature_width - stem_depth))),
                jnp.pad(row[None], ((0, 15 - 2 * stem_rows), (0, feature_width - row.shape[0]))),
            ]
        )
        small_full, reduce_full, diff_full, mid_full, expand_full = gather_all(
            [small, reduce_weight, diff_weight, mid_weight, expand_weight], fsdp, reps, 1, "gather_weights"
        )
        lateral_full = small_full[:, :stem_rows].reshape(stem_width, feature_width)
        stem_full = small_full[:, stem_rows : 2 * stem_rows, :stem_depth].reshape(stem_width, stem_depth)
        full = []
        start = 0
        for vector in vectors:
            size = vector.shape[0]
            full.append(small_full[:, 2 * stem_rows, start : start + size].reshape(-1).astype(f32))
            start += size
        (gain_three_full, shift_three_full, gain_one_full, shift_one_full, gate_full, gain_two_full,
         shift_two_full, stem_gain_full, stem_shift_full) = full
        reduce_full = reduce_full.reshape(-1, mid_width)
        diff_full = diff_full.reshape(2, -1, mid_width)
        mid_full = mid_full.reshape(-1, mid_width)
        expand_full = expand_full.reshape(mid_width, -1)

        def moments(values, collective_id, name):
            total = jnp.sum(values * valid, axis=(0, 1, 2))
            off = values - total / local_count
            squares = jnp.sum(off * off * valid, axis=(0, 1, 2))
            total, squares, count = exchange(
                [total, squares, jnp.broadcast_to(local_count, total.shape)], fsdp, reps, True, collective_id, name
            )
            total, squares, count = total[0], squares[0], count[0]
            centre = total / count
            return centre, lax.rsqrt(squares / count + epsilon), count

        def norm(values, stats, gain, shift):
            normed = (values - stats[0]) * stats[1]
            return valid * (gain * normed + shift), normed

        def norm_back(grad_out, normed, stats, gain, collective_id, name):
            masked = grad_out * valid
            shift_sum, gain_sum = exchange(
                [jnp.sum(masked, axis=(0, 1, 2)), jnp.sum(masked * normed, axis=(0, 1, 2))],
                fsdp, reps, False, collective_id, name,
            )
            shift_sum, gain_sum = shift_sum[0], gain_sum[0]
            grad_in = valid * stats[1] * gain * (masked - shift_sum / stats[2] - normed * gain_sum / stats[2])
            return grad_in.astype(bf16), gain_sum, shift_sum

        moving = frames.astype(f32)
        motion = (moving[:, :, 1:] - moving[:, :, :-1]) * valid_seg[:, :, None, None, None]
        motion = jnp.transpose(motion.astype(bf16), (4, 0, 1, 2, 3)).reshape(GRID, GRID, slots, -1)
        stem_kernel = jnp.transpose(stem_full.reshape(stem_width, GRID, GRID, -1), (1, 2, 3, 0))
        stem_pre = convolve(motion, stem_kernel, 3, 1)
        stem_stats = moments(stem_pre, 2, "stem_moments")
        stem_norm, stem_normed = norm(stem_pre, stem_stats, stem_gain_full, stem_shift_full)
        pool_low = pool_mean(jax.nn.gelu(stem_norm)).astype(bf16)
        turned = jnp.transpose(features.reshape(slots, GRID, GRID, feature_width), (1, 2, 0, 3))
        block_in = turned.astype(f32) + project(pool_low, lateral_full)
        block_low = block_in.astype(bf16)
        reduced = project(block_low, reduce_full)
        stats_one = moments(reduced, 3, "moments_one")
        zeta_one, normed_one = norm(reduced, stats_one, gain_one_full, shift_one_full)
        act_one = jax.nn.gelu(zeta_one)
        def later_of(values):
            grid = values.reshape(GRID, GRID, clip_count, seg_slots, -1)
            return jnp.pad(grid[:, :, :, 1:], ((0, 0), (0, 0), (0, 0), (0, 1), (0, 0))).reshape(values.shape)

        def earlier_of(values):
            grid = values.reshape(GRID, GRID, clip_count, seg_slots, -1)
            return jnp.pad(grid[:, :, :, :-1], ((0, 0), (0, 0), (0, 0), (1, 0), (0, 0))).reshape(values.shape)

        change = ((later_of(act_one) - act_one) * pair).astype(bf16)
        gate_pre = convolve(change, diff_full[0], 1, 1) + convolve(change, diff_full[1], 1, 2)
        gate = jax.nn.sigmoid(gate_pre + gate_full)
        modulated = (act_one * (1.0 + gate)).astype(bf16)
        middle = convolve(modulated, mid_full, 1, 1)
        stats_two = moments(middle, 4, "moments_two")
        zeta_two, normed_two = norm(middle, stats_two, gain_two_full, shift_two_full)
        act_two = jax.nn.gelu(zeta_two).astype(bf16)
        expanded = project(act_two, expand_full)
        stats_three = moments(expanded, 5, "moments_three")
        zeta_three, normed_three = norm(expanded, stats_three, gain_three_full, shift_three_full)
        pre_out = block_in + zeta_three
        block_out = jax.nn.gelu(pre_out) * valid
        summed = jnp.sum(block_out.reshape(pixels, clip_count, seg_slots, feature_width), axis=2)
        pooled = jnp.transpose((summed / count_float[None, :, None]).astype(bf16), (1, 0, 2))

        spread = jnp.transpose(pooled_grad, (1, 0, 2)).astype(f32)[:, :, None]
        spread = spread * (valid_seg / count_float[:, None])[None, :, :, None]
        grad_pre = gelu_back(pre_out, spread.reshape(pre_out.shape))
        grad_expanded, gain_three_sum, shift_three_sum = norm_back(
            grad_pre, normed_three, stats_three, gain_three_full, 6, "sums_three"
        )
        expand_terms = project_terms(act_two, grad_expanded, bf16)
        grad_act_two = project_back(grad_expanded, expand_full)
        grad_middle, gain_two_sum, shift_two_sum = norm_back(
            gelu_back(zeta_two, grad_act_two), normed_two, stats_two, gain_two_full, 7, "sums_two"
        )
        mid_terms = convolve_terms(modulated, grad_middle, 1, 1, bf16)
        grad_modulated = convolve_back(grad_middle, mid_full, 1, 1)
        grad_gate_pre = grad_modulated * act_one * gate * (1.0 - gate)
        gate_terms = jnp.sum(grad_gate_pre, axis=(0, 1, 2))
        grad_gate = grad_gate_pre.astype(bf16)
        diff_terms = [convolve_terms(change, grad_gate, 1, 1, bf16), convolve_terms(change, grad_gate, 1, 2, bf16)]
        grad_change = convolve_back(grad_gate, diff_full[0], 1, 1) + convolve_back(grad_gate, diff_full[1], 1, 2)
        grad_change = grad_change * pair
        grad_act_one = grad_modulated * (1.0 + gate) + earlier_of(grad_change) - grad_change
        grad_reduced, gain_one_sum, shift_one_sum = norm_back(
            gelu_back(zeta_one, grad_act_one), normed_one, stats_one, gain_one_full, 8, "sums_one"
        )
        reduce_terms = project_terms(block_low, grad_reduced, bf16)
        features_grad = grad_pre + project_back(grad_reduced, reduce_full)
        grad_lateral = features_grad.astype(bf16)
        lateral_terms = project_terms(pool_low, grad_lateral, bf16)
        grad_act = pool_mean(project_back(grad_lateral, lateral_full))
        grad_stem, stem_gain_sum, stem_shift_sum = norm_back(
            gelu_back(stem_norm, grad_act), stem_normed, stem_stats, stem_gain_full, 9, "sums_stem"
        )
        stem_terms = convolve_terms(motion, grad_stem, 3, 1, bf16)
        stem_terms = jnp.transpose(stem_terms, (3, 0, 1, 2)).reshape(fsdp, stem_rows, stem_depth)
        gate_rows = gate_shift.shape[0]
        small_terms = jnp.concatenate(
            [
                lateral_terms.reshape(fsdp, stem_rows, feature_width),
                jnp.pad(stem_terms, ((0, 0), (0, 0), (0, feature_width - stem_depth))),
                jnp.pad(
                    gate_terms.astype(bf16).reshape(fsdp, 1, gate_rows),
                    ((0, 0), (0, 15 - 2 * stem_rows), (0, feature_width - gate_rows)),
                ),
            ],
            axis=1,
        )

        def owned(terms, shard):
            return terms.reshape(shard.shape[:-2] + (fsdp,) + shard.shape[-2:])

        diff_one, diff_two, mid_part, expand_part, reduce_part, small_part = scatter_all(
            [
                owned(diff_terms[0], diff_weight[0]), owned(diff_terms[1], diff_weight[1]),
                owned(mid_terms, mid_weight), owned(expand_terms, expand_weight),
                owned(reduce_terms, reduce_weight), small_terms,
            ],
            fsdp, reps, 10, "scatter_terms",
        )

        def own_share(whole):
            share = whole.shape[0] // fsdp
            return lax.dynamic_slice_in_dim(whole, lax.axis_index("fsdp") * share, share)

        out = jnp.transpose(features_grad, (2, 0, 1, 3)).reshape(features.shape)
        return (
            pooled,
            out,
            small_part[stem_rows : 2 * stem_rows, :stem_depth],
            own_share(stem_gain_sum),
            own_share(stem_shift_sum),
            small_part[:stem_rows],
            reduce_part,
            own_share(gain_one_sum),
            own_share(shift_one_sum),
            jnp.stack([diff_one, diff_two]),
            small_part[2 * stem_rows, :gate_rows],
            mid_part,
            own_share(gain_two_sum),
            own_share(shift_two_sum),
            expand_part,
            own_share(gain_three_sum),
            own_share(shift_three_sum),
        )

    return shards


def solution(mesh):
    whole = ("fsdp", "rep")
    matrix, vector = P("fsdp", None), P("fsdp")
    in_specs = (
        P(whole, None, None, None, None), P(whole, None, None, None), P(whole),
        matrix, vector, vector, matrix, matrix, vector, vector, P(None, "fsdp", None), vector,
        matrix, vector, vector, matrix, vector, vector, P(whole, None, None),
    )
    out_specs = (
        P(whole, None, None), P(whole, None, None, None), matrix, vector, vector, matrix, matrix,
        vector, vector, P(None, "fsdp", None), vector, matrix, vector, vector, matrix, vector, vector,
    )
    body = make_shards(mesh.shape["fsdp"], mesh.shape["rep"])
    return jax.shard_map(body, mesh=mesh, in_specs=in_specs, out_specs=out_specs, check_vma=False)
```

```python
import functools

import jax
import jax.numpy as jnp
from jax import lax
from jax.experimental import pallas as pl
from jax.experimental.pallas import tpu as pltpu
from jax.sharding import PartitionSpec as P

GRID = 7
LANES = 128
PIXELS = GRID * GRID
epsilon = 1e-05
MESH = pl.DeviceIdType.MESH
ANY = pl.BlockSpec(memory_space=pl.ANY)
IN_VMEM = pl.BlockSpec(memory_space=pltpu.VMEM)
VMEM_LIMIT = 60 * 1024 * 1024
bf16 = jnp.bfloat16
f32 = jnp.float32
DMA = pltpu.SemaphoreType.DMA


def factor_three(size):
    best = None
    for b in range(1, size + 1):
        for c in range(1, b + 1):
            if size % (b * c) == 0 and size // (b * c) >= b:
                a = size // (b * c)
                if best is None or a + b + c < sum(best):
                    best = (a, b, c)
    return best


class Place:
    def __init__(self, dims, reps, rep=None):
        self.dims, self.reps = dims, reps
        size_a, size_b, size_c = dims
        self.me = lax.axis_index("fsdp")
        self.rep = lax.axis_index("rep") if rep is None else rep
        ib, ic = (self.me // size_c) % size_b, self.me % size_c
        self.ia = self.me // (size_b * size_c)
        odd = self.rep % 2 if size_b == size_c else 0
        self.stride_u = size_c * (1 - odd) + odd
        self.stride_v = (1 - odd) + size_c * odd
        self.iu = ib * (1 - odd) + ic * odd
        self.iv = ic * (1 - odd) + ib * odd

    def at(self, da, du, dv):
        size_a, size_b, size_c = self.dims
        a = (self.ia + da + size_a) % size_a
        u = (self.iu + du + size_b) % size_b
        v = (self.iv + dv + size_c) % size_c
        return a * (size_b * size_c) + u * self.stride_u + v * self.stride_v

    def greet(self):
        size_a, size_b, size_c = self.dims
        peers = [(self.at(d, 0, 0), self.rep) for d in range(1, size_a)]
        peers += [(self.at(0, d, 0), self.rep) for d in range(1, size_b)]
        peers += [(self.at(0, 0, d), self.rep) for d in range(1, size_c)]
        peers += [(self.me, (self.rep + d) % self.reps) for d in range(1, self.reps)]
        greet(peers)


def greet(peers):
    barrier = pltpu.get_barrier_semaphore()
    for target, rep in peers:
        pl.semaphore_signal(
            barrier, inc=1, device_id={"fsdp": target, "rep": rep}, device_id_type=MESH
        )
    pl.semaphore_wait(barrier, len(peers))


def remote(src, dst, sems, target, rep):
    return pltpu.make_async_remote_copy(
        src_ref=src,
        dst_ref=dst,
        send_sem=sems.at[0],
        recv_sem=sems.at[1],
        device_id={"fsdp": target, "rep": rep},
        device_id_type=MESH,
    )


def columns(width, which):
    start = which * width
    return pl.ds(start if isinstance(start, int) else pl.multiple_of(start, width), width)


def views(refs):
    out = []
    for ref, stacked in refs:
        out += [ref.at[j] for j in range(ref.shape[0])] if stacked else [ref]
    return out


def gather_kernel(dims, reps, stacked, *refs):
    number = len(stacked)
    shards = views(zip(refs[:number], stacked))
    fulls = views(zip(refs[number : 2 * number], stacked))
    own_sem, a_sem, b_sem, c_sem, r_sem = refs[2 * number :]
    count = len(shards)
    size_a, size_b, size_c = dims
    place = Place(dims, reps)
    me, rep = place.me, place.rep
    place.greet()
    waits = []

    def slot(k, index, which):
        return fulls[k].at[index, :, columns(fulls[k].shape[-1] // reps, which)]

    def push(k, da, du, dv, target, target_rep, sems):
        index = place.at(-da, -du, -dv)
        if (da, du, dv) == (0, 0, 0):
            source = shards[k].at[:, columns(shards[k].shape[-1] // reps, rep)]
        else:
            source = slot(k, index, rep)
        copy = remote(source, slot(k, index, rep), sems, target, target_rep)
        copy.start()
        waits.append(copy)

    def landed(k, da, du, dv, which, sems):
        there = slot(k, place.at(-da, -du, -dv), which)
        remote(there, there, sems, me, rep).wait_recv()

    def forward(k, da, du, dv):
        if dv == 0 and du == 0:
            for d in range(1, size_b):
                push(k, da, 0, 0, place.at(0, d, 0), rep, b_sem.at[k, da, d - 1])
        if dv == 0:
            for d in range(1, size_c):
                push(k, da, du, 0, place.at(0, 0, d), rep, c_sem.at[k, da, du, d - 1])
        if (da, du, dv) != (0, 0, 0):
            for d in range(1, reps):
                push(k, da, du, dv, me, (rep + d) % reps, r_sem.at[k, da, du, dv, d - 1])

    local = []
    for k in range(count):
        copy = pltpu.make_async_copy(shards[k], fulls[k].at[me], own_sem.at[k])
        copy.start()
        local.append(copy)
    for k in range(count):
        for d in range(1, size_a):
            push(k, 0, 0, 0, place.at(d, 0, 0), rep, a_sem.at[k, d - 1])
        forward(k, 0, 0, 0)
    for step in range(count + 2):
        if step < count:
            for da in range(1, size_a):
                landed(step, da, 0, 0, rep, a_sem.at[step, da - 1])
                forward(step, da, 0, 0)
        if 0 <= step - 1 < count:
            for du in range(1, size_b):
                for da in range(size_a):
                    landed(step - 1, da, du, 0, rep, b_sem.at[step - 1, da, du - 1])
                    forward(step - 1, da, du, 0)
        if 0 <= step - 2 < count:
            for dv in range(1, size_c):
                for du in range(size_b):
                    for da in range(size_a):
                        landed(step - 2, da, du, dv, rep, c_sem.at[step - 2, da, du, dv - 1])
                        forward(step - 2, da, du, dv)
    for k in range(count):
        for dv in range(size_c):
            for du in range(size_b):
                for da in range(size_a):
                    if (da, du, dv) != (0, 0, 0):
                        for d in range(1, reps):
                            landed(k, da, du, dv, (rep + reps - d) % reps, r_sem.at[k, da, du, dv, d - 1])
    for copy in waits:
        copy.wait_send()
    for copy in local:
        copy.wait()


def gather_all(shards, fsdp, reps, collective_id, name):
    dims = factor_three(fsdp)
    size_a, size_b, size_c = dims
    stacked = [s.ndim == 3 for s in shards]
    count = sum(s.shape[0] if s.ndim == 3 else 1 for s in shards)
    return pl.pallas_call(
        functools.partial(gather_kernel, dims, reps, stacked),
        out_shape=[
            jax.ShapeDtypeStruct(s.shape[:-2] + (fsdp,) + s.shape[-2:], s.dtype) for s in shards
        ],
        in_specs=[ANY] * len(shards),
        out_specs=[ANY] * len(shards),
        scratch_shapes=[
            DMA((count,)),
            DMA((count, max(size_a - 1, 1), 2)),
            DMA((count, size_a, max(size_b - 1, 1), 2)),
            DMA((count, size_a, size_b, max(size_c - 1, 1), 2)),
            DMA((count, size_a, size_b, size_c, max(reps - 1, 1), 2)),
        ],
        compiler_params=pltpu.CompilerParams(
            collective_id=collective_id, has_side_effects=True, vmem_limit_bytes=VMEM_LIMIT
        ),
        name=name,
    )(*shards)


def scatter_kernel(dims, reps, stacked, *refs):
    number = len(stacked)
    partials = views(zip(refs[:number], stacked))
    totals = views(zip(refs[number : 2 * number], stacked))
    count = len(partials)
    rest = refs[2 * number :]
    held, from_rep, from_v, from_u, from_a, share = (rest[i * count : (i + 1) * count] for i in range(6))
    own_sem, r_sem, v_sem, u_sem, a_sem, s_sem = rest[6 * count :]
    size_a, size_b, size_c = dims
    place = Place(dims, reps)
    me, rep = place.me, place.rep
    place.greet()
    waits = []

    def push(source, there, sems, target, target_rep):
        copy = remote(source, there, sems, target, target_rep)
        copy.start()
        waits.append(copy)

    def landed(there, sems):
        remote(there, there, sems, me, rep).wait_recv()

    def order():
        for dv in list(range(1, size_c)) + [0]:
            for du in list(range(1, size_b)) + [0]:
                for da in list(range(1, size_a)) + [0]:
                    yield da, du, dv

    local = {}
    for k in range(count):
        width = partials[k].shape[-1] // reps
        for da, du, dv in order():
            for d in range(1, reps):
                other = (rep + d) % reps
                index = Place(dims, reps, other).at(da, du, dv)
                push(
                    partials[k].at[index, :, columns(width, other)],
                    from_rep[k].at[d - 1, index],
                    r_sem.at[k, da, du, dv, d - 1],
                    me,
                    other,
                )
            index = place.at(da, du, dv)
            copy = pltpu.make_async_copy(
                partials[k].at[index, :, columns(width, rep)],
                held[k].at[index],
                own_sem.at[k, da, du, dv],
            )
            copy.start()
            local[k, da, du, dv] = copy

    def handle(k, da, du, dv):
        index = place.at(da, du, dv)
        local[k, da, du, dv].wait()
        total = held[k][index].astype(f32)
        for d in range(1, reps):
            landed(from_rep[k].at[d - 1, index], r_sem.at[k, da, du, dv, d - 1])
            total = total + from_rep[k][d - 1, index].astype(f32)
        if dv == 0:
            for e in range(1, size_c):
                landed(from_v[k].at[e - 1, da, du], v_sem.at[k, da, du, e - 1])
                total = total + from_v[k][e - 1, da, du].astype(f32)
            if du == 0:
                for e in range(1, size_b):
                    landed(from_u[k].at[e - 1, da], u_sem.at[k, da, e - 1])
                    total = total + from_u[k][e - 1, da].astype(f32)
                if da == 0:
                    for e in range(1, size_a):
                        landed(from_a[k].at[e - 1], a_sem.at[k, e - 1])
                        total = total + from_a[k][e - 1].astype(f32)
        if (da, du, dv) == (0, 0, 0):
            share[k][rep] = total.astype(bf16)
            for d in range(1, reps):
                push(share[k].at[rep], share[k].at[rep], s_sem.at[k, d - 1], me, (rep + d) % reps)
            return
        held[k][index] = total.astype(bf16)
        if dv:
            push(held[k].at[index], from_v[k].at[dv - 1, da, du], v_sem.at[k, da, du, dv - 1], place.at(0, 0, dv), rep)
        elif du:
            push(held[k].at[index], from_u[k].at[du - 1, da], u_sem.at[k, da, du - 1], place.at(0, du, 0), rep)
        else:
            push(held[k].at[index], from_a[k].at[da - 1], a_sem.at[k, da - 1], place.at(da, 0, 0), rep)

    for step in range(count + 3):
        for lag in range(4):
            k = step - lag
            for da, du, dv in order() if 0 <= k < count else ():
                if lag == (0 if dv else 1 if du else 2 if da else 3):
                    handle(k, da, du, dv)
    for k in range(count):
        width = partials[k].shape[-1] // reps
        for d in range(1, reps):
            landed(share[k].at[(rep + reps - d) % reps], s_sem.at[k, d - 1])
        for which in range(reps):
            totals[k][:, which * width : (which + 1) * width] = share[k][which].astype(f32)
    for copy in waits:
        copy.wait_send()


def scatter_all(partials, fsdp, reps, collective_id, name):
    dims = factor_three(fsdp)
    size_a, size_b, size_c = dims
    stacked = [p.ndim == 4 for p in partials]
    shapes = []
    for p in partials:
        shapes += [(p.shape[-2], p.shape[-1] // reps)] * (p.shape[0] if p.ndim == 4 else 1)
    count = len(shapes)

    def buffers(*lead):
        return [pltpu.VMEM(lead + shape, bf16) for shape in shapes]

    return pl.pallas_call(
        functools.partial(scatter_kernel, dims, reps, stacked),
        out_shape=[
            jax.ShapeDtypeStruct(p.shape[:-3] + p.shape[-2:], f32) for p in partials
        ],
        in_specs=[ANY] * len(partials),
        out_specs=[IN_VMEM] * len(partials),
        scratch_shapes=buffers(fsdp)
        + buffers(max(reps - 1, 1), fsdp)
        + buffers(max(size_c - 1, 1), size_a, size_b)
        + buffers(max(size_b - 1, 1), size_a)
        + buffers(max(size_a - 1, 1))
        + buffers(reps)
        + [
            DMA((count, size_a, size_b, size_c)),
            DMA((count, size_a, size_b, size_c, max(reps - 1, 1), 2)),
            DMA((count, size_a, size_b, max(size_c - 1, 1), 2)),
            DMA((count, size_a, max(size_b - 1, 1), 2)),
            DMA((count, max(size_a - 1, 1), 2)),
            DMA((count, max(reps - 1, 1), 2)),
        ],
        compiler_params=pltpu.CompilerParams(
            collective_id=collective_id, has_side_effects=True, vmem_limit_bytes=VMEM_LIMIT
        ),
        name=name,
    )(*partials)


def stage_sizes(devices):
    sizes = []
    while devices > 1:
        size = next(s for s in (8, 4, 2, 7, 5, 3, devices) if devices % s == 0)
        sizes.append(size)
        devices //= size
    return sizes


def exchange_kernel(sizes, reps, moments, width, *refs):
    number = 3 if moments else 2
    sources, results = refs[:number], refs[number : 2 * number]
    mine, slots, sems = refs[2 * number], refs[2 * number + 1 : -1], refs[-1]
    place = lax.axis_index("fsdp") * reps + lax.axis_index("rep")
    stages = []
    stride = 1
    for size in sizes:
        position = (place // stride) % size
        peers = []
        for d in range(1, size):
            target = place + ((position + d) % size - position) * stride
            peers.append((target // reps, target % reps))
        stages.append((size, position, peers))
        stride *= size
    greet([peer for stage in stages for peer in stage[2]])
    spans = [(0, width), (width, width), (2 * width, LANES)][:number]
    current = [source[...] for source in sources]
    waits = []
    for index, (size, position, peers) in enumerate(stages):
        for (start, length), value in zip(spans, current):
            mine[index, :, start : start + length] = value
        for d, (target, rep) in enumerate(peers, 1):
            copy = remote(mine.at[index], slots[index].at[position], sems.at[index, d - 1], target, rep)
            copy.start()
            waits.append(copy)
        slots[index][position] = mine[index]
        for d, (target, rep) in enumerate(peers, 1):
            there = slots[index].at[(position + size - d) % size]
            remote(there, there, sems.at[index, d - 1], target, rep).wait_recv()
        parts = [
            [slots[index][j, :, start : start + length] for start, length in spans] for j in range(size)
        ]
        current = [functools.reduce(jnp.add, [part[row] for part in parts]) for row in range(number)]
        if moments:
            centre = current[0] / current[2][:, :1]
            squares = current[1]
            for part in parts:
                count = part[2][:, :1]
                off = part[0] / count - centre
                squares = squares + count * off * off
            current[1] = squares
    for result, value in zip(results, current):
        result[...] = value
    for copy in waits:
        copy.wait_send()


def exchange(rows, fsdp, reps, moments, collective_id, name):
    sizes = stage_sizes(fsdp * reps)
    width = rows[0].shape[-1]
    padded = -(-width // LANES) * LANES
    rows = [jnp.pad(row.reshape(1, -1), ((0, 0), (0, padded - width))) for row in rows[:2]] + [
        jnp.broadcast_to(row.reshape(1, 1), (1, LANES)) for row in rows[2:]
    ]
    total = sum(row.shape[1] for row in rows)
    results = pl.pallas_call(
        functools.partial(exchange_kernel, sizes, reps, moments, padded),
        out_shape=[jax.ShapeDtypeStruct(row.shape, f32) for row in rows],
        in_specs=[IN_VMEM] * len(rows),
        out_specs=[IN_VMEM] * len(rows),
        scratch_shapes=[pltpu.VMEM((len(sizes), 1, total), f32)]
        + [pltpu.VMEM((size, 1, total), f32) for size in sizes]
        + [DMA((len(sizes), max(max(sizes) - 1, 1), 2))],
        compiler_params=pltpu.CompilerParams(
            collective_id=collective_id, has_side_effects=True, vmem_limit_bytes=4 * 1024 * 1024
        ),
        name=name,
    )(*rows)
    return [result[0, :width] for result in results[:2]] + [result[0, 0] for result in results[2:]]


ORDER = ("HWNC", "HWIO", "HWNC")


def pad_of(span):
    return ((span, span), (span, span))


def convolve(source, weight, span, stride):
    side = 2 * span + 1
    kernel = weight.reshape(side, side, source.shape[-1], -1)
    return lax.conv_general_dilated(
        source, kernel, (1, 1), pad_of(span * stride), rhs_dilation=(stride, stride),
        dimension_numbers=ORDER, preferred_element_type=f32,
    )


def convolve_back(grads, weight, span, stride):
    side = 2 * span + 1
    kernel = weight.reshape(side, side, -1, grads.shape[-1])[::-1, ::-1]
    return lax.conv_general_dilated(
        grads, kernel, (1, 1), pad_of(span * stride), rhs_dilation=(stride, stride),
        dimension_numbers=("HWNC", "HWOI", "HWNC"), preferred_element_type=f32,
    )


def convolve_terms(source, grads, span, stride, kind):
    return lax.conv_general_dilated(
        source, grads, (stride, stride), pad_of(span * stride),
        dimension_numbers=("HWCN", "HWIO", "HWNC"), preferred_element_type=kind,
    )


def pool_mean(source):
    total = lax.reduce_window(source, 0.0, lax.add, (3, 3, 1, 1), (1, 1, 1, 1), "SAME")
    return total / 9.0


def project(source, weight):
    return jnp.einsum("yxnc,cd->yxnd", source, weight, preferred_element_type=f32)


def project_back(grads, weight):
    return jnp.einsum("yxnd,cd->yxnc", grads, weight, preferred_element_type=f32)


def project_terms(source, grads, kind):
    return jnp.einsum("yxnc,yxnd->cd", source, grads, preferred_element_type=kind)


def gelu_back(pre_act, grads):
    return jax.vjp(jax.nn.gelu, pre_act)[1](grads)[0]


def make_shards(fsdp, reps):
    def shards(
        frames, features, seg_counts, stem_weight, stem_gain, stem_shift, lateral, reduce_weight,
        gain_one, shift_one, diff_weight, gate_shift, mid_weight, gain_two, shift_two,
        expand_weight, gain_three, shift_three, pooled_grad,
    ):
        clip_count, seg_slots, pixels, feature_width = features.shape
        slots = clip_count * seg_slots
        mid_width = reduce_weight.shape[1]
        stem_rows, stem_depth = stem_weight.shape
        stem_width = stem_rows * fsdp

        seg_index = lax.broadcasted_iota(jnp.int32, (clip_count, seg_slots), 1)
        valid_seg = (seg_index < seg_counts[:, None]).astype(f32)
        pair_seg = valid_seg * jnp.concatenate(
            [valid_seg[:, 1:], jnp.zeros((clip_count, 1), f32)], axis=1
        )
        valid = valid_seg.reshape(1, 1, slots, 1)
        pair = pair_seg.reshape(1, 1, slots, 1)
        count_float = seg_counts.astype(f32)
        local_count = jnp.sum(count_float) * pixels

        vectors = [gain_three, shift_three, gain_one, shift_one, gate_shift, gain_two, shift_two, stem_gain, stem_shift]
        row = jnp.concatenate(vectors)
        small = jnp.concatenate(
            [
                lateral,
                jnp.pad(stem_weight, ((0, 0), (0, feature_width - stem_depth))),
                jnp.pad(row[None], ((0, 15 - 2 * stem_rows), (0, feature_width - row.shape[0]))),
            ]
        )
        small_full, reduce_full, diff_full, mid_full, expand_full = gather_all(
            [small, reduce_weight, diff_weight, mid_weight, expand_weight], fsdp, reps, 1, "gather_weights"
        )
        lateral_full = small_full[:, :stem_rows].reshape(stem_width, feature_width)
        stem_full = small_full[:, stem_rows : 2 * stem_rows, :stem_depth].reshape(stem_width, stem_depth)
        full = []
        start = 0
        for vector in vectors:
            size = vector.shape[0]
            full.append(small_full[:, 2 * stem_rows, start : start + size].reshape(-1).astype(f32))
            start += size
        (gain_three_full, shift_three_full, gain_one_full, shift_one_full, gate_full, gain_two_full,
         shift_two_full, stem_gain_full, stem_shift_full) = full
        reduce_full = reduce_full.reshape(-1, mid_width)
        diff_full = diff_full.reshape(2, -1, mid_width)
        mid_full = mid_full.reshape(-1, mid_width)
        expand_full = expand_full.reshape(mid_width, -1)

        def moments(values, collective_id, name):
            total = jnp.sum(values * valid, axis=(0, 1, 2))
            off = values - total / local_count
            squares = jnp.sum(off * off * valid, axis=(0, 1, 2))
            total, squares, count = exchange(
                [total, squares, local_count], fsdp, reps, True, collective_id, name
            )
            centre = total / count
            return centre, lax.rsqrt(squares / count + epsilon), count

        def norm(values, stats, gain, shift):
            normed = (values - stats[0]) * stats[1]
            return valid * (gain * normed + shift), normed

        def norm_back(grad_out, normed, stats, gain, collective_id, name):
            masked = grad_out * valid
            shift_sum, gain_sum = exchange(
                [jnp.sum(masked, axis=(0, 1, 2)), jnp.sum(masked * normed, axis=(0, 1, 2))],
                fsdp, reps, False, collective_id, name,
            )
            grad_in = valid * stats[1] * gain * (masked - shift_sum / stats[2] - normed * gain_sum / stats[2])
            return grad_in.astype(bf16), gain_sum, shift_sum

        moving = frames.astype(f32)
        motion = (moving[:, :, 1:] - moving[:, :, :-1]) * valid_seg[:, :, None, None, None]
        motion = jnp.transpose(motion.astype(bf16), (4, 0, 1, 2, 3)).reshape(GRID, GRID, slots, -1)
        stem_kernel = jnp.transpose(stem_full.reshape(stem_width, GRID, GRID, -1), (1, 2, 3, 0))
        stem_pre = convolve(motion, stem_kernel, 3, 1)
        stem_stats = moments(stem_pre, 2, "stem_moments")
        stem_norm, stem_normed = norm(stem_pre, stem_stats, stem_gain_full, stem_shift_full)
        pool_low = pool_mean(jax.nn.gelu(stem_norm)).astype(bf16)
        turned = jnp.transpose(features.reshape(slots, GRID, GRID, feature_width), (1, 2, 0, 3))
        block_in = turned.astype(f32) + project(pool_low, lateral_full)
        block_low = block_in.astype(bf16)
        reduced = project(block_low, reduce_full)
        stats_one = moments(reduced, 3, "moments_one")
        zeta_one, normed_one = norm(reduced, stats_one, gain_one_full, shift_one_full)
        act_one = jax.nn.gelu(zeta_one)
        def later_of(values):
            grid = values.reshape(GRID, GRID, clip_count, seg_slots, -1)
            return jnp.pad(grid[:, :, :, 1:], ((0, 0), (0, 0), (0, 0), (0, 1), (0, 0))).reshape(values.shape)

        def earlier_of(values):
            grid = values.reshape(GRID, GRID, clip_count, seg_slots, -1)
            return jnp.pad(grid[:, :, :, :-1], ((0, 0), (0, 0), (0, 0), (1, 0), (0, 0))).reshape(values.shape)

        change = ((later_of(act_one) - act_one) * pair).astype(bf16)
        gate_pre = convolve(change, diff_full[0], 1, 1) + convolve(change, diff_full[1], 1, 2)
        gate = jax.nn.sigmoid(gate_pre + gate_full)
        modulated = (act_one * (1.0 + gate)).astype(bf16)
        middle = convolve(modulated, mid_full, 1, 1)
        stats_two = moments(middle, 4, "moments_two")
        zeta_two, normed_two = norm(middle, stats_two, gain_two_full, shift_two_full)
        act_two = jax.nn.gelu(zeta_two).astype(bf16)
        expanded = project(act_two, expand_full)
        stats_three = moments(expanded, 5, "moments_three")
        zeta_three, normed_three = norm(expanded, stats_three, gain_three_full, shift_three_full)
        pre_out = block_in + zeta_three
        block_out = jax.nn.gelu(pre_out) * valid
        summed = jnp.sum(block_out.reshape(pixels, clip_count, seg_slots, feature_width), axis=2)
        pooled = jnp.transpose((summed / count_float[None, :, None]).astype(bf16), (1, 0, 2))

        spread = jnp.transpose(pooled_grad, (1, 0, 2)).astype(f32)[:, :, None]
        spread = spread * (valid_seg / count_float[:, None])[None, :, :, None]
        grad_pre = gelu_back(pre_out, spread.reshape(pre_out.shape))
        grad_expanded, gain_three_sum, shift_three_sum = norm_back(
            grad_pre, normed_three, stats_three, gain_three_full, 6, "sums_three"
        )
        expand_terms = project_terms(act_two, grad_expanded, bf16)
        grad_act_two = project_back(grad_expanded, expand_full)
        grad_middle, gain_two_sum, shift_two_sum = norm_back(
            gelu_back(zeta_two, grad_act_two), normed_two, stats_two, gain_two_full, 7, "sums_two"
        )
        mid_terms = convolve_terms(modulated, grad_middle, 1, 1, bf16)
        grad_modulated = convolve_back(grad_middle, mid_full, 1, 1)
        grad_gate_pre = grad_modulated * act_one * gate * (1.0 - gate)
        gate_terms = jnp.sum(grad_gate_pre, axis=(0, 1, 2))
        grad_gate = grad_gate_pre.astype(bf16)
        diff_terms = [convolve_terms(change, grad_gate, 1, 1, bf16), convolve_terms(change, grad_gate, 1, 2, bf16)]
        grad_change = convolve_back(grad_gate, diff_full[0], 1, 1) + convolve_back(grad_gate, diff_full[1], 1, 2)
        grad_change = grad_change * pair
        grad_act_one = grad_modulated * (1.0 + gate) + earlier_of(grad_change) - grad_change
        grad_reduced, gain_one_sum, shift_one_sum = norm_back(
            gelu_back(zeta_one, grad_act_one), normed_one, stats_one, gain_one_full, 8, "sums_one"
        )
        reduce_terms = project_terms(block_low, grad_reduced, bf16)
        features_grad = grad_pre + project_back(grad_reduced, reduce_full)
        grad_lateral = features_grad.astype(bf16)
        lateral_terms = project_terms(pool_low, grad_lateral, bf16)
        grad_act = pool_mean(project_back(grad_lateral, lateral_full))
        grad_stem, stem_gain_sum, stem_shift_sum = norm_back(
            gelu_back(stem_norm, grad_act), stem_normed, stem_stats, stem_gain_full, 9, "sums_stem"
        )
        stem_terms = convolve_terms(motion, grad_stem, 3, 1, bf16)
        stem_terms = jnp.transpose(stem_terms, (3, 0, 1, 2)).reshape(fsdp, stem_rows, stem_depth)
        gate_rows = gate_shift.shape[0]
        small_terms = jnp.concatenate(
            [
                lateral_terms.reshape(fsdp, stem_rows, feature_width),
                jnp.pad(stem_terms, ((0, 0), (0, 0), (0, feature_width - stem_depth))),
                jnp.pad(
                    gate_terms.astype(bf16).reshape(fsdp, 1, gate_rows),
                    ((0, 0), (0, 15 - 2 * stem_rows), (0, feature_width - gate_rows)),
                ),
            ],
            axis=1,
        )

        def owned(terms, shard):
            return terms.reshape(shard.shape[:-2] + (fsdp,) + shard.shape[-2:])

        diff_one, diff_two, mid_part, expand_part, reduce_part, small_part = scatter_all(
            [
                owned(diff_terms[0], diff_weight[0]), owned(diff_terms[1], diff_weight[1]),
                owned(mid_terms, mid_weight), owned(expand_terms, expand_weight),
                owned(reduce_terms, reduce_weight), small_terms,
            ],
            fsdp, reps, 10, "scatter_terms",
        )

        def own_share(whole):
            share = whole.shape[0] // fsdp
            return lax.dynamic_slice_in_dim(whole, lax.axis_index("fsdp") * share, share)

        out = jnp.transpose(features_grad, (2, 0, 1, 3)).reshape(features.shape)
        return (
            pooled,
            out,
            small_part[stem_rows : 2 * stem_rows, :stem_depth],
            own_share(stem_gain_sum),
            own_share(stem_shift_sum),
            small_part[:stem_rows],
            reduce_part,
            own_share(gain_one_sum),
            own_share(shift_one_sum),
            jnp.stack([diff_one, diff_two]),
            small_part[2 * stem_rows, :gate_rows],
            mid_part,
            own_share(gain_two_sum),
            own_share(shift_two_sum),
            expand_part,
            own_share(gain_three_sum),
            own_share(shift_three_sum),
        )

    return shards


def solution(mesh):
    whole = ("fsdp", "rep")
    matrix, vector = P("fsdp", None), P("fsdp")
    in_specs = (
        P(whole, None, None, None, None), P(whole, None, None, None), P(whole),
        matrix, vector, vector, matrix, matrix, vector, vector, P(None, "fsdp", None), vector,
        matrix, vector, vector, matrix, vector, vector, P(whole, None, None),
    )
    out_specs = (
        P(whole, None, None), P(whole, None, None, None), matrix, vector, vector, matrix, matrix,
        vector, vector, P(None, "fsdp", None), vector, matrix, vector, vector, matrix, vector, vector,
    )
    body = make_shards(mesh.shape["fsdp"], mesh.shape["rep"])
    return jax.shard_map(body, mesh=mesh, in_specs=in_specs, out_specs=out_specs, check_vma=False)
```

```python
import functools

import jax
import jax.numpy as jnp
from jax import lax
from jax.experimental import pallas as pl
from jax.experimental.pallas import tpu as pltpu
from jax.sharding import PartitionSpec as P

GRID = 7
LANES = 128
PIXELS = GRID * GRID
epsilon = 1e-05
MESH = pl.DeviceIdType.MESH
ANY = pl.BlockSpec(memory_space=pl.ANY)
IN_VMEM = pl.BlockSpec(memory_space=pltpu.VMEM)
VMEM_LIMIT = 60 * 1024 * 1024
bf16 = jnp.bfloat16
f32 = jnp.float32
DMA = pltpu.SemaphoreType.DMA


def factor_three(size):
    best = None
    for b in range(1, size + 1):
        for c in range(1, b + 1):
            if size % (b * c) == 0 and size // (b * c) >= b:
                a = size // (b * c)
                if best is None or a + b + c < sum(best):
                    best = (a, b, c)
    return best


class Place:
    def __init__(self, dims, reps, rep=None):
        self.dims, self.reps = dims, reps
        size_a, size_b, size_c = dims
        self.me = lax.axis_index("fsdp")
        self.rep = lax.axis_index("rep") if rep is None else rep
        ib, ic = (self.me // size_c) % size_b, self.me % size_c
        self.ia = self.me // (size_b * size_c)
        odd = self.rep % 2 if size_b == size_c else 0
        self.stride_u = size_c * (1 - odd) + odd
        self.stride_v = (1 - odd) + size_c * odd
        self.iu = ib * (1 - odd) + ic * odd
        self.iv = ic * (1 - odd) + ib * odd

    def at(self, da, du, dv):
        size_a, size_b, size_c = self.dims
        a = (self.ia + da + size_a) % size_a
        u = (self.iu + du + size_b) % size_b
        v = (self.iv + dv + size_c) % size_c
        return a * (size_b * size_c) + u * self.stride_u + v * self.stride_v

    def greet(self):
        size_a, size_b, size_c = self.dims
        peers = [(self.at(d, 0, 0), self.rep) for d in range(1, size_a)]
        peers += [(self.at(0, d, 0), self.rep) for d in range(1, size_b)]
        peers += [(self.at(0, 0, d), self.rep) for d in range(1, size_c)]
        peers += [(self.me, (self.rep + d) % self.reps) for d in range(1, self.reps)]
        greet(peers)


def greet(peers):
    barrier = pltpu.get_barrier_semaphore()
    for target, rep in peers:
        pl.semaphore_signal(
            barrier, inc=1, device_id={"fsdp": target, "rep": rep}, device_id_type=MESH
        )
    pl.semaphore_wait(barrier, len(peers))


def remote(src, dst, sems, target, rep):
    return pltpu.make_async_remote_copy(
        src_ref=src,
        dst_ref=dst,
        send_sem=sems.at[0],
        recv_sem=sems.at[1],
        device_id={"fsdp": target, "rep": rep},
        device_id_type=MESH,
    )


def columns(width, which):
    start = which * width
    return pl.ds(start if isinstance(start, int) else pl.multiple_of(start, width), width)


def views(refs):
    out = []
    for ref, stacked in refs:
        out += [ref.at[j] for j in range(ref.shape[0])] if stacked else [ref]
    return out


def gather_kernel(dims, reps, stacked, *refs):
    number = len(stacked)
    shards = views(zip(refs[:number], stacked))
    fulls = views(zip(refs[number : 2 * number], stacked))
    own_sem, a_sem, b_sem, c_sem, r_sem = refs[2 * number :]
    count = len(shards)
    size_a, size_b, size_c = dims
    place = Place(dims, reps)
    me, rep = place.me, place.rep
    place.greet()
    waits = []

    def slot(k, index, which):
        return fulls[k].at[index, :, columns(fulls[k].shape[-1] // reps, which)]

    def push(k, da, du, dv, target, target_rep, sems):
        index = place.at(-da, -du, -dv)
        if (da, du, dv) == (0, 0, 0):
            source = shards[k].at[:, columns(shards[k].shape[-1] // reps, rep)]
        else:
            source = slot(k, index, rep)
        copy = remote(source, slot(k, index, rep), sems, target, target_rep)
        copy.start()
        waits.append(copy)

    def landed(k, da, du, dv, which, sems):
        there = slot(k, place.at(-da, -du, -dv), which)
        remote(there, there, sems, me, rep).wait_recv()

    def forward(k, da, du, dv):
        if dv == 0 and du == 0:
            for d in range(1, size_b):
                push(k, da, 0, 0, place.at(0, d, 0), rep, b_sem.at[k, da, d - 1])
        if dv == 0:
            for d in range(1, size_c):
                push(k, da, du, 0, place.at(0, 0, d), rep, c_sem.at[k, da, du, d - 1])
        if (da, du, dv) != (0, 0, 0):
            for d in range(1, reps):
                push(k, da, du, dv, me, (rep + d) % reps, r_sem.at[k, da, du, dv, d - 1])

    local = []
    for k in range(count):
        copy = pltpu.make_async_copy(shards[k], fulls[k].at[me], own_sem.at[k])
        copy.start()
        local.append(copy)
    for k in range(count):
        for d in range(1, size_a):
            push(k, 0, 0, 0, place.at(d, 0, 0), rep, a_sem.at[k, d - 1])
        forward(k, 0, 0, 0)
    for step in range(count + 2):
        if step < count:
            for da in range(1, size_a):
                landed(step, da, 0, 0, rep, a_sem.at[step, da - 1])
                forward(step, da, 0, 0)
        if 0 <= step - 1 < count:
            for du in range(1, size_b):
                for da in range(size_a):
                    landed(step - 1, da, du, 0, rep, b_sem.at[step - 1, da, du - 1])
                    forward(step - 1, da, du, 0)
        if 0 <= step - 2 < count:
            for dv in range(1, size_c):
                for du in range(size_b):
                    for da in range(size_a):
                        landed(step - 2, da, du, dv, rep, c_sem.at[step - 2, da, du, dv - 1])
                        forward(step - 2, da, du, dv)
    for k in range(count):
        for dv in range(size_c):
            for du in range(size_b):
                for da in range(size_a):
                    if (da, du, dv) != (0, 0, 0):
                        for d in range(1, reps):
                            landed(k, da, du, dv, (rep + reps - d) % reps, r_sem.at[k, da, du, dv, d - 1])
    for copy in waits:
        copy.wait_send()
    for copy in local:
        copy.wait()


def gather_all(shards, fsdp, reps, collective_id, name):
    dims = factor_three(fsdp)
    size_a, size_b, size_c = dims
    stacked = [s.ndim == 3 for s in shards]
    count = sum(s.shape[0] if s.ndim == 3 else 1 for s in shards)
    return pl.pallas_call(
        functools.partial(gather_kernel, dims, reps, stacked),
        out_shape=[
            jax.ShapeDtypeStruct(s.shape[:-2] + (fsdp,) + s.shape[-2:], s.dtype) for s in shards
        ],
        in_specs=[ANY] * len(shards),
        out_specs=[ANY] * len(shards),
        scratch_shapes=[
            DMA((count,)),
            DMA((count, max(size_a - 1, 1), 2)),
            DMA((count, size_a, max(size_b - 1, 1), 2)),
            DMA((count, size_a, size_b, max(size_c - 1, 1), 2)),
            DMA((count, size_a, size_b, size_c, max(reps - 1, 1), 2)),
        ],
        compiler_params=pltpu.CompilerParams(
            collective_id=collective_id, has_side_effects=True, vmem_limit_bytes=VMEM_LIMIT
        ),
        name=name,
    )(*shards)


def scatter_kernel(dims, reps, stacked, *refs):
    number = len(stacked)
    partials = views(zip(refs[:number], stacked))
    totals = views(zip(refs[number : 2 * number], stacked))
    count = len(partials)
    rest = refs[2 * number :]
    held, from_rep, from_v, from_u, from_a, share = (rest[i * count : (i + 1) * count] for i in range(6))
    own_sem, r_sem, v_sem, u_sem, a_sem, s_sem = rest[6 * count :]
    size_a, size_b, size_c = dims
    place = Place(dims, reps)
    me, rep = place.me, place.rep
    place.greet()
    waits = []

    def push(source, there, sems, target, target_rep):
        copy = remote(source, there, sems, target, target_rep)
        copy.start()
        waits.append(copy)

    def landed(there, sems):
        remote(there, there, sems, me, rep).wait_recv()

    def order():
        for dv in list(range(1, size_c)) + [0]:
            for du in list(range(1, size_b)) + [0]:
                for da in list(range(1, size_a)) + [0]:
                    yield da, du, dv

    local = {}
    for k in range(count):
        width = partials[k].shape[-1] // reps
        for da, du, dv in order():
            for d in range(1, reps):
                other = (rep + d) % reps
                index = Place(dims, reps, other).at(da, du, dv)
                push(
                    partials[k].at[index, :, columns(width, other)],
                    from_rep[k].at[d - 1, index],
                    r_sem.at[k, da, du, dv, d - 1],
                    me,
                    other,
                )
            index = place.at(da, du, dv)
            copy = pltpu.make_async_copy(
                partials[k].at[index, :, columns(width, rep)],
                held[k].at[index],
                own_sem.at[k, da, du, dv],
            )
            copy.start()
            local[k, da, du, dv] = copy

    def handle(k, da, du, dv):
        index = place.at(da, du, dv)
        local[k, da, du, dv].wait()
        total = held[k][index].astype(f32)
        for d in range(1, reps):
            landed(from_rep[k].at[d - 1, index], r_sem.at[k, da, du, dv, d - 1])
            total = total + from_rep[k][d - 1, index].astype(f32)
        if dv == 0:
            for e in range(1, size_c):
                landed(from_v[k].at[e - 1, da, du], v_sem.at[k, da, du, e - 1])
                total = total + from_v[k][e - 1, da, du].astype(f32)
            if du == 0:
                for e in range(1, size_b):
                    landed(from_u[k].at[e - 1, da], u_sem.at[k, da, e - 1])
                    total = total + from_u[k][e - 1, da].astype(f32)
                if da == 0:
                    for e in range(1, size_a):
                        landed(from_a[k].at[e - 1], a_sem.at[k, e - 1])
                        total = total + from_a[k][e - 1].astype(f32)
        if (da, du, dv) == (0, 0, 0):
            share[k][rep] = total.astype(bf16)
            for d in range(1, reps):
                push(share[k].at[rep], share[k].at[rep], s_sem.at[k, d - 1], me, (rep + d) % reps)
            return
        held[k][index] = total.astype(bf16)
        if dv:
            push(held[k].at[index], from_v[k].at[dv - 1, da, du], v_sem.at[k, da, du, dv - 1], place.at(0, 0, dv), rep)
        elif du:
            push(held[k].at[index], from_u[k].at[du - 1, da], u_sem.at[k, da, du - 1], place.at(0, du, 0), rep)
        else:
            push(held[k].at[index], from_a[k].at[da - 1], a_sem.at[k, da - 1], place.at(da, 0, 0), rep)

    for step in range(count + 3):
        for lag in range(4):
            k = step - lag
            for da, du, dv in order() if 0 <= k < count else ():
                if lag == (0 if dv else 1 if du else 2 if da else 3):
                    handle(k, da, du, dv)
    for k in range(count):
        width = partials[k].shape[-1] // reps
        for d in range(1, reps):
            landed(share[k].at[(rep + reps - d) % reps], s_sem.at[k, d - 1])
        for which in range(reps):
            totals[k][:, which * width : (which + 1) * width] = share[k][which].astype(f32)
    for copy in waits:
        copy.wait_send()


def scatter_all(partials, fsdp, reps, collective_id, name):
    dims = factor_three(fsdp)
    size_a, size_b, size_c = dims
    stacked = [p.ndim == 4 for p in partials]
    shapes = []
    for p in partials:
        shapes += [(p.shape[-2], p.shape[-1] // reps)] * (p.shape[0] if p.ndim == 4 else 1)
    count = len(shapes)

    def buffers(*lead):
        return [pltpu.VMEM(lead + shape, bf16) for shape in shapes]

    return pl.pallas_call(
        functools.partial(scatter_kernel, dims, reps, stacked),
        out_shape=[
            jax.ShapeDtypeStruct(p.shape[:-3] + p.shape[-2:], f32) for p in partials
        ],
        in_specs=[ANY] * len(partials),
        out_specs=[IN_VMEM] * len(partials),
        scratch_shapes=buffers(fsdp)
        + buffers(max(reps - 1, 1), fsdp)
        + buffers(max(size_c - 1, 1), size_a, size_b)
        + buffers(max(size_b - 1, 1), size_a)
        + buffers(max(size_a - 1, 1))
        + buffers(reps)
        + [
            DMA((count, size_a, size_b, size_c)),
            DMA((count, size_a, size_b, size_c, max(reps - 1, 1), 2)),
            DMA((count, size_a, size_b, max(size_c - 1, 1), 2)),
            DMA((count, size_a, max(size_b - 1, 1), 2)),
            DMA((count, max(size_a - 1, 1), 2)),
            DMA((count, max(reps - 1, 1), 2)),
        ],
        compiler_params=pltpu.CompilerParams(
            collective_id=collective_id, has_side_effects=True, vmem_limit_bytes=VMEM_LIMIT
        ),
        name=name,
    )(*partials)


def stage_sizes(devices):
    sizes = []
    while devices > 1:
        size = next(s for s in (8, 4, 2, 7, 5, 3, devices) if devices % s == 0)
        sizes.append(size)
        devices //= size
    return sizes


class Exchange:
    def __init__(self, sizes, reps, buffers):
        self.sizes, self.reps = sizes, reps
        self.mine, self.slots, self.sems = buffers[0], buffers[1:-1], buffers[-1]
        place = lax.axis_index("fsdp") * reps + lax.axis_index("rep")
        self.stages = []
        stride = 1
        for size in sizes:
            position = (place // stride) % size
            peers = []
            for d in range(1, size):
                target = place + ((position + d) % size - position) * stride
                peers.append((target // reps, target % reps))
            self.stages.append((size, position, peers))
            stride *= size
        self.peers = [peer for stage in self.stages for peer in stage[2]]
        self.waits = []

    def total(self, round, current, moments):
        number = len(current)
        spans, start = [], 0
        for value in current:
            spans.append((start, value.shape[1]))
            start += value.shape[1]
        for index, (size, position, peers) in enumerate(self.stages):
            used = pl.ds(0, sum(length for _, length in spans))
            mine = self.mine.at[round, index, :, used]
            slots = self.slots[index].at[round, :, :, used]
            for (start, length), value in zip(spans, current):
                mine[:, start : start + length] = value
            for d, (target, rep) in enumerate(peers, 1):
                copy = remote(mine, slots.at[position], self.sems.at[round, index, d - 1], target, rep)
                copy.start()
                self.waits.append(copy)
            slots[position] = mine[...]
            for d, (target, rep) in enumerate(peers, 1):
                there = slots.at[(position + size - d) % size]
                remote(there, there, self.sems.at[round, index, d - 1], target, rep).wait_recv()
            parts = [
                [slots[j, :, start : start + length] for start, length in spans] for j in range(size)
            ]
            current = [functools.reduce(jnp.add, [part[row] for part in parts]) for row in range(number)]
            if moments:
                centre = current[0] / current[2][:, :1]
                squares = current[1]
                for part in parts:
                    count = part[2][:, :1]
                    off = part[0] / count - centre
                    squares = squares + count * off * off
                current[1] = squares
        return current

    def finish(self):
        for copy in self.waits:
            copy.wait_send()


def exchange_buffers(sizes, rounds, total):
    return (
        [pltpu.VMEM((rounds, len(sizes), 1, total), f32)]
        + [pltpu.VMEM((rounds, size, 1, total), f32) for size in sizes]
        + [DMA((rounds, len(sizes), max(max(sizes) - 1, 1), 2))]
    )


def exchange_kernel(sizes, reps, moments, *refs):
    number = 3 if moments else 2
    sources, results = refs[:number], refs[number : 2 * number]
    over = Exchange(sizes, reps, refs[2 * number :])
    greet(over.peers)
    current = over.total(0, [source[...] for source in sources], moments)
    for result, value in zip(results, current):
        result[...] = value
    over.finish()


def exchange(rows, fsdp, reps, moments, collective_id, name):
    sizes = stage_sizes(fsdp * reps)
    width = rows[0].shape[-1]
    padded = -(-width // LANES) * LANES
    rows = [jnp.pad(row.reshape(1, -1), ((0, 0), (0, padded - width))) for row in rows[:2]] + [
        jnp.broadcast_to(row.reshape(1, 1), (1, LANES)) for row in rows[2:]
    ]
    results = pl.pallas_call(
        functools.partial(exchange_kernel, sizes, reps, moments),
        out_shape=[jax.ShapeDtypeStruct(row.shape, f32) for row in rows],
        in_specs=[IN_VMEM] * len(rows),
        out_specs=[IN_VMEM] * len(rows),
        scratch_shapes=exchange_buffers(sizes, 1, sum(row.shape[1] for row in rows)),
        compiler_params=pltpu.CompilerParams(
            collective_id=collective_id, has_side_effects=True, vmem_limit_bytes=4 * 1024 * 1024
        ),
        name=name,
    )(*rows)
    return [result[0, :width] for result in results[:2]] + [result[0, 0] for result in results[2:]]


def dot(left, right):
    return jnp.dot(left, right, preferred_element_type=f32)


def dot_t(left, right):
    return lax.dot_general(left, right, (((1,), (1,)), ((), ())), preferred_element_type=f32)


class Scatter:
    def __init__(self, dims, reps, terms, rows, buffers):
        count = len(terms)
        self.dims, self.reps, self.terms, self.rows = dims, reps, terms, rows
        self.from_rep, self.from_v, self.from_u, self.from_a, self.share = (
            buffers[i * count : (i + 1) * count] for i in range(5)
        )
        self.r_sem, self.v_sem, self.u_sem, self.a_sem, self.s_sem = buffers[5 * count :]
        self.place = Place(dims, reps)
        self.waits = []

    def push(self, source, there, sems, target, target_rep):
        copy = remote(source, there, sems, target, target_rep)
        copy.start()
        self.waits.append(copy)

    def landed(self, there, sems):
        remote(there, there, sems, self.place.me, self.place.rep).wait_recv()

    def part(self, k, index, which):
        rows = self.rows[k]
        start = pl.multiple_of(index * rows, rows)
        return self.terms[k].at[pl.ds(start, rows), columns(self.terms[k].shape[1] // self.reps, which)]

    def order(self):
        size_a, size_b, size_c = self.dims
        for dv in list(range(1, size_c)) + [0]:
            for du in list(range(1, size_b)) + [0]:
                for da in list(range(1, size_a)) + [0]:
                    yield da, du, dv

    def cores(self, k):
        place = self.place
        for da, du, dv in self.order():
            for d in range(1, self.reps):
                other = (place.rep + d) % self.reps
                index = Place(self.dims, self.reps, other).at(da, du, dv)
                self.push(
                    self.part(k, index, other), self.from_rep[k].at[d - 1, index],
                    self.r_sem.at[k, da, du, dv, d - 1], place.me, other,
                )

    def hop(self, k, lag):
        if 0 <= k < len(self.terms):
            for da, du, dv in self.order():
                if lag == (0 if dv else 1 if du else 2 if da else 3):
                    self.handle(k, da, du, dv)

    def handle(self, k, da, du, dv):
        size_a, size_b, size_c = self.dims
        place, reps, rep = self.place, self.reps, self.place.rep
        index = place.at(da, du, dv)
        mine = self.part(k, index, rep)
        total = mine[...].astype(f32)
        for d in range(1, reps):
            self.landed(self.from_rep[k].at[d - 1, index], self.r_sem.at[k, da, du, dv, d - 1])
            total = total + self.from_rep[k][d - 1, index].astype(f32)
        if dv == 0:
            for e in range(1, size_c):
                self.landed(self.from_v[k].at[e - 1, da, du], self.v_sem.at[k, da, du, e - 1])
                total = total + self.from_v[k][e - 1, da, du].astype(f32)
            if du == 0:
                for e in range(1, size_b):
                    self.landed(self.from_u[k].at[e - 1, da], self.u_sem.at[k, da, e - 1])
                    total = total + self.from_u[k][e - 1, da].astype(f32)
                if da == 0:
                    for e in range(1, size_a):
                        self.landed(self.from_a[k].at[e - 1], self.a_sem.at[k, e - 1])
                        total = total + self.from_a[k][e - 1].astype(f32)
        if (da, du, dv) == (0, 0, 0):
            self.share[k][rep] = total.astype(bf16)
            for d in range(1, reps):
                self.push(self.share[k].at[rep], self.share[k].at[rep], self.s_sem.at[k, d - 1], place.me, (rep + d) % reps)
            return
        mine[...] = total.astype(bf16)
        if dv:
            self.push(mine, self.from_v[k].at[dv - 1, da, du], self.v_sem.at[k, da, du, dv - 1], place.at(0, 0, dv), rep)
        elif du:
            self.push(mine, self.from_u[k].at[du - 1, da], self.u_sem.at[k, da, du - 1], place.at(0, du, 0), rep)
        else:
            self.push(mine, self.from_a[k].at[da - 1], self.a_sem.at[k, da - 1], place.at(da, 0, 0), rep)

    def finish(self, totals):
        for k, total in enumerate(totals):
            width = self.terms[k].shape[1] // self.reps
            for d in range(1, self.reps):
                self.landed(self.share[k].at[(self.place.rep + self.reps - d) % self.reps], self.s_sem.at[k, d - 1])
            for which in range(self.reps):
                total[:, which * width : (which + 1) * width] = self.share[k][which].astype(f32)
        for copy in self.waits:
            copy.wait_send()


def scatter_buffers(dims, reps, shapes):
    size_a, size_b, size_c = dims
    count = len(shapes)
    others = max(reps - 1, 1)

    def buffers(*lead):
        return [pltpu.VMEM(lead + (rows, width // reps), bf16) for rows, width in shapes]

    return (
        buffers(others, size_a * size_b * size_c)
        + buffers(max(size_c - 1, 1), size_a, size_b)
        + buffers(max(size_b - 1, 1), size_a)
        + buffers(max(size_a - 1, 1))
        + buffers(reps)
        + [
            DMA((count, size_a, size_b, size_c, others, 2)),
            DMA((count, size_a, size_b, max(size_c - 1, 1), 2)),
            DMA((count, size_a, max(size_b - 1, 1), 2)),
            DMA((count, max(size_a - 1, 1), 2)),
            DMA((count, others, 2)),
        ]
    )


def terms_kernel(dims, reps, rows, *refs):
    (small, block_low, grad_reduced, act_two, grad_expanded, modulated, grad_middle, change, grad_gate) = refs[:9]
    totals = refs[9:15]
    terms = refs[15:21]
    pads, line, turned, chunk, pad_sem, line_sem, chunk_sem, small_sem = refs[21:29]
    scatter = Scatter(dims, reps, terms, rows, refs[29:])
    slots, mid_width = modulated.shape[2:]
    lines = block_low.shape[0]
    width = block_low.shape[2]
    step = chunk.shape[-1]
    chunks = width // step
    ring = 2

    place = scatter.place
    small_copy = pltpu.make_async_copy(small, terms[0], small_sem)
    small_copy.start()
    sources = [(block_low, j) for j in range(chunks)] + [(grad_expanded, j) for j in range(chunks)]

    def load(number):
        source, j = sources[number]
        return pltpu.make_async_copy(
            source.at[:, :, j * step : (j + 1) * step], chunk.at[number % 2], chunk_sem.at[number % 2]
        )

    gradients = [grad_reduced, act_two, grad_middle, grad_gate]

    def turn(number):
        pltpu.make_async_copy(gradients[number], line, line_sem).wait()
        turned[...] = jnp.transpose(line[...].reshape(-1, mid_width))
        if number + 1 < len(gradients):
            pltpu.make_async_copy(gradients[number + 1], line, line_sem).start()

    load(0).start()
    pltpu.make_async_copy(gradients[0], line, line_sem).start()
    inner = pl.ds(ring, GRID)
    for index, source in enumerate((modulated, change)):
        for side in (slice(0, ring), slice(GRID + ring, GRID + 2 * ring)):
            pads[index, side] = jnp.zeros((ring, GRID + 2 * ring, slots, mid_width), bf16)
            pads[index, ring : GRID + ring, side] = jnp.zeros((GRID, ring, slots, mid_width), bf16)
        pltpu.make_async_copy(source, pads.at[index, inner, inner], pad_sem.at[index]).start()
    place.greet()

    small_copy.wait()
    scatter.cores(0)
    turn(0)
    for j in range(chunks):
        if j + 1 < len(sources):
            load(j + 1).start()
        load(j).wait()
        values = dot(turned[...], chunk[j % 2].reshape(-1, step))
        terms[1][j * step : (j + 1) * step, :] = jnp.transpose(values).astype(bf16)
    scatter.cores(1)
    scatter.hop(0, 0)
    turn(1)
    for j in range(chunks):
        number = chunks + j
        if number + 1 < len(sources):
            load(number + 1).start()
        load(number).wait()
        terms[2][:, j * step : (j + 1) * step] = dot(turned[...], chunk[number % 2].reshape(-1, step)).astype(bf16)
    scatter.cores(2)
    scatter.hop(1, 0)
    scatter.hop(0, 1)

    def taps(k, pad, stride):
        def tap(t, _):
            top = ring + (t // 3 - 1) * stride
            left = ring + (t % 3 - 1) * stride
            source = pads[pad, pl.ds(top, GRID), pl.ds(left, GRID)].reshape(-1, mid_width)
            values = dot(turned[...], source)
            start = pl.multiple_of(t * mid_width, mid_width)
            terms[k][pl.ds(start, mid_width), :] = jnp.transpose(values).astype(bf16)
            return 0

        lax.fori_loop(0, 9, tap, 0)
        scatter.cores(k)

    for k, pad, stride in ((3, 0, 1), (4, 1, 1), (5, 1, 2)):
        if k < 5:
            turn(k - 1)
            pltpu.make_async_copy((modulated, change)[pad], pads.at[pad, inner, inner], pad_sem.at[pad]).wait()
        taps(k, pad, stride)
        for lag in range(4):
            scatter.hop(k - 1 - lag, lag)
    for k in range(6, 10):
        for lag in range(4):
            scatter.hop(k - 1 - lag, lag)
    scatter.finish(totals)


def terms_all(small, block_low, grad_reduced, act_two, grad_expanded, modulated, grad_middle, change, grad_gate, rows, fsdp, reps, collective_id):
    dims = factor_three(fsdp)
    lines, line_rows, width = block_low.shape
    mid_width = act_two.shape[-1]
    slots = modulated.shape[2]
    shapes = [(rows[0], width), (rows[1], mid_width), (rows[2], width)] + [(rows[3], mid_width)] * 3
    rows = [rows[0], rows[1], rows[2], rows[3], rows[3], rows[3]]
    side = GRID + 4
    return pl.pallas_call(
        functools.partial(terms_kernel, dims, reps, rows),
        out_shape=[jax.ShapeDtypeStruct(shape, f32) for shape in shapes],
        in_specs=[ANY] * 9,
        out_specs=[IN_VMEM] * 6,
        scratch_shapes=[pltpu.VMEM((fsdp * a, b), bf16) for a, b in shapes]
        + [
            pltpu.VMEM((2, side, side, slots, mid_width), bf16),
            pltpu.VMEM((lines, line_rows, mid_width), bf16),
            pltpu.VMEM((mid_width, lines * line_rows), bf16),
            pltpu.VMEM((2, lines, line_rows, 256), bf16),
            DMA((2,)), DMA(()), DMA((2,)), DMA(()),
        ]
        + scatter_buffers(dims, reps, shapes),
        compiler_params=pltpu.CompilerParams(
            collective_id=collective_id, has_side_effects=True, vmem_limit_bytes=VMEM_LIMIT
        ),
        name="terms",
    )(small, block_low, grad_reduced, act_two, grad_expanded, modulated, grad_middle, change, grad_gate)


TANH_SCALE = 0.7978845608028654
CUBIC = 0.044715


def gelu_parts(x):
    square = x * x
    bend = jnp.tanh(TANH_SCALE * x * (1.0 + CUBIC * square))
    half = 0.5 * (1.0 + bend)
    slope = half + 0.5 * x * (1.0 - bend * bend) * (TANH_SCALE * (1.0 + 3.0 * CUBIC * square))
    return x * half, slope


def fold_rows(values):
    groups, slots, width = values.shape
    return jnp.sum(values.reshape(groups * slots // 8, 8, width), axis=0)


def whole_row(values):
    return jnp.sum(values, axis=0, keepdims=True)


def tail_kernel(sizes, reps, clip_count, *refs):
    (middle, expand, valid, spread, count, gain_two, shift_two, gain_three, shift_three, pooled_grad, block_in) = refs[:11]
    (pooled, grad_pre, grad_expanded, act_two, grad_middle, gain_three_sum, shift_three_sum, gain_two_sum, shift_two_sum) = refs[11:20]
    (wide, wide_grad, narrow, narrow_grad, block, low, totals, first, block_sem, pre_sem, low_sem) = refs[20:31]
    over = Exchange(sizes, reps, refs[31:])
    lines, rows, mid_width = middle.shape
    width = expand.shape[1]
    slots = valid.shape[0]
    segs = slots // clip_count
    groups = rows // slots
    step = 256
    chunks = width // step

    barrier = pltpu.get_barrier_semaphore()
    for target, rep in over.peers:
        pl.semaphore_signal(barrier, inc=1, device_id={"fsdp": target, "rep": rep}, device_id_type=MESH)

    def fetch(y, slot):
        return pltpu.make_async_copy(block_in.at[y], block.at[slot], block_sem.at[slot])

    fetch(0, 0).start()
    mask = valid[:, :1].reshape(1, slots, 1)
    own = count[:, :1]

    def grouped(values):
        return values.reshape(groups, slots, values.shape[-1])

    def moments(carry, origin):
        away, squares = whole_row(carry[0]), whole_row(carry[1])
        return away + own * origin, jnp.maximum(squares - away * away / own, 0.0)

    def gather_moments(carry, values, origin):
        off = (grouped(values) - origin.reshape(1, 1, -1)) * mask
        return carry[0] + fold_rows(off), carry[1] + fold_rows(off * off)

    def blank(n):
        return jnp.zeros((8, n), f32), jnp.zeros((8, n), f32)

    origin = middle[0, 0:1, :]
    carry = lax.fori_loop(0, lines, lambda y, c: gather_moments(c, middle[y], origin), blank(mid_width))
    pl.semaphore_wait(barrier, len(over.peers))
    total, squares, number = over.total(0, list(moments(carry, origin)) + [count[...]], True)
    number = number[:, :1]
    centre_two, inverse_two = total / number, lax.rsqrt(squares / number + epsilon)
    gain2, shift2 = gain_two[...], shift_two[...]

    def zeta_two(normed):
        return mask * (grouped(normed) * gain2.reshape(1, 1, -1) + shift2.reshape(1, 1, -1))

    def forward_two(y, _):
        normed = (middle[y] - centre_two) * inverse_two
        narrow[y] = normed
        act_two[y] = gelu_parts(zeta_two(normed))[0].astype(bf16).reshape(rows, mid_width)
        return 0

    lax.fori_loop(0, lines, forward_two, 0)

    def expand_chunk(j, _):
        cols = pl.ds(pl.multiple_of(j * step, step), step)
        weight = expand[:, cols]
        origin = dot(act_two[0, 0:16, :], weight)[0:1]

        def line(y, carry):
            values = dot(act_two[y], weight)
            wide[y, :, cols] = values
            return gather_moments(carry, values, origin)

        total, squares = moments(lax.fori_loop(0, lines, line, blank(step)), origin)
        totals[0, :, cols] = total
        totals[1, :, cols] = squares
        return 0

    lax.fori_loop(0, chunks, expand_chunk, 0)
    total, squares, _ = over.total(1, [totals[0], totals[1], count[...]], True)
    totals[0] = total / number
    totals[1] = lax.rsqrt(squares / number + epsilon)
    for index in range(2):
        first[index] = jnp.zeros((8, width), f32)

    def out_pre(y):
        return pltpu.make_async_copy(wide_grad.at[y], grad_pre.at[y], pre_sem.at[y])

    def forward_three(y, _):
        slot = y % 2
        fetch(y, slot).wait()

        @pl.when(y + 1 < lines)
        def _():
            fetch(y + 1, 1 - slot).start()

        def chunk(j, _):
            cols = pl.ds(pl.multiple_of(j * step, step), step)
            normed = (wide[y, :, cols] - totals[0, :, cols]) * totals[1, :, cols]
            wide[y, :, cols] = normed
            normed = grouped(normed)
            scaled = mask * (gain_three[:, cols].reshape(1, 1, step) * normed + shift_three[:, cols].reshape(1, 1, step))
            out, slope = gelu_parts(grouped(block[slot, :, cols]) + scaled)
            grads = []
            for clip in range(clip_count):
                span = slice(clip * segs, (clip + 1) * segs)
                share = spread[span, :1].reshape(1, segs, 1)
                pixels = pl.ds(y * groups, groups)
                pooled[clip, pixels, :, cols] = jnp.sum(out[:, span] * share, axis=1, keepdims=True)
                grads.append(slope[:, span] * (pooled_grad[clip, pixels, :, cols] * share))
            grad = jnp.concatenate(grads, axis=1)
            wide_grad[y, :, cols] = grad.reshape(rows, step)
            first[0, :, cols] += fold_rows(grad)
            first[1, :, cols] += fold_rows(grad * normed)
            return 0

        lax.fori_loop(0, chunks, chunk, 0)
        out_pre(y).start()
        return 0

    lax.fori_loop(0, lines, forward_three, 0)
    shift_sum, gain_sum = over.total(2, [whole_row(first[0]), whole_row(first[1])], False)
    shift_three_sum[...] = shift_sum
    gain_three_sum[...] = gain_sum
    totals[2] = shift_sum / number
    totals[3] = gain_sum / number
    totals[1] = totals[1] * gain_three[...]

    def out_low(y):
        return pltpu.make_async_copy(low.at[y % 2], grad_expanded.at[y], low_sem.at[y % 2])

    def back_three(y, carry):
        slot = y % 2

        @pl.when(y >= 2)
        def _():
            out_low(y - 2).wait()

        def chunk(j, _):
            cols = pl.ds(pl.multiple_of(j * step, step), step)
            grad = wide_grad[y, :, cols] - totals[2, :, cols] - wide[y, :, cols] * totals[3, :, cols]
            low[slot, :, cols] = (mask * grouped(grad * totals[1, :, cols])).astype(bf16).reshape(rows, step)
            return 0

        lax.fori_loop(0, chunks, chunk, 0)
        out_low(y).start()
        normed = narrow[y]
        grad = grouped(dot_t(low[slot], expand[...])) * gelu_parts(zeta_two(normed))[1] * mask
        narrow_grad[y] = grad.reshape(rows, mid_width)
        return carry[0] + fold_rows(grad), carry[1] + fold_rows(grad * grouped(normed))

    carry = lax.fori_loop(0, lines, back_three, blank(mid_width))
    shift_sum, gain_sum = over.total(3, [whole_row(carry[0]), whole_row(carry[1])], False)
    shift_two_sum[...] = shift_sum
    gain_two_sum[...] = gain_sum
    shift_mean, gain_mean, scale = shift_sum / number, gain_sum / number, inverse_two * gain2

    def back_two(y, _):
        grad = (narrow_grad[y] - shift_mean - narrow[y] * gain_mean) * scale
        grad_middle[y] = (mask * grouped(grad)).astype(bf16).reshape(rows, mid_width)
        return 0

    lax.fori_loop(0, lines, back_two, 0)
    lax.fori_loop(0, lines, lambda y, _: (out_pre(y).wait(), 0)[1], 0)
    for y in (lines - 2, lines - 1):
        out_low(y).wait()
    over.finish()


def tail(middle, expand, valid, spread, count, gain_two, shift_two, gain_three, shift_three, pooled_grad, block_in, clip_count, fsdp, reps, collective_id):
    sizes = stage_sizes(fsdp * reps)
    lines, rows, mid_width = middle.shape
    width = expand.shape[1]
    pixels = pooled_grad.shape[1]
    shape = jax.ShapeDtypeStruct
    return pl.pallas_call(
        functools.partial(tail_kernel, sizes, reps, clip_count),
        out_shape=[
            shape((clip_count, pixels, 1, width), f32), shape((lines, rows, width), f32), shape((lines, rows, width), bf16),
            shape((lines, rows, mid_width), bf16), shape((lines, rows, mid_width), bf16),
            shape((1, width), f32), shape((1, width), f32), shape((1, mid_width), f32), shape((1, mid_width), f32),
        ],
        in_specs=[IN_VMEM] * 10 + [ANY],
        out_specs=[IN_VMEM, ANY, ANY] + [IN_VMEM] * 6,
        scratch_shapes=[
            pltpu.VMEM((lines, rows, width), f32), pltpu.VMEM((lines, rows, width), f32),
            pltpu.VMEM((lines, rows, mid_width), f32), pltpu.VMEM((lines, rows, mid_width), f32),
            pltpu.VMEM((2, rows, width), f32), pltpu.VMEM((2, rows, width), bf16),
            pltpu.VMEM((4, 1, width), f32), pltpu.VMEM((2, 8, width), f32),
            DMA((2,)), DMA((lines,)), DMA((2,)),
        ] + exchange_buffers(sizes, 4, 2 * width + LANES),
        compiler_params=pltpu.CompilerParams(collective_id=collective_id, has_side_effects=True, vmem_limit_bytes=VMEM_LIMIT),
        name="tail",
    )(middle, expand, valid, spread, count, gain_two, shift_two, gain_three, shift_three, pooled_grad, block_in)


ORDER = ("HWNC", "HWIO", "HWNC")


def pad_of(span):
    return ((span, span), (span, span))


def convolve(source, weight, span, stride):
    side = 2 * span + 1
    kernel = weight.reshape(side, side, source.shape[-1], -1)
    return lax.conv_general_dilated(
        source, kernel, (1, 1), pad_of(span * stride), rhs_dilation=(stride, stride),
        dimension_numbers=ORDER, preferred_element_type=f32,
    )


def convolve_back(grads, weight, span, stride):
    side = 2 * span + 1
    kernel = weight.reshape(side, side, -1, grads.shape[-1])[::-1, ::-1]
    return lax.conv_general_dilated(
        grads, kernel, (1, 1), pad_of(span * stride), rhs_dilation=(stride, stride),
        dimension_numbers=("HWNC", "HWOI", "HWNC"), preferred_element_type=f32,
    )


def convolve_terms(source, grads, span, stride, kind):
    return lax.conv_general_dilated(
        source, grads, (stride, stride), pad_of(span * stride),
        dimension_numbers=("HWCN", "HWIO", "HWNC"), preferred_element_type=kind,
    )


def pool_mean(source):
    total = lax.reduce_window(source, 0.0, lax.add, (3, 3, 1, 1), (1, 1, 1, 1), "SAME")
    return total / 9.0


def project(source, weight):
    return jnp.einsum("yxnc,cd->yxnd", source, weight, preferred_element_type=f32)


def project_back(grads, weight):
    return jnp.einsum("yxnd,cd->yxnc", grads, weight, preferred_element_type=f32)


def project_terms(source, grads, kind):
    return jnp.einsum("yxnc,yxnd->cd", source, grads, preferred_element_type=kind)


def gelu_back(pre_act, grads):
    return jax.vjp(jax.nn.gelu, pre_act)[1](grads)[0]


def make_shards(fsdp, reps):
    def shards(
        frames, features, seg_counts, stem_weight, stem_gain, stem_shift, lateral, reduce_weight,
        gain_one, shift_one, diff_weight, gate_shift, mid_weight, gain_two, shift_two,
        expand_weight, gain_three, shift_three, pooled_grad,
    ):
        clip_count, seg_slots, pixels, feature_width = features.shape
        slots = clip_count * seg_slots
        mid_width = reduce_weight.shape[1]
        stem_rows, stem_depth = stem_weight.shape
        stem_width = stem_rows * fsdp

        seg_index = lax.broadcasted_iota(jnp.int32, (clip_count, seg_slots), 1)
        valid_seg = (seg_index < seg_counts[:, None]).astype(f32)
        pair_seg = valid_seg * jnp.concatenate(
            [valid_seg[:, 1:], jnp.zeros((clip_count, 1), f32)], axis=1
        )
        valid = valid_seg.reshape(1, 1, slots, 1)
        pair = pair_seg.reshape(1, 1, slots, 1)
        count_float = seg_counts.astype(f32)
        local_count = jnp.sum(count_float) * pixels

        vectors = [gain_three, shift_three, gain_one, shift_one, gate_shift, gain_two, shift_two, stem_gain, stem_shift]
        row = jnp.concatenate(vectors)
        small = jnp.concatenate(
            [
                lateral,
                jnp.pad(stem_weight, ((0, 0), (0, feature_width - stem_depth))),
                jnp.pad(row[None], ((0, 15 - 2 * stem_rows), (0, feature_width - row.shape[0]))),
            ]
        )
        small_full, reduce_full, diff_full, mid_full, expand_full = gather_all(
            [small, reduce_weight, diff_weight, mid_weight, expand_weight], fsdp, reps, 1, "gather_weights"
        )
        lateral_full = small_full[:, :stem_rows].reshape(stem_width, feature_width)
        stem_full = small_full[:, stem_rows : 2 * stem_rows, :stem_depth].reshape(stem_width, stem_depth)
        full = []
        start = 0
        for vector in vectors:
            size = vector.shape[0]
            full.append(small_full[:, 2 * stem_rows, start : start + size].reshape(-1).astype(f32))
            start += size
        (gain_three_full, shift_three_full, gain_one_full, shift_one_full, gate_full, gain_two_full,
         shift_two_full, stem_gain_full, stem_shift_full) = full
        reduce_full = reduce_full.reshape(-1, mid_width)
        diff_full = diff_full.reshape(2, -1, mid_width)
        mid_full = mid_full.reshape(-1, mid_width)
        expand_full = expand_full.reshape(mid_width, -1)

        def moments(values, collective_id, name):
            total = jnp.sum(values * valid, axis=(0, 1, 2))
            off = values - total / local_count
            squares = jnp.sum(off * off * valid, axis=(0, 1, 2))
            total, squares, count = exchange(
                [total, squares, local_count], fsdp, reps, True, collective_id, name
            )
            centre = total / count
            return centre, lax.rsqrt(squares / count + epsilon), count

        def norm(values, stats, gain, shift):
            normed = (values - stats[0]) * stats[1]
            return valid * (gain * normed + shift), normed

        def norm_back(grad_out, normed, stats, gain, collective_id, name):
            masked = grad_out * valid
            shift_sum, gain_sum = exchange(
                [jnp.sum(masked, axis=(0, 1, 2)), jnp.sum(masked * normed, axis=(0, 1, 2))],
                fsdp, reps, False, collective_id, name,
            )
            grad_in = valid * stats[1] * gain * (masked - shift_sum / stats[2] - normed * gain_sum / stats[2])
            return grad_in.astype(bf16), gain_sum, shift_sum

        moving = frames.astype(f32)
        motion = (moving[:, :, 1:] - moving[:, :, :-1]) * valid_seg[:, :, None, None, None]
        motion = jnp.transpose(motion.astype(bf16), (4, 0, 1, 2, 3)).reshape(GRID, GRID, slots, -1)
        stem_kernel = jnp.transpose(stem_full.reshape(stem_width, GRID, GRID, -1), (1, 2, 3, 0))
        stem_pre = convolve(motion, stem_kernel, 3, 1)
        stem_stats = moments(stem_pre, 2, "stem_moments")
        stem_norm, stem_normed = norm(stem_pre, stem_stats, stem_gain_full, stem_shift_full)
        pool_low = pool_mean(jax.nn.gelu(stem_norm)).astype(bf16)
        turned = jnp.transpose(features.reshape(slots, GRID, GRID, feature_width), (1, 2, 0, 3))
        block_in = turned.astype(f32) + project(pool_low, lateral_full)
        block_low = block_in.astype(bf16)
        reduced = project(block_low, reduce_full)
        stats_one = moments(reduced, 3, "moments_one")
        zeta_one, normed_one = norm(reduced, stats_one, gain_one_full, shift_one_full)
        act_one = jax.nn.gelu(zeta_one)
        def later_of(values):
            grid = values.reshape(GRID, GRID, clip_count, seg_slots, -1)
            return jnp.pad(grid[:, :, :, 1:], ((0, 0), (0, 0), (0, 0), (0, 1), (0, 0))).reshape(values.shape)

        def earlier_of(values):
            grid = values.reshape(GRID, GRID, clip_count, seg_slots, -1)
            return jnp.pad(grid[:, :, :, :-1], ((0, 0), (0, 0), (0, 0), (1, 0), (0, 0))).reshape(values.shape)

        change = ((later_of(act_one) - act_one) * pair).astype(bf16)
        gate_pre = convolve(change, diff_full[0], 1, 1) + convolve(change, diff_full[1], 1, 2)
        gate = jax.nn.sigmoid(gate_pre + gate_full)
        modulated = (act_one * (1.0 + gate)).astype(bf16)
        middle = convolve(modulated, mid_full, 1, 1)
        flat = (GRID, GRID * slots, -1)
        lanes = lambda column: jnp.broadcast_to(column.reshape(-1, 1), (column.size, LANES))
        (pooled, grad_pre, grad_expanded, act_two, grad_middle, gain_three_sum, shift_three_sum, gain_two_sum,
         shift_two_sum) = tail(
            middle.reshape(flat), expand_full, lanes(valid_seg), lanes(valid_seg / count_float[:, None]), lanes(local_count),
            gain_two_full[None], shift_two_full[None], gain_three_full[None], shift_three_full[None],
            pooled_grad.astype(f32)[:, :, None], block_in.reshape(flat), clip_count, fsdp, reps, 4,
        )
        pooled = pooled.reshape(pooled_grad.shape).astype(bf16)
        gain_three_sum, shift_three_sum, gain_two_sum, shift_two_sum = (
            row[0] for row in (gain_three_sum, shift_three_sum, gain_two_sum, shift_two_sum)
        )
        cube = (GRID, GRID, slots, -1)
        grad_pre, grad_expanded, act_two, grad_middle = (
            block.reshape(cube) for block in (grad_pre, grad_expanded, act_two, grad_middle)
        )
        grad_modulated = convolve_back(grad_middle, mid_full, 1, 1)
        grad_gate_pre = grad_modulated * act_one * gate * (1.0 - gate)
        gate_terms = jnp.sum(grad_gate_pre, axis=(0, 1, 2))
        grad_gate = grad_gate_pre.astype(bf16)
        grad_change = convolve_back(grad_gate, diff_full[0], 1, 1) + convolve_back(grad_gate, diff_full[1], 1, 2)
        grad_change = grad_change * pair
        grad_act_one = grad_modulated * (1.0 + gate) + earlier_of(grad_change) - grad_change
        grad_reduced, gain_one_sum, shift_one_sum = norm_back(
            gelu_back(zeta_one, grad_act_one), normed_one, stats_one, gain_one_full, 8, "sums_one"
        )
        features_grad = grad_pre + project_back(grad_reduced, reduce_full)
        grad_lateral = features_grad.astype(bf16)
        lateral_terms = project_terms(pool_low, grad_lateral, bf16)
        grad_act = pool_mean(project_back(grad_lateral, lateral_full))
        grad_stem, stem_gain_sum, stem_shift_sum = norm_back(
            gelu_back(stem_norm, grad_act), stem_normed, stem_stats, stem_gain_full, 9, "sums_stem"
        )
        stem_terms = convolve_terms(motion, grad_stem, 3, 1, bf16)
        stem_terms = jnp.transpose(stem_terms, (3, 0, 1, 2)).reshape(fsdp, stem_rows, stem_depth)
        gate_rows = gate_shift.shape[0]
        small_terms = jnp.concatenate(
            [
                lateral_terms.reshape(fsdp, stem_rows, feature_width),
                jnp.pad(stem_terms, ((0, 0), (0, 0), (0, feature_width - stem_depth))),
                jnp.pad(
                    gate_terms.astype(bf16).reshape(fsdp, 1, gate_rows),
                    ((0, 0), (0, 15 - 2 * stem_rows), (0, feature_width - gate_rows)),
                ),
            ],
            axis=1,
        )

        conv_rows = mid_weight.shape[0]
        if conv_rows % 32 == 0:
            small_part, reduce_part, expand_part, mid_part, diff_one, diff_two = terms_all(
                small_terms.reshape(-1, feature_width), block_low.reshape(flat), grad_reduced.reshape(flat),
                act_two.reshape(flat), grad_expanded.reshape(flat), modulated, grad_middle.reshape(flat), change,
                grad_gate.reshape(flat),
                [small_terms.shape[1], reduce_weight.shape[0], expand_weight.shape[0], conv_rows], fsdp, reps, 10,
            )
        else:
            def owned(terms, shard):
                return terms.reshape((fsdp,) + shard.shape[-2:])

            small_part, reduce_part, expand_part, mid_part, diff_one, diff_two = scatter_all(
                [
                    small_terms,
                    owned(project_terms(block_low, grad_reduced, bf16), reduce_weight),
                    owned(project_terms(act_two, grad_expanded, bf16), expand_weight),
                    owned(convolve_terms(modulated, grad_middle, 1, 1, bf16), mid_weight),
                    owned(convolve_terms(change, grad_gate, 1, 1, bf16), diff_weight),
                    owned(convolve_terms(change, grad_gate, 1, 2, bf16), diff_weight),
                ],
                fsdp, reps, 11, "scatter_terms",
            )

        def own_share(whole):
            share = whole.shape[0] // fsdp
            return lax.dynamic_slice_in_dim(whole, lax.axis_index("fsdp") * share, share)

        out = jnp.transpose(features_grad, (2, 0, 1, 3)).reshape(features.shape)
        return (
            pooled,
            out,
            small_part[stem_rows : 2 * stem_rows, :stem_depth],
            own_share(stem_gain_sum),
            own_share(stem_shift_sum),
            small_part[:stem_rows],
            reduce_part,
            own_share(gain_one_sum),
            own_share(shift_one_sum),
            jnp.stack([diff_one, diff_two]),
            small_part[2 * stem_rows, :gate_rows],
            mid_part,
            own_share(gain_two_sum),
            own_share(shift_two_sum),
            expand_part,
            own_share(gain_three_sum),
            own_share(shift_three_sum),
        )

    return shards


def solution(mesh):
    whole = ("fsdp", "rep")
    matrix, vector = P("fsdp", None), P("fsdp")
    in_specs = (
        P(whole, None, None, None, None), P(whole, None, None, None), P(whole),
        matrix, vector, vector, matrix, matrix, vector, vector, P(None, "fsdp", None), vector,
        matrix, vector, vector, matrix, vector, vector, P(whole, None, None),
    )
    out_specs = (
        P(whole, None, None), P(whole, None, None, None), matrix, vector, vector, matrix, matrix,
        vector, vector, P(None, "fsdp", None), vector, matrix, vector, vector, matrix, vector, vector,
    )
    body = make_shards(mesh.shape["fsdp"], mesh.shape["rep"])
    return jax.shard_map(body, mesh=mesh, in_specs=in_specs, out_specs=out_specs, check_vma=False)
```

```python
import functools

import jax
import jax.numpy as jnp
from jax import lax
from jax.experimental import pallas as pl
from jax.experimental.pallas import tpu as pltpu
from jax.sharding import PartitionSpec as P

GRID = 7
LANES = 128
PIXELS = GRID * GRID
epsilon = 1e-05
MESH = pl.DeviceIdType.MESH
ANY = pl.BlockSpec(memory_space=pl.ANY)
IN_VMEM = pl.BlockSpec(memory_space=pltpu.VMEM)
VMEM_LIMIT = 60 * 1024 * 1024
bf16 = jnp.bfloat16
f32 = jnp.float32
DMA = pltpu.SemaphoreType.DMA


def factor_three(size):
    best = None
    for b in range(1, size + 1):
        for c in range(1, b + 1):
            if size % (b * c) == 0 and size // (b * c) >= b:
                a = size // (b * c)
                if best is None or a + b + c < sum(best):
                    best = (a, b, c)
    return best


class Place:
    def __init__(self, dims, reps, rep=None):
        self.dims, self.reps = dims, reps
        size_a, size_b, size_c = dims
        self.me = lax.axis_index("fsdp")
        self.rep = lax.axis_index("rep") if rep is None else rep
        ib, ic = (self.me // size_c) % size_b, self.me % size_c
        self.ia = self.me // (size_b * size_c)
        odd = self.rep % 2 if size_b == size_c else 0
        self.stride_u = size_c * (1 - odd) + odd
        self.stride_v = (1 - odd) + size_c * odd
        self.iu = ib * (1 - odd) + ic * odd
        self.iv = ic * (1 - odd) + ib * odd

    def at(self, da, du, dv):
        size_a, size_b, size_c = self.dims
        a = (self.ia + da + size_a) % size_a
        u = (self.iu + du + size_b) % size_b
        v = (self.iv + dv + size_c) % size_c
        return a * (size_b * size_c) + u * self.stride_u + v * self.stride_v

    def greet(self, more=()):
        size_a, size_b, size_c = self.dims
        peers = [(self.at(d, 0, 0), self.rep) for d in range(1, size_a)]
        peers += [(self.at(0, d, 0), self.rep) for d in range(1, size_b)]
        peers += [(self.at(0, 0, d), self.rep) for d in range(1, size_c)]
        peers += [(self.me, (self.rep + d) % self.reps) for d in range(1, self.reps)]
        greet(peers + list(more))


def greet(peers):
    barrier = pltpu.get_barrier_semaphore()
    for target, rep in peers:
        pl.semaphore_signal(
            barrier, inc=1, device_id={"fsdp": target, "rep": rep}, device_id_type=MESH
        )
    pl.semaphore_wait(barrier, len(peers))


def remote(src, dst, sems, target, rep):
    return pltpu.make_async_remote_copy(
        src_ref=src,
        dst_ref=dst,
        send_sem=sems.at[0],
        recv_sem=sems.at[1],
        device_id={"fsdp": target, "rep": rep},
        device_id_type=MESH,
    )


def columns(width, which):
    start = which * width
    return pl.ds(start if isinstance(start, int) else pl.multiple_of(start, width), width)


def views(refs):
    out = []
    for ref, stacked in refs:
        out += [ref.at[j] for j in range(ref.shape[0])] if stacked else [ref]
    return out


def scatter_kernel(dims, reps, stacked, *refs):
    number = len(stacked)
    partials = views(zip(refs[:number], stacked))
    totals = views(zip(refs[number : 2 * number], stacked))
    count = len(partials)
    rest = refs[2 * number :]
    held, from_rep, from_v, from_u, from_a, share = (rest[i * count : (i + 1) * count] for i in range(6))
    own_sem, r_sem, v_sem, u_sem, a_sem, s_sem = rest[6 * count :]
    size_a, size_b, size_c = dims
    place = Place(dims, reps)
    me, rep = place.me, place.rep
    place.greet()
    waits = []

    def push(source, there, sems, target, target_rep):
        copy = remote(source, there, sems, target, target_rep)
        copy.start()
        waits.append(copy)

    def landed(there, sems):
        remote(there, there, sems, me, rep).wait_recv()

    def order():
        for dv in list(range(1, size_c)) + [0]:
            for du in list(range(1, size_b)) + [0]:
                for da in list(range(1, size_a)) + [0]:
                    yield da, du, dv

    local = {}
    for k in range(count):
        width = partials[k].shape[-1] // reps
        for da, du, dv in order():
            for d in range(1, reps):
                other = (rep + d) % reps
                index = Place(dims, reps, other).at(da, du, dv)
                push(
                    partials[k].at[index, :, columns(width, other)],
                    from_rep[k].at[d - 1, index],
                    r_sem.at[k, da, du, dv, d - 1],
                    me,
                    other,
                )
            index = place.at(da, du, dv)
            copy = pltpu.make_async_copy(
                partials[k].at[index, :, columns(width, rep)],
                held[k].at[index],
                own_sem.at[k, da, du, dv],
            )
            copy.start()
            local[k, da, du, dv] = copy

    def handle(k, da, du, dv):
        index = place.at(da, du, dv)
        local[k, da, du, dv].wait()
        total = held[k][index].astype(f32)
        for d in range(1, reps):
            landed(from_rep[k].at[d - 1, index], r_sem.at[k, da, du, dv, d - 1])
            total = total + from_rep[k][d - 1, index].astype(f32)
        if dv == 0:
            for e in range(1, size_c):
                landed(from_v[k].at[e - 1, da, du], v_sem.at[k, da, du, e - 1])
                total = total + from_v[k][e - 1, da, du].astype(f32)
            if du == 0:
                for e in range(1, size_b):
                    landed(from_u[k].at[e - 1, da], u_sem.at[k, da, e - 1])
                    total = total + from_u[k][e - 1, da].astype(f32)
                if da == 0:
                    for e in range(1, size_a):
                        landed(from_a[k].at[e - 1], a_sem.at[k, e - 1])
                        total = total + from_a[k][e - 1].astype(f32)
        if (da, du, dv) == (0, 0, 0):
            share[k][rep] = total.astype(bf16)
            for d in range(1, reps):
                push(share[k].at[rep], share[k].at[rep], s_sem.at[k, d - 1], me, (rep + d) % reps)
            return
        held[k][index] = total.astype(bf16)
        if dv:
            push(held[k].at[index], from_v[k].at[dv - 1, da, du], v_sem.at[k, da, du, dv - 1], place.at(0, 0, dv), rep)
        elif du:
            push(held[k].at[index], from_u[k].at[du - 1, da], u_sem.at[k, da, du - 1], place.at(0, du, 0), rep)
        else:
            push(held[k].at[index], from_a[k].at[da - 1], a_sem.at[k, da - 1], place.at(da, 0, 0), rep)

    for step in range(count + 3):
        for lag in range(4):
            k = step - lag
            for da, du, dv in order() if 0 <= k < count else ():
                if lag == (0 if dv else 1 if du else 2 if da else 3):
                    handle(k, da, du, dv)
    for k in range(count):
        width = partials[k].shape[-1] // reps
        for d in range(1, reps):
            landed(share[k].at[(rep + reps - d) % reps], s_sem.at[k, d - 1])
        for which in range(reps):
            totals[k][:, which * width : (which + 1) * width] = share[k][which].astype(f32)
    for copy in waits:
        copy.wait_send()


def scatter_all(partials, fsdp, reps, collective_id, name):
    dims = factor_three(fsdp)
    size_a, size_b, size_c = dims
    stacked = [p.ndim == 4 for p in partials]
    shapes = []
    for p in partials:
        shapes += [(p.shape[-2], p.shape[-1] // reps)] * (p.shape[0] if p.ndim == 4 else 1)
    count = len(shapes)

    def buffers(*lead):
        return [pltpu.VMEM(lead + shape, bf16) for shape in shapes]

    return pl.pallas_call(
        functools.partial(scatter_kernel, dims, reps, stacked),
        out_shape=[
            jax.ShapeDtypeStruct(p.shape[:-3] + p.shape[-2:], f32) for p in partials
        ],
        in_specs=[ANY] * len(partials),
        out_specs=[IN_VMEM] * len(partials),
        scratch_shapes=buffers(fsdp)
        + buffers(max(reps - 1, 1), fsdp)
        + buffers(max(size_c - 1, 1), size_a, size_b)
        + buffers(max(size_b - 1, 1), size_a)
        + buffers(max(size_a - 1, 1))
        + buffers(reps)
        + [
            DMA((count, size_a, size_b, size_c)),
            DMA((count, size_a, size_b, size_c, max(reps - 1, 1), 2)),
            DMA((count, size_a, size_b, max(size_c - 1, 1), 2)),
            DMA((count, size_a, max(size_b - 1, 1), 2)),
            DMA((count, max(size_a - 1, 1), 2)),
            DMA((count, max(reps - 1, 1), 2)),
        ],
        compiler_params=pltpu.CompilerParams(
            collective_id=collective_id, has_side_effects=True, vmem_limit_bytes=VMEM_LIMIT
        ),
        name=name,
    )(*partials)


def stage_sizes(devices):
    sizes = []
    while devices > 1:
        size = next(s for s in (8, 4, 2, 7, 5, 3, devices) if devices % s == 0)
        sizes.append(size)
        devices //= size
    return sizes


class Exchange:
    def __init__(self, sizes, reps, buffers):
        self.sizes, self.reps = sizes, reps
        self.mine, self.slots, self.sems = buffers[0], buffers[1:-1], buffers[-1]
        place = lax.axis_index("fsdp") * reps + lax.axis_index("rep")
        self.stages = []
        stride = 1
        for size in sizes:
            position = (place // stride) % size
            peers = []
            for d in range(1, size):
                target = place + ((position + d) % size - position) * stride
                peers.append((target // reps, target % reps))
            self.stages.append((size, position, peers))
            stride *= size
        self.peers = [peer for stage in self.stages for peer in stage[2]]
        self.waits = []

    def total(self, round, current, moments):
        number = len(current)
        spans, start = [], 0
        for value in current:
            spans.append((start, value.shape[1]))
            start += value.shape[1]
        for index, (size, position, peers) in enumerate(self.stages):
            used = pl.ds(0, sum(length for _, length in spans))
            mine = self.mine.at[round, index, :, used]
            slots = self.slots[index].at[round, :, :, used]
            for (start, length), value in zip(spans, current):
                mine[:, start : start + length] = value
            for d, (target, rep) in enumerate(peers, 1):
                copy = remote(mine, slots.at[position], self.sems.at[round, index, d - 1], target, rep)
                copy.start()
                self.waits.append(copy)
            slots[position] = mine[...]
            for d, (target, rep) in enumerate(peers, 1):
                there = slots.at[(position + size - d) % size]
                remote(there, there, self.sems.at[round, index, d - 1], target, rep).wait_recv()
            parts = [
                [slots[j, :, start : start + length] for start, length in spans] for j in range(size)
            ]
            current = [functools.reduce(jnp.add, [part[row] for part in parts]) for row in range(number)]
            if moments:
                centre = current[0] / current[2][:, :1]
                squares = current[1]
                for part in parts:
                    count = part[2][:, :1]
                    off = part[0] / count - centre
                    squares = squares + count * off * off
                current[1] = squares
        return current

    def finish(self):
        for copy in self.waits:
            copy.wait_send()


def exchange_buffers(sizes, rounds, total):
    return (
        [pltpu.VMEM((rounds, len(sizes), 1, total), f32)]
        + [pltpu.VMEM((rounds, size, 1, total), f32) for size in sizes]
        + [DMA((rounds, len(sizes), max(max(sizes) - 1, 1), 2))]
    )


def exchange_kernel(sizes, reps, moments, *refs):
    number = 3 if moments else 2
    sources, results = refs[:number], refs[number : 2 * number]
    over = Exchange(sizes, reps, refs[2 * number :])
    greet(over.peers)
    current = over.total(0, [source[...] for source in sources], moments)
    for result, value in zip(results, current):
        result[...] = value
    over.finish()


def exchange(rows, fsdp, reps, moments, collective_id, name):
    sizes = stage_sizes(fsdp * reps)
    width = rows[0].shape[-1]
    padded = -(-width // LANES) * LANES
    rows = [jnp.pad(row.reshape(1, -1), ((0, 0), (0, padded - width))) for row in rows[:2]] + [
        jnp.broadcast_to(row.reshape(1, 1), (1, LANES)) for row in rows[2:]
    ]
    results = pl.pallas_call(
        functools.partial(exchange_kernel, sizes, reps, moments),
        out_shape=[jax.ShapeDtypeStruct(row.shape, f32) for row in rows],
        in_specs=[IN_VMEM] * len(rows),
        out_specs=[IN_VMEM] * len(rows),
        scratch_shapes=exchange_buffers(sizes, 1, sum(row.shape[1] for row in rows)),
        compiler_params=pltpu.CompilerParams(
            collective_id=collective_id, has_side_effects=True, vmem_limit_bytes=4 * 1024 * 1024
        ),
        name=name,
    )(*rows)
    return [result[0, :width] for result in results[:2]] + [result[0, 0] for result in results[2:]]


TANH_SCALE = 0.7978845608028654
CUBIC = 0.044715


def gelu_parts(x):
    square = x * x
    bend = jnp.tanh(TANH_SCALE * x * (1.0 + CUBIC * square))
    half = 0.5 * (1.0 + bend)
    slope = half + 0.5 * x * (1.0 - bend * bend) * (TANH_SCALE * (1.0 + 3.0 * CUBIC * square))
    return x * half, slope


def fold_rows(values):
    groups, slots, width = values.shape
    return jnp.sum(values.reshape(groups * slots // 8, 8, width), axis=0)


def whole_row(values):
    return jnp.sum(values, axis=0, keepdims=True)


def dot(left, right):
    return jnp.dot(left, right, preferred_element_type=f32)


def dot_t(left, right):
    return lax.dot_general(left, right, (((1,), (1,)), ((), ())), preferred_element_type=f32)


class Scatter:
    def __init__(self, dims, reps, terms, rows, buffers):
        count = len(terms)
        self.dims, self.reps, self.terms, self.rows = dims, reps, terms, rows
        self.from_rep, self.from_v, self.from_u, self.from_a, self.share = (
            buffers[i * count : (i + 1) * count] for i in range(5)
        )
        self.r_sem, self.v_sem, self.u_sem, self.a_sem, self.s_sem = buffers[5 * count :]
        self.place = Place(dims, reps)
        self.waits = []

    def push(self, source, there, sems, target, target_rep):
        copy = remote(source, there, sems, target, target_rep)
        copy.start()
        self.waits.append(copy)

    def landed(self, there, sems):
        remote(there, there, sems, self.place.me, self.place.rep).wait_recv()

    def part(self, k, index, which):
        rows = self.rows[k]
        start = pl.multiple_of(index * rows, rows)
        return self.terms[k].at[pl.ds(start, rows), columns(self.terms[k].shape[1] // self.reps, which)]

    def order(self):
        size_a, size_b, size_c = self.dims
        for dv in list(range(1, size_c)) + [0]:
            for du in list(range(1, size_b)) + [0]:
                for da in list(range(1, size_a)) + [0]:
                    yield da, du, dv

    def cores(self, k):
        place = self.place
        for da, du, dv in self.order():
            for d in range(1, self.reps):
                other = (place.rep + d) % self.reps
                index = Place(self.dims, self.reps, other).at(da, du, dv)
                self.push(
                    self.part(k, index, other), self.from_rep[k].at[d - 1, index],
                    self.r_sem.at[k, da, du, dv, d - 1], place.me, other,
                )

    def hop(self, k, lag):
        if 0 <= k < len(self.terms):
            for da, du, dv in self.order():
                if lag == (0 if dv else 1 if du else 2 if da else 3):
                    self.handle(k, da, du, dv)

    def handle(self, k, da, du, dv):
        size_a, size_b, size_c = self.dims
        place, reps, rep = self.place, self.reps, self.place.rep
        index = place.at(da, du, dv)
        mine = self.part(k, index, rep)
        total = mine[...].astype(f32)
        for d in range(1, reps):
            self.landed(self.from_rep[k].at[d - 1, index], self.r_sem.at[k, da, du, dv, d - 1])
            total = total + self.from_rep[k][d - 1, index].astype(f32)
        if dv == 0:
            for e in range(1, size_c):
                self.landed(self.from_v[k].at[e - 1, da, du], self.v_sem.at[k, da, du, e - 1])
                total = total + self.from_v[k][e - 1, da, du].astype(f32)
            if du == 0:
                for e in range(1, size_b):
                    self.landed(self.from_u[k].at[e - 1, da], self.u_sem.at[k, da, e - 1])
                    total = total + self.from_u[k][e - 1, da].astype(f32)
                if da == 0:
                    for e in range(1, size_a):
                        self.landed(self.from_a[k].at[e - 1], self.a_sem.at[k, e - 1])
                        total = total + self.from_a[k][e - 1].astype(f32)
        if (da, du, dv) == (0, 0, 0):
            self.share[k][rep] = total.astype(bf16)
            for d in range(1, reps):
                self.push(self.share[k].at[rep], self.share[k].at[rep], self.s_sem.at[k, d - 1], place.me, (rep + d) % reps)
            return
        mine[...] = total.astype(bf16)
        if dv:
            self.push(mine, self.from_v[k].at[dv - 1, da, du], self.v_sem.at[k, da, du, dv - 1], place.at(0, 0, dv), rep)
        elif du:
            self.push(mine, self.from_u[k].at[du - 1, da], self.u_sem.at[k, da, du - 1], place.at(0, du, 0), rep)
        else:
            self.push(mine, self.from_a[k].at[da - 1], self.a_sem.at[k, da - 1], place.at(da, 0, 0), rep)

    def finish(self, totals):
        for k, total in enumerate(totals):
            width = self.terms[k].shape[1] // self.reps
            for d in range(1, self.reps):
                self.landed(self.share[k].at[(self.place.rep + self.reps - d) % self.reps], self.s_sem.at[k, d - 1])
            for which in range(self.reps):
                total[:, which * width : (which + 1) * width] = self.share[k][which].astype(f32)
        for copy in self.waits:
            copy.wait_send()


def scatter_buffers(dims, reps, shapes):
    size_a, size_b, size_c = dims
    count = len(shapes)
    others = max(reps - 1, 1)

    def buffers(*lead):
        return [pltpu.VMEM(lead + (rows, width // reps), bf16) for rows, width in shapes]

    return (
        buffers(others, size_a * size_b * size_c)
        + buffers(max(size_c - 1, 1), size_a, size_b)
        + buffers(max(size_b - 1, 1), size_a)
        + buffers(max(size_a - 1, 1))
        + buffers(reps)
        + [
            DMA((count, size_a, size_b, size_c, others, 2)),
            DMA((count, size_a, size_b, max(size_c - 1, 1), 2)),
            DMA((count, size_a, max(size_b - 1, 1), 2)),
            DMA((count, max(size_a - 1, 1), 2)),
            DMA((count, others, 2)),
        ]
    )


def terms_kernel(dims, reps, rows, *refs):
    (small, block_low, grad_reduced, act_two, grad_expanded, modulated, grad_middle, change, grad_gate) = refs[:9]
    totals = refs[9:15]
    terms = refs[15:21]
    pads, line, turned, chunk, pad_sem, line_sem, chunk_sem, small_sem = refs[21:29]
    scatter = Scatter(dims, reps, terms, rows, refs[29:])
    slots, mid_width = modulated.shape[2:]
    lines = block_low.shape[0]
    width = block_low.shape[2]
    step = chunk.shape[-1]
    chunks = width // step
    ring = 2

    place = scatter.place
    small_copy = pltpu.make_async_copy(small, terms[0], small_sem)
    small_copy.start()
    sources = [(block_low, j) for j in range(chunks)] + [(grad_expanded, j) for j in range(chunks)]

    def load(number):
        source, j = sources[number]
        return pltpu.make_async_copy(
            source.at[:, :, j * step : (j + 1) * step], chunk.at[number % 2], chunk_sem.at[number % 2]
        )

    gradients = [grad_reduced, act_two, grad_middle, grad_gate]

    def turn(number):
        pltpu.make_async_copy(gradients[number], line, line_sem).wait()
        turned[...] = jnp.transpose(line[...].reshape(-1, mid_width))
        if number + 1 < len(gradients):
            pltpu.make_async_copy(gradients[number + 1], line, line_sem).start()

    load(0).start()
    pltpu.make_async_copy(gradients[0], line, line_sem).start()
    inner = pl.ds(ring, GRID)
    for index, source in enumerate((modulated, change)):
        for side in (slice(0, ring), slice(GRID + ring, GRID + 2 * ring)):
            pads[index, side] = jnp.zeros((ring, GRID + 2 * ring, slots, mid_width), bf16)
            pads[index, ring : GRID + ring, side] = jnp.zeros((GRID, ring, slots, mid_width), bf16)
        pltpu.make_async_copy(source, pads.at[index, inner, inner], pad_sem.at[index]).start()
    place.greet()

    small_copy.wait()
    scatter.cores(0)
    turn(0)
    for j in range(chunks):
        if j + 1 < len(sources):
            load(j + 1).start()
        load(j).wait()
        values = dot(turned[...], chunk[j % 2].reshape(-1, step))
        terms[1][j * step : (j + 1) * step, :] = jnp.transpose(values).astype(bf16)
    scatter.cores(1)
    scatter.hop(0, 0)
    turn(1)
    for j in range(chunks):
        number = chunks + j
        if number + 1 < len(sources):
            load(number + 1).start()
        load(number).wait()
        terms[2][:, j * step : (j + 1) * step] = dot(turned[...], chunk[number % 2].reshape(-1, step)).astype(bf16)
    scatter.cores(2)
    scatter.hop(1, 0)
    scatter.hop(0, 1)

    def taps(k, pad, stride):
        def tap(t, _):
            top = ring + (t // 3 - 1) * stride
            left = ring + (t % 3 - 1) * stride
            source = pads[pad, pl.ds(top, GRID), pl.ds(left, GRID)].reshape(-1, mid_width)
            values = dot(turned[...], source)
            start = pl.multiple_of(t * mid_width, mid_width)
            terms[k][pl.ds(start, mid_width), :] = jnp.transpose(values).astype(bf16)
            return 0

        lax.fori_loop(0, 9, tap, 0)
        scatter.cores(k)

    for k, pad, stride in ((3, 0, 1), (4, 1, 1), (5, 1, 2)):
        if k < 5:
            turn(k - 1)
            pltpu.make_async_copy((modulated, change)[pad], pads.at[pad, inner, inner], pad_sem.at[pad]).wait()
        taps(k, pad, stride)
        for lag in range(4):
            scatter.hop(k - 1 - lag, lag)
    for k in range(6, 10):
        for lag in range(4):
            scatter.hop(k - 1 - lag, lag)
    scatter.finish(totals)


def terms_all(small, block_low, grad_reduced, act_two, grad_expanded, modulated, grad_middle, change, grad_gate, rows, fsdp, reps, collective_id):
    dims = factor_three(fsdp)
    lines, line_rows, width = block_low.shape
    mid_width = act_two.shape[-1]
    slots = modulated.shape[2]
    shapes = [(rows[0], width), (rows[1], mid_width), (rows[2], width)] + [(rows[3], mid_width)] * 3
    rows = [rows[0], rows[1], rows[2], rows[3], rows[3], rows[3]]
    side = GRID + 4
    return pl.pallas_call(
        functools.partial(terms_kernel, dims, reps, rows),
        out_shape=[jax.ShapeDtypeStruct(shape, f32) for shape in shapes],
        in_specs=[ANY] * 9,
        out_specs=[IN_VMEM] * 6,
        scratch_shapes=[pltpu.VMEM((fsdp * a, b), bf16) for a, b in shapes]
        + [
            pltpu.VMEM((2, side, side, slots, mid_width), bf16),
            pltpu.VMEM((lines, line_rows, mid_width), bf16),
            pltpu.VMEM((mid_width, lines * line_rows), bf16),
            pltpu.VMEM((2, lines, line_rows, 256), bf16),
            DMA((2,)), DMA(()), DMA((2,)), DMA(()),
        ]
        + scatter_buffers(dims, reps, shapes),
        compiler_params=pltpu.CompilerParams(
            collective_id=collective_id, has_side_effects=True, vmem_limit_bytes=VMEM_LIMIT
        ),
        name="terms",
    )(small, block_low, grad_reduced, act_two, grad_expanded, modulated, grad_middle, change, grad_gate)


class Gather:
    def __init__(self, dims, reps, shards, fulls, buffers):
        self.dims, self.reps, self.shards, self.fulls = dims, reps, shards, fulls
        self.own_sem, self.a_sem, self.b_sem, self.c_sem, self.r_sem = buffers
        self.place = Place(dims, reps)
        self.waits, self.local = [], []

    def slot(self, k, index, which):
        full = self.fulls[k]
        return full.at[index, :, columns(full.shape[-1] // self.reps, which)]

    def push(self, k, da, du, dv, target, target_rep, sems):
        index, rep = self.place.at(-da, -du, -dv), self.place.rep
        if (da, du, dv) == (0, 0, 0):
            source = self.shards[k].at[:, columns(self.shards[k].shape[-1] // self.reps, rep)]
        else:
            source = self.slot(k, index, rep)
        copy = remote(source, self.slot(k, index, rep), sems, target, target_rep)
        copy.start()
        self.waits.append(copy)

    def landed(self, k, da, du, dv, which, sems):
        there = self.slot(k, self.place.at(-da, -du, -dv), which)
        remote(there, there, sems, self.place.me, self.place.rep).wait_recv()

    def forward(self, k, da, du, dv):
        size_a, size_b, size_c = self.dims
        place, rep = self.place, self.place.rep
        if dv == 0 and du == 0:
            for d in range(1, size_b):
                self.push(k, da, 0, 0, place.at(0, d, 0), rep, self.b_sem.at[k, da, d - 1])
        if dv == 0:
            for d in range(1, size_c):
                self.push(k, da, du, 0, place.at(0, 0, d), rep, self.c_sem.at[k, da, du, d - 1])
        if (da, du, dv) != (0, 0, 0):
            for d in range(1, self.reps):
                self.push(k, da, du, dv, place.me, (rep + d) % self.reps, self.r_sem.at[k, da, du, dv, d - 1])

    def begin(self, k):
        place = self.place
        copy = pltpu.make_async_copy(self.shards[k], self.fulls[k].at[place.me], self.own_sem.at[k])
        copy.start()
        self.local.append(copy)
        for d in range(1, self.dims[0]):
            self.push(k, 0, 0, 0, place.at(d, 0, 0), place.rep, self.a_sem.at[k, d - 1])
        self.forward(k, 0, 0, 0)

    def hop(self, k, lag):
        size_a, size_b, size_c = self.dims
        place, reps, rep = self.place, self.reps, self.place.rep
        if lag == 0:
            for da in range(1, size_a):
                self.landed(k, da, 0, 0, rep, self.a_sem.at[k, da - 1])
                self.forward(k, da, 0, 0)
        elif lag == 1:
            for du in range(1, size_b):
                for da in range(size_a):
                    self.landed(k, da, du, 0, rep, self.b_sem.at[k, da, du - 1])
                    self.forward(k, da, du, 0)
        elif lag == 2:
            for dv in range(1, size_c):
                for du in range(size_b):
                    for da in range(size_a):
                        self.landed(k, da, du, dv, rep, self.c_sem.at[k, da, du, dv - 1])
                        self.forward(k, da, du, dv)
        else:
            for dv in range(size_c):
                for du in range(size_b):
                    for da in range(size_a):
                        if (da, du, dv) != (0, 0, 0):
                            for d in range(1, reps):
                                self.landed(k, da, du, dv, (rep + reps - d) % reps, self.r_sem.at[k, da, du, dv, d - 1])
            self.local[k].wait()

    def finish(self):
        for copy in self.waits:
            copy.wait_send()


def gather_buffers(dims, reps, count):
    size_a, size_b, size_c = dims
    return [
        DMA((count,)),
        DMA((count, max(size_a - 1, 1), 2)),
        DMA((count, size_a, max(size_b - 1, 1), 2)),
        DMA((count, size_a, size_b, max(size_c - 1, 1), 2)),
        DMA((count, size_a, size_b, size_c, max(reps - 1, 1), 2)),
    ]


def head_kernel(dims, reps, sizes, stem_rows, *refs):
    stem_own, reduce_own, diff_own, mid_own, expand_own = refs[:5]
    lateral_own, wide_own, narrow_own, least_own, lhs, valid, pair, count, features = refs[5:14]
    (lateral_out, vector_out, reduce_out, diff_out, mid_out, expand_out, block_in, block_low, stem_normed, pool_low, stem_inverse,
     number_out, normed_one, inverse_one, act_one, change) = refs[14:30]
    (small_own, small, stem_taps, reduce_full, tap_rows, lateral, stem_values, stem_act, loaded, wide, low, reduced) = refs[30:42]
    load_sem, wide_sem, low_sem, out_sem = refs[42:46]
    gather = Gather(
        dims, reps, [small_own, stem_own, reduce_own, diff_own.at[0], diff_own.at[1], mid_own, expand_own],
        [small, stem_taps, reduce_full, diff_out.at[0], diff_out.at[1], mid_out, expand_out], refs[46:51],
    )
    over = Exchange(sizes, reps, refs[51:])
    fsdp = small.shape[0]
    me = gather.place.me
    stem_width = stem_rows * fsdp
    lines, rows, mid_width = reduced.shape
    clips, pixels, segs, width = features.shape
    slots = valid.shape[0]
    groups = rows // slots
    step = 256
    chunks = width // step
    mask = valid[:, :1].reshape(1, slots, 1)
    pairs = pair[:, :1].reshape(1, slots, 1)
    own = count[:, :1]

    def load(j):
        cols = slice(j * step, (j + 1) * step)
        return [
            pltpu.make_async_copy(
                features.at[clip, :, :, cols], loaded.at[j % 2, :, clip * segs : (clip + 1) * segs, :], load_sem.at[j % 2, clip]
            )
            for clip in range(clips)
        ]

    def grouped(values):
        return values.reshape(groups, slots, values.shape[-1])

    def moments(carry, origin):
        away, squares = whole_row(carry[0]), whole_row(carry[1])
        return [away + own * origin, jnp.maximum(squares - away * away / own, 0.0), count[...]]

    def add_moments(carry, values, origin):
        off = (grouped(values) - origin.reshape(1, 1, -1)) * mask
        return carry[0] + fold_rows(off), carry[1] + fold_rows(off * off)

    def blank(n):
        return jnp.zeros((8, n), f32), jnp.zeros((8, n), f32)

    for copy in load(0):
        copy.start()

    def placed(values, length):
        share = values.shape[1]
        one = lax.broadcasted_iota(jnp.int32, (share, length), 1) - me * share
        hot = (one == lax.broadcasted_iota(jnp.int32, (share, length), 0)).astype(f32).astype(bf16)
        return dot(values, hot)

    least = placed(least_own[...], LANES * -(-stem_width // LANES))
    narrow = placed(narrow_own[...], mid_width)
    pieces = [narrow[n : n + 1] for n in range(narrow.shape[0])] + [least[n : n + 1] for n in range(least.shape[0])]
    joined = jnp.concatenate(pieces, axis=1)
    joined = jnp.concatenate([joined, jnp.zeros((1, -joined.shape[1] % width), f32)], axis=1)
    small_rows = [lateral_own[...].astype(f32), placed(wide_own[...], width)]
    small_rows += [joined[:, n * width : (n + 1) * width] for n in range(joined.shape[1] // width)]
    taken = sum(row.shape[0] for row in small_rows)
    small_rows.append(jnp.zeros((small_own.shape[0] - taken, width), f32))
    small_own[...] = jnp.concatenate(small_rows, axis=0).astype(bf16)
    gather.place.greet(over.peers)
    for k in range(3):
        gather.begin(k)
    stem_act[...] = jnp.zeros(stem_act.shape, f32)
    for lag in range(3):
        gather.hop(0, lag)
        gather.hop(1, lag)
    for k in range(3, 7):
        gather.begin(k)
    gather.hop(0, 3)
    gather.hop(1, 3)
    vectors = jnp.zeros((taken - stem_rows, width), f32)
    for device in range(fsdp):
        values = small[device].astype(f32)
        span = slice(device * stem_rows, (device + 1) * stem_rows)
        lateral[span, :] = values[:stem_rows]
        vectors = vectors + values[stem_rows:taken]
        taps = stem_taps[device].astype(f32)
        for x in range(GRID):
            tap_rows[x, span, :] = taps[x * stem_rows : (x + 1) * stem_rows]
    lateral_low = lateral[...].astype(bf16)
    vector_out[...] = vectors
    lateral_out[...] = lateral_low

    def vector(position, length):
        row, start = 2 + position // width, position % width
        return vectors[row : row + 1, start : start + length]

    gain_one, shift_one = vector(0, mid_width), vector(mid_width, mid_width)
    start = mid_width * narrow.shape[0]
    stem_gain, stem_shift = vector(start, stem_width), vector(start + least.shape[1], stem_width)
    gather.hop(2, 0)

    def stem_column(x, _):
        stem_values[x] = dot_t(lhs[...], tap_rows[x].astype(bf16))
        return 0

    lax.fori_loop(0, GRID, stem_column, 0)
    origin = stem_values[0, 0:1, :]
    carry = lax.fori_loop(0, GRID, lambda x, c: add_moments(c, stem_values[x], origin), blank(stem_width))
    gather.hop(3, 0)
    gather.hop(2, 1)
    total, squares, number = over.total(0, moments(carry, origin), True)
    number_out[...] = number
    number = number[:, :1]
    centre, inverse = total / number, lax.rsqrt(squares / number + epsilon)
    stem_inverse[...] = inverse
    gather.hop(2, 2)

    def stem_norm(x, _):
        normed = (stem_values[x] - centre) * inverse
        stem_normed[:, x] = grouped(normed)
        zeta = mask * (grouped(normed) * stem_gain.reshape(1, 1, -1) + stem_shift.reshape(1, 1, -1))
        stem_act[x + 1, 1 : GRID + 1] = gelu_parts(zeta)[0]
        return 0

    lax.fori_loop(0, GRID, stem_norm, 0)

    def stem_pool(x, _):
        total = stem_act[x] + stem_act[x + 1] + stem_act[x + 2]
        total = total[0:GRID] + total[1 : GRID + 1] + total[2 : GRID + 2]
        pool_low[:, x] = (total / 9.0).astype(bf16)
        return 0

    lax.fori_loop(0, GRID, stem_pool, 0)
    gather.hop(4, 0)
    gather.hop(3, 1)
    gather.hop(2, 3)

    later = [(5, 0), (4, 1), (3, 2), (6, 0), (5, 1), (4, 2)]
    for j in range(chunks):
        slot = j % 2
        cols = slice(j * step, (j + 1) * step)
        for copy in load(j + 1) if j + 1 < chunks else ():
            copy.start()
        for copy in load(j):
            copy.wait()
        out_wide = pltpu.make_async_copy(wide.at[slot], block_in.at[:, :, cols], wide_sem.at[slot])
        out_low = pltpu.make_async_copy(low.at[slot], block_low.at[:, :, cols], low_sem.at[slot])

        if j >= 2:
            out_wide.wait()
            out_low.wait()
        shares = step // reduce_full.shape[1]
        weight = reduce_full[j * shares : (j + 1) * shares].reshape(step, mid_width)

        def line(y, _):
            values = loaded[slot, pl.ds(y * groups, groups)].astype(f32).reshape(rows, step)
            values = values + dot(pool_low[y].reshape(rows, stem_width), lateral_low[:, cols])
            wide[slot, y] = values
            rounded = values.astype(bf16)
            low[slot, y] = rounded
            product = dot(rounded, weight)
            reduced[y] = product if j == 0 else reduced[y] + product
            return 0

        lax.fori_loop(0, lines, line, 0)
        out_wide.start()
        out_low.start()
        if j < len(later):
            gather.hop(*later[j])
    pltpu.make_async_copy(reduce_full, reduce_out, out_sem).start()

    origin = reduced[0, 0:1, :]
    carry = lax.fori_loop(0, lines, lambda y, c: add_moments(c, reduced[y], origin), blank(mid_width))
    total, squares, _ = over.total(1, moments(carry, origin), True)
    centre, inverse = total / number, lax.rsqrt(squares / number + epsilon)
    inverse_one[...] = inverse
    gather.hop(6, 1)
    gather.hop(5, 2)

    def first(y, _):
        normed = (reduced[y] - centre) * inverse
        normed_one[y] = normed
        zeta = mask * (grouped(normed) * gain_one.reshape(1, 1, -1) + shift_one.reshape(1, 1, -1))
        act = gelu_parts(zeta)[0].reshape(rows, mid_width)
        act_one[y] = act
        change[y] = (pairs * grouped(pltpu.roll(act, rows - 1, 0) - act)).astype(bf16).reshape(rows, mid_width)
        return 0

    lax.fori_loop(0, lines, first, 0)
    gather.hop(6, 2)
    for k in range(3, 7):
        gather.hop(k, 3)
    for j in (chunks - 2, chunks - 1):
        cols = slice(j * step, (j + 1) * step)
        pltpu.make_async_copy(wide.at[j % 2], block_in.at[:, :, cols], wide_sem.at[j % 2]).wait()
        pltpu.make_async_copy(low.at[j % 2], block_low.at[:, :, cols], low_sem.at[j % 2]).wait()
    pltpu.make_async_copy(reduce_full, reduce_out, out_sem).wait()
    gather.finish()
    over.finish()


def head(stem_taps, reduce_weight, diff_weight, mid_weight, expand_weight, lateral, wide, narrow, least, lhs, valid, pair, count, features, fsdp, reps, collective_id):
    dims, sizes = factor_three(fsdp), stage_sizes(fsdp * reps)
    shape = jax.ShapeDtypeStruct
    clips, pixels, segs, width = features.shape
    slots = clips * segs
    mid_width = reduce_weight.shape[1]
    stem_rows = lateral.shape[0]
    stem_width = stem_rows * fsdp
    rows = GRID * slots
    step = 256
    side = GRID + 2
    lengths = narrow.shape[0] * mid_width + least.shape[0] * (-(-stem_width // LANES) * LANES)
    vectors = 2 + -(-lengths // width)
    small = shape((-(-(stem_rows + vectors) // 16) * 16, width), bf16)

    def full(shard):
        return shape(shard.shape[:-2] + (fsdp,) + shard.shape[-2:], shard.dtype)

    def whole(shard):
        return pltpu.VMEM((fsdp,) + shard.shape, shard.dtype)

    return pl.pallas_call(
        functools.partial(head_kernel, dims, reps, sizes, stem_rows),
        out_shape=[
            shape((stem_width, width), bf16), shape((vectors, width), f32),
            full(reduce_weight), full(diff_weight), full(mid_weight), full(expand_weight),
            shape((GRID, rows, width), f32), shape((GRID, rows, width), bf16),
            shape((GRID, GRID, slots, stem_width), f32), shape((GRID, GRID, slots, stem_width), bf16),
            shape((1, stem_width), f32), shape((1, LANES), f32),
            shape((GRID, rows, mid_width), f32), shape((1, mid_width), f32), shape((GRID, rows, mid_width), f32),
            shape((GRID, rows, mid_width), bf16),
        ],
        in_specs=[ANY] * 5 + [IN_VMEM] * 8 + [ANY],
        out_specs=[IN_VMEM] * 2 + [ANY] * 6 + [IN_VMEM] * 8,
        scratch_shapes=[
            pltpu.VMEM(small.shape, bf16), whole(small), whole(stem_taps), whole(reduce_weight),
            pltpu.VMEM((GRID, stem_width, stem_taps.shape[1]), f32), pltpu.VMEM((stem_width, width), f32),
            pltpu.VMEM((GRID, rows, stem_width), f32), pltpu.VMEM((side, side, slots, stem_width), f32),
            pltpu.VMEM((2, pixels, slots, step), bf16),
            pltpu.VMEM((2, GRID, rows, step), f32), pltpu.VMEM((2, GRID, rows, step), bf16),
            pltpu.VMEM((GRID, rows, mid_width), f32),
            DMA((2, clips)), DMA((2,)), DMA((2,)), DMA(()),
        ] + gather_buffers(dims, reps, 7) + exchange_buffers(sizes, 2, 2 * mid_width + LANES),
        compiler_params=pltpu.CompilerParams(
            collective_id=collective_id, has_side_effects=True, vmem_limit_bytes=VMEM_LIMIT
        ),
        name="head",
    )(stem_taps, reduce_weight, diff_weight, mid_weight, expand_weight, lateral, wide, narrow, least, lhs, valid, pair, count, features)


def tail_kernel(sizes, reps, clip_count, *refs):
    (middle, expand, valid, spread, count, gain_two, shift_two, gain_three, shift_three, pooled_grad, block_in) = refs[:11]
    (pooled, grad_pre, grad_expanded, act_two, grad_middle, gain_three_sum, shift_three_sum, gain_two_sum, shift_two_sum) = refs[11:20]
    (wide, wide_grad, narrow, narrow_grad, block, low, totals, first, block_sem, pre_sem, low_sem) = refs[20:31]
    over = Exchange(sizes, reps, refs[31:])
    lines, rows, mid_width = middle.shape
    width = expand.shape[1]
    slots = valid.shape[0]
    segs = slots // clip_count
    groups = rows // slots
    step = 256
    chunks = width // step

    barrier = pltpu.get_barrier_semaphore()
    for target, rep in over.peers:
        pl.semaphore_signal(barrier, inc=1, device_id={"fsdp": target, "rep": rep}, device_id_type=MESH)

    def fetch(y, slot):
        return pltpu.make_async_copy(block_in.at[y], block.at[slot], block_sem.at[slot])

    fetch(0, 0).start()
    mask = valid[:, :1].reshape(1, slots, 1)
    own = count[:, :1]

    def grouped(values):
        return values.reshape(groups, slots, values.shape[-1])

    def moments(carry, origin):
        away, squares = whole_row(carry[0]), whole_row(carry[1])
        return away + own * origin, jnp.maximum(squares - away * away / own, 0.0)

    def gather_moments(carry, values, origin):
        off = (grouped(values) - origin.reshape(1, 1, -1)) * mask
        return carry[0] + fold_rows(off), carry[1] + fold_rows(off * off)

    def blank(n):
        return jnp.zeros((8, n), f32), jnp.zeros((8, n), f32)

    origin = middle[0, 0:1, :]
    carry = lax.fori_loop(0, lines, lambda y, c: gather_moments(c, middle[y], origin), blank(mid_width))
    pl.semaphore_wait(barrier, len(over.peers))
    total, squares, number = over.total(0, list(moments(carry, origin)) + [count[...]], True)
    number = number[:, :1]
    centre_two, inverse_two = total / number, lax.rsqrt(squares / number + epsilon)
    gain2, shift2 = gain_two[...], shift_two[...]

    def zeta_two(normed):
        return mask * (grouped(normed) * gain2.reshape(1, 1, -1) + shift2.reshape(1, 1, -1))

    def forward_two(y, _):
        normed = (middle[y] - centre_two) * inverse_two
        narrow[y] = normed
        act_two[y] = gelu_parts(zeta_two(normed))[0].astype(bf16).reshape(rows, mid_width)
        return 0

    lax.fori_loop(0, lines, forward_two, 0)

    def expand_chunk(j, _):
        cols = pl.ds(pl.multiple_of(j * step, step), step)
        weight = expand[:, cols]
        origin = dot(act_two[0, 0:16, :], weight)[0:1]

        def line(y, carry):
            values = dot(act_two[y], weight)
            wide[y, :, cols] = values
            return gather_moments(carry, values, origin)

        total, squares = moments(lax.fori_loop(0, lines, line, blank(step)), origin)
        totals[0, :, cols] = total
        totals[1, :, cols] = squares
        return 0

    lax.fori_loop(0, chunks, expand_chunk, 0)
    total, squares, _ = over.total(1, [totals[0], totals[1], count[...]], True)
    totals[0] = total / number
    totals[1] = lax.rsqrt(squares / number + epsilon)
    for index in range(2):
        first[index] = jnp.zeros((8, width), f32)

    def out_pre(y):
        return pltpu.make_async_copy(wide_grad.at[y], grad_pre.at[y], pre_sem.at[y])

    def forward_three(y, _):
        slot = y % 2
        fetch(y, slot).wait()

        @pl.when(y + 1 < lines)
        def _():
            fetch(y + 1, 1 - slot).start()

        def chunk(j, _):
            cols = pl.ds(pl.multiple_of(j * step, step), step)
            normed = (wide[y, :, cols] - totals[0, :, cols]) * totals[1, :, cols]
            wide[y, :, cols] = normed
            normed = grouped(normed)
            scaled = mask * (gain_three[:, cols].reshape(1, 1, step) * normed + shift_three[:, cols].reshape(1, 1, step))
            out, slope = gelu_parts(grouped(block[slot, :, cols]) + scaled)
            grads = []
            for clip in range(clip_count):
                span = slice(clip * segs, (clip + 1) * segs)
                share = spread[span, :1].reshape(1, segs, 1)
                pixels = pl.ds(y * groups, groups)
                pooled[clip, pixels, :, cols] = jnp.sum(out[:, span] * share, axis=1, keepdims=True)
                grads.append(slope[:, span] * (pooled_grad[clip, pixels, :, cols] * share))
            grad = jnp.concatenate(grads, axis=1)
            wide_grad[y, :, cols] = grad.reshape(rows, step)
            first[0, :, cols] += fold_rows(grad)
            first[1, :, cols] += fold_rows(grad * normed)
            return 0

        lax.fori_loop(0, chunks, chunk, 0)
        out_pre(y).start()
        return 0

    lax.fori_loop(0, lines, forward_three, 0)
    shift_sum, gain_sum = over.total(2, [whole_row(first[0]), whole_row(first[1])], False)
    shift_three_sum[...] = shift_sum
    gain_three_sum[...] = gain_sum
    totals[2] = shift_sum / number
    totals[3] = gain_sum / number
    totals[1] = totals[1] * gain_three[...]

    def out_low(y):
        return pltpu.make_async_copy(low.at[y % 2], grad_expanded.at[y], low_sem.at[y % 2])

    def back_three(y, carry):
        slot = y % 2

        @pl.when(y >= 2)
        def _():
            out_low(y - 2).wait()

        def chunk(j, _):
            cols = pl.ds(pl.multiple_of(j * step, step), step)
            grad = wide_grad[y, :, cols] - totals[2, :, cols] - wide[y, :, cols] * totals[3, :, cols]
            low[slot, :, cols] = (mask * grouped(grad * totals[1, :, cols])).astype(bf16).reshape(rows, step)
            return 0

        lax.fori_loop(0, chunks, chunk, 0)
        out_low(y).start()
        normed = narrow[y]
        grad = grouped(dot_t(low[slot], expand[...])) * gelu_parts(zeta_two(normed))[1] * mask
        narrow_grad[y] = grad.reshape(rows, mid_width)
        return carry[0] + fold_rows(grad), carry[1] + fold_rows(grad * grouped(normed))

    carry = lax.fori_loop(0, lines, back_three, blank(mid_width))
    shift_sum, gain_sum = over.total(3, [whole_row(carry[0]), whole_row(carry[1])], False)
    shift_two_sum[...] = shift_sum
    gain_two_sum[...] = gain_sum
    shift_mean, gain_mean, scale = shift_sum / number, gain_sum / number, inverse_two * gain2

    def back_two(y, _):
        grad = (narrow_grad[y] - shift_mean - narrow[y] * gain_mean) * scale
        grad_middle[y] = (mask * grouped(grad)).astype(bf16).reshape(rows, mid_width)
        return 0

    lax.fori_loop(0, lines, back_two, 0)
    lax.fori_loop(0, lines, lambda y, _: (out_pre(y).wait(), 0)[1], 0)
    for y in (lines - 2, lines - 1):
        out_low(y).wait()
    over.finish()


def tail(middle, expand, valid, spread, count, gain_two, shift_two, gain_three, shift_three, pooled_grad, block_in, clip_count, fsdp, reps, collective_id):
    sizes = stage_sizes(fsdp * reps)
    lines, rows, mid_width = middle.shape
    width = expand.shape[1]
    pixels = pooled_grad.shape[1]
    shape = jax.ShapeDtypeStruct
    return pl.pallas_call(
        functools.partial(tail_kernel, sizes, reps, clip_count),
        out_shape=[
            shape((clip_count, pixels, 1, width), f32), shape((lines, rows, width), f32), shape((lines, rows, width), bf16),
            shape((lines, rows, mid_width), bf16), shape((lines, rows, mid_width), bf16),
            shape((1, width), f32), shape((1, width), f32), shape((1, mid_width), f32), shape((1, mid_width), f32),
        ],
        in_specs=[IN_VMEM] * 10 + [ANY],
        out_specs=[IN_VMEM, ANY, ANY] + [IN_VMEM] * 6,
        scratch_shapes=[
            pltpu.VMEM((lines, rows, width), f32), pltpu.VMEM((lines, rows, width), f32),
            pltpu.VMEM((lines, rows, mid_width), f32), pltpu.VMEM((lines, rows, mid_width), f32),
            pltpu.VMEM((2, rows, width), f32), pltpu.VMEM((2, rows, width), bf16),
            pltpu.VMEM((4, 1, width), f32), pltpu.VMEM((2, 8, width), f32),
            DMA((2,)), DMA((lines,)), DMA((2,)),
        ] + exchange_buffers(sizes, 4, 2 * width + LANES),
        compiler_params=pltpu.CompilerParams(collective_id=collective_id, has_side_effects=True, vmem_limit_bytes=VMEM_LIMIT),
        name="tail",
    )(middle, expand, valid, spread, count, gain_two, shift_two, gain_three, shift_three, pooled_grad, block_in)


ORDER = ("HWNC", "HWIO", "HWNC")


def pad_of(span):
    return ((span, span), (span, span))


def convolve(source, weight, span, stride):
    side = 2 * span + 1
    kernel = weight.reshape(side, side, source.shape[-1], -1)
    return lax.conv_general_dilated(
        source, kernel, (1, 1), pad_of(span * stride), rhs_dilation=(stride, stride),
        dimension_numbers=ORDER, preferred_element_type=f32,
    )


def convolve_back(grads, weight, span, stride):
    side = 2 * span + 1
    kernel = weight.reshape(side, side, -1, grads.shape[-1])[::-1, ::-1]
    return lax.conv_general_dilated(
        grads, kernel, (1, 1), pad_of(span * stride), rhs_dilation=(stride, stride),
        dimension_numbers=("HWNC", "HWOI", "HWNC"), preferred_element_type=f32,
    )


def convolve_terms(source, grads, span, stride, kind):
    return lax.conv_general_dilated(
        source, grads, (stride, stride), pad_of(span * stride),
        dimension_numbers=("HWCN", "HWIO", "HWNC"), preferred_element_type=kind,
    )


def pool_mean(source):
    total = lax.reduce_window(source, 0.0, lax.add, (3, 3, 1, 1), (1, 1, 1, 1), "SAME")
    return total / 9.0


def project(source, weight):
    return jnp.einsum("yxnc,cd->yxnd", source, weight, preferred_element_type=f32)


def project_back(grads, weight):
    return jnp.einsum("yxnd,cd->yxnc", grads, weight, preferred_element_type=f32)


def project_terms(source, grads, kind):
    return jnp.einsum("yxnc,yxnd->cd", source, grads, preferred_element_type=kind)


def gelu_back(pre_act, grads):
    return jax.vjp(jax.nn.gelu, pre_act)[1](grads)[0]


def make_shards(fsdp, reps):
    def shards(
        frames, features, seg_counts, stem_weight, stem_gain, stem_shift, lateral, reduce_weight,
        gain_one, shift_one, diff_weight, gate_shift, mid_weight, gain_two, shift_two,
        expand_weight, gain_three, shift_three, pooled_grad,
    ):
        clip_count, seg_slots, pixels, feature_width = features.shape
        slots = clip_count * seg_slots
        mid_width = reduce_weight.shape[1]
        stem_rows, stem_depth = stem_weight.shape
        stem_width = stem_rows * fsdp

        seg_index = lax.broadcasted_iota(jnp.int32, (clip_count, seg_slots), 1)
        valid_seg = (seg_index < seg_counts[:, None]).astype(f32)
        pair_seg = valid_seg * jnp.concatenate(
            [valid_seg[:, 1:], jnp.zeros((clip_count, 1), f32)], axis=1
        )
        valid = valid_seg.reshape(1, 1, slots, 1)
        pair = pair_seg.reshape(1, 1, slots, 1)
        count_float = seg_counts.astype(f32)
        local_count = jnp.sum(count_float) * pixels

        taps = jnp.pad(stem_weight.reshape(stem_rows, GRID, GRID, -1), ((0, 0), (0, 0), (3, 3), (0, 0)))
        taps = jnp.stack([taps[:, :, 6 - x : 13 - x] for x in range(GRID)]).reshape(GRID * stem_rows, stem_depth)
        taps = jnp.pad(taps, ((0, -taps.shape[0] % 16), (0, -stem_depth % (LANES * reps))))
        moving = frames.astype(f32)
        motion = (moving[:, :, 1:] - moving[:, :, :-1]) * valid_seg[:, :, None, None, None]
        motion = jnp.transpose(motion.astype(bf16), (4, 0, 1, 2, 3)).reshape(GRID, GRID, slots, -1)
        strips = jnp.transpose(motion, (0, 2, 1, 3)).reshape(GRID, slots, -1)
        strips = jnp.pad(strips, ((3, 3), (0, 0), (0, 0)))
        strips = jnp.concatenate([strips[dy : dy + GRID] for dy in range(GRID)], axis=-1).reshape(GRID * slots, -1)
        strips = jnp.pad(strips, ((0, 0), (0, -stem_depth % (LANES * reps))))
        lanes = lambda column: jnp.broadcast_to(column.reshape(-1, 1), (column.size, LANES))
        (lateral_full, vectors, reduce_full, diff_full, mid_full, expand_full, block_in, block_low, stem_normed, pool_low,
         stem_inverse, number, normed_one, inverse_one, act_one, change) = head(
            taps, reduce_weight, diff_weight, mid_weight, expand_weight, lateral, jnp.stack([gain_three, shift_three]),
            jnp.stack([gain_one, shift_one, gate_shift, gain_two, shift_two]), jnp.stack([stem_gain, stem_shift]),
            strips, lanes(valid_seg), lanes(pair_seg), lanes(local_count), jnp.transpose(features, (0, 2, 1, 3)),
            fsdp, reps, 1,
        )
        row = vectors[2:].reshape(-1)
        gain_one_full, shift_one_full, gate_full, gain_two_full, shift_two_full = (
            row[n * mid_width : (n + 1) * mid_width] for n in range(5)
        )
        gain_three_full, shift_three_full = vectors[0], vectors[1]
        start = 5 * mid_width
        stem_gain_full = row[start : start + stem_width]
        start += -(-stem_width // LANES) * LANES
        stem_shift_full = row[start : start + stem_width]
        reduce_full = reduce_full.reshape(-1, mid_width)
        diff_full = diff_full.reshape(2, -1, mid_width)
        mid_full = mid_full.reshape(-1, mid_width)
        expand_full = expand_full.reshape(mid_width, -1)
        cube = (GRID, GRID, slots, -1)
        flat = (GRID, GRID * slots, -1)
        normed_one, act_one, change = normed_one.reshape(cube), act_one.reshape(cube), change.reshape(cube)
        stats_one = (None, inverse_one[0], number[0, 0])
        stem_stats = (None, stem_inverse[0], number[0, 0])
        zeta_one = valid * (gain_one_full * normed_one + shift_one_full)
        stem_norm = valid * (stem_gain_full * stem_normed + stem_shift_full)

        def norm_back(grad_out, normed, stats, gain, collective_id, name):
            masked = grad_out * valid
            shift_sum, gain_sum = exchange(
                [jnp.sum(masked, axis=(0, 1, 2)), jnp.sum(masked * normed, axis=(0, 1, 2))],
                fsdp, reps, False, collective_id, name,
            )
            grad_in = valid * stats[1] * gain * (masked - shift_sum / stats[2] - normed * gain_sum / stats[2])
            return grad_in.astype(bf16), gain_sum, shift_sum

        def earlier_of(values):
            grid = values.reshape(GRID, GRID, clip_count, seg_slots, -1)
            return jnp.pad(grid[:, :, :, :-1], ((0, 0), (0, 0), (0, 0), (1, 0), (0, 0))).reshape(values.shape)

        gate_pre = convolve(change, diff_full[0], 1, 1) + convolve(change, diff_full[1], 1, 2)
        gate = jax.nn.sigmoid(gate_pre + gate_full)
        modulated = (act_one * (1.0 + gate)).astype(bf16)
        middle = convolve(modulated, mid_full, 1, 1)
        (pooled, grad_pre, grad_expanded, act_two, grad_middle, gain_three_sum, shift_three_sum, gain_two_sum,
         shift_two_sum) = tail(
            middle.reshape(flat), expand_full, lanes(valid_seg), lanes(valid_seg / count_float[:, None]), lanes(local_count),
            gain_two_full[None], shift_two_full[None], gain_three_full[None], shift_three_full[None],
            pooled_grad.astype(f32)[:, :, None], block_in, clip_count, fsdp, reps, 4,
        )
        pooled = pooled.reshape(pooled_grad.shape).astype(bf16)
        gain_three_sum, shift_three_sum, gain_two_sum, shift_two_sum = (
            row[0] for row in (gain_three_sum, shift_three_sum, gain_two_sum, shift_two_sum)
        )
        grad_pre, grad_expanded, act_two, grad_middle = (
            block.reshape(cube) for block in (grad_pre, grad_expanded, act_two, grad_middle)
        )
        grad_modulated = convolve_back(grad_middle, mid_full, 1, 1)
        grad_gate_pre = grad_modulated * act_one * gate * (1.0 - gate)
        gate_terms = jnp.sum(grad_gate_pre, axis=(0, 1, 2))
        grad_gate = grad_gate_pre.astype(bf16)
        grad_change = convolve_back(grad_gate, diff_full[0], 1, 1) + convolve_back(grad_gate, diff_full[1], 1, 2)
        grad_change = grad_change * pair
        grad_act_one = grad_modulated * (1.0 + gate) + earlier_of(grad_change) - grad_change
        grad_reduced, gain_one_sum, shift_one_sum = norm_back(
            gelu_back(zeta_one, grad_act_one), normed_one, stats_one, gain_one_full, 8, "sums_one"
        )
        features_grad = grad_pre + project_back(grad_reduced, reduce_full)
        grad_lateral = features_grad.astype(bf16)
        lateral_terms = project_terms(pool_low, grad_lateral, bf16)
        grad_act = pool_mean(project_back(grad_lateral, lateral_full))
        grad_stem, stem_gain_sum, stem_shift_sum = norm_back(
            gelu_back(stem_norm, grad_act), stem_normed, stem_stats, stem_gain_full, 9, "sums_stem"
        )
        stem_terms = convolve_terms(motion, grad_stem, 3, 1, bf16)
        stem_terms = jnp.transpose(stem_terms, (3, 0, 1, 2)).reshape(fsdp, stem_rows, stem_depth)
        gate_rows = gate_shift.shape[0]
        small_terms = jnp.concatenate(
            [
                lateral_terms.reshape(fsdp, stem_rows, feature_width),
                jnp.pad(stem_terms, ((0, 0), (0, 0), (0, feature_width - stem_depth))),
                jnp.pad(
                    gate_terms.astype(bf16).reshape(fsdp, 1, gate_rows),
                    ((0, 0), (0, 15 - 2 * stem_rows), (0, feature_width - gate_rows)),
                ),
            ],
            axis=1,
        )

        conv_rows = mid_weight.shape[0]
        if conv_rows % 32 == 0:
            small_part, reduce_part, expand_part, mid_part, diff_one, diff_two = terms_all(
                small_terms.reshape(-1, feature_width), block_low, grad_reduced.reshape(flat),
                act_two.reshape(flat), grad_expanded.reshape(flat), modulated, grad_middle.reshape(flat), change,
                grad_gate.reshape(flat),
                [small_terms.shape[1], reduce_weight.shape[0], expand_weight.shape[0], conv_rows], fsdp, reps, 10,
            )
        else:
            def owned(terms, shard):
                return terms.reshape((fsdp,) + shard.shape[-2:])

            small_part, reduce_part, expand_part, mid_part, diff_one, diff_two = scatter_all(
                [
                    small_terms,
                    owned(project_terms(block_low.reshape(cube), grad_reduced, bf16), reduce_weight),
                    owned(project_terms(act_two, grad_expanded, bf16), expand_weight),
                    owned(convolve_terms(modulated, grad_middle, 1, 1, bf16), mid_weight),
                    owned(convolve_terms(change, grad_gate, 1, 1, bf16), diff_weight),
                    owned(convolve_terms(change, grad_gate, 1, 2, bf16), diff_weight),
                ],
                fsdp, reps, 11, "scatter_terms",
            )

        def own_share(whole):
            share = whole.shape[0] // fsdp
            return lax.dynamic_slice_in_dim(whole, lax.axis_index("fsdp") * share, share)

        out = jnp.transpose(features_grad, (2, 0, 1, 3)).reshape(features.shape)
        return (
            pooled,
            out,
            small_part[stem_rows : 2 * stem_rows, :stem_depth],
            own_share(stem_gain_sum),
            own_share(stem_shift_sum),
            small_part[:stem_rows],
            reduce_part,
            own_share(gain_one_sum),
            own_share(shift_one_sum),
            jnp.stack([diff_one, diff_two]),
            small_part[2 * stem_rows, :gate_rows],
            mid_part,
            own_share(gain_two_sum),
            own_share(shift_two_sum),
            expand_part,
            own_share(gain_three_sum),
            own_share(shift_three_sum),
        )

    return shards


def solution(mesh):
    whole = ("fsdp", "rep")
    matrix, vector = P("fsdp", None), P("fsdp")
    in_specs = (
        P(whole, None, None, None, None), P(whole, None, None, None), P(whole),
        matrix, vector, vector, matrix, matrix, vector, vector, P(None, "fsdp", None), vector,
        matrix, vector, vector, matrix, vector, vector, P(whole, None, None),
    )
    out_specs = (
        P(whole, None, None), P(whole, None, None, None), matrix, vector, vector, matrix, matrix,
        vector, vector, P(None, "fsdp", None), vector, matrix, vector, vector, matrix, vector, vector,
    )
    body = make_shards(mesh.shape["fsdp"], mesh.shape["rep"])
    return jax.shard_map(body, mesh=mesh, in_specs=in_specs, out_specs=out_specs, check_vma=False)
```

```python
import functools

import jax
import jax.numpy as jnp
from jax import lax
from jax.experimental import pallas as pl
from jax.experimental.pallas import tpu as pltpu
from jax.sharding import PartitionSpec as P

GRID = 7
LANES = 128
PIXELS = GRID * GRID
epsilon = 1e-05
MESH = pl.DeviceIdType.MESH
ANY = pl.BlockSpec(memory_space=pl.ANY)
IN_VMEM = pl.BlockSpec(memory_space=pltpu.VMEM)
VMEM_LIMIT = 60 * 1024 * 1024
bf16 = jnp.bfloat16
f32 = jnp.float32
DMA = pltpu.SemaphoreType.DMA


def factor_three(size):
    best = None
    for b in range(1, size + 1):
        for c in range(1, b + 1):
            if size % (b * c) == 0 and size // (b * c) >= b:
                a = size // (b * c)
                if best is None or a + b + c < sum(best):
                    best = (a, b, c)
    return best


class Place:
    def __init__(self, dims, reps, rep=None):
        self.dims, self.reps = dims, reps
        size_a, size_b, size_c = dims
        self.me = lax.axis_index("fsdp")
        self.rep = lax.axis_index("rep") if rep is None else rep
        ib, ic = (self.me // size_c) % size_b, self.me % size_c
        self.ia = self.me // (size_b * size_c)
        odd = self.rep % 2 if size_b == size_c else 0
        self.stride_u = size_c * (1 - odd) + odd
        self.stride_v = (1 - odd) + size_c * odd
        self.iu = ib * (1 - odd) + ic * odd
        self.iv = ic * (1 - odd) + ib * odd

    def at(self, da, du, dv):
        size_a, size_b, size_c = self.dims
        a = (self.ia + da + size_a) % size_a
        u = (self.iu + du + size_b) % size_b
        v = (self.iv + dv + size_c) % size_c
        return a * (size_b * size_c) + u * self.stride_u + v * self.stride_v

    def greet(self, more=()):
        size_a, size_b, size_c = self.dims
        peers = [(self.at(d, 0, 0), self.rep) for d in range(1, size_a)]
        peers += [(self.at(0, d, 0), self.rep) for d in range(1, size_b)]
        peers += [(self.at(0, 0, d), self.rep) for d in range(1, size_c)]
        peers += [(self.me, (self.rep + d) % self.reps) for d in range(1, self.reps)]
        greet(peers + list(more))


def greet(peers):
    barrier = pltpu.get_barrier_semaphore()
    for target, rep in peers:
        pl.semaphore_signal(
            barrier, inc=1, device_id={"fsdp": target, "rep": rep}, device_id_type=MESH
        )
    pl.semaphore_wait(barrier, len(peers))


def remote(src, dst, sems, target, rep):
    return pltpu.make_async_remote_copy(
        src_ref=src,
        dst_ref=dst,
        send_sem=sems.at[0],
        recv_sem=sems.at[1],
        device_id={"fsdp": target, "rep": rep},
        device_id_type=MESH,
    )


def columns(width, which):
    start = which * width
    return pl.ds(start if isinstance(start, int) else pl.multiple_of(start, width), width)


def views(refs):
    out = []
    for ref, stacked in refs:
        out += [ref.at[j] for j in range(ref.shape[0])] if stacked else [ref]
    return out


def scatter_kernel(dims, reps, stacked, *refs):
    number = len(stacked)
    partials = views(zip(refs[:number], stacked))
    totals = views(zip(refs[number : 2 * number], stacked))
    count = len(partials)
    rest = refs[2 * number :]
    held, from_rep, from_v, from_u, from_a, share = (rest[i * count : (i + 1) * count] for i in range(6))
    own_sem, r_sem, v_sem, u_sem, a_sem, s_sem = rest[6 * count :]
    size_a, size_b, size_c = dims
    place = Place(dims, reps)
    me, rep = place.me, place.rep
    place.greet()
    waits = []

    def push(source, there, sems, target, target_rep):
        copy = remote(source, there, sems, target, target_rep)
        copy.start()
        waits.append(copy)

    def landed(there, sems):
        remote(there, there, sems, me, rep).wait_recv()

    def order():
        for dv in list(range(1, size_c)) + [0]:
            for du in list(range(1, size_b)) + [0]:
                for da in list(range(1, size_a)) + [0]:
                    yield da, du, dv

    local = {}
    for k in range(count):
        width = partials[k].shape[-1] // reps
        for da, du, dv in order():
            for d in range(1, reps):
                other = (rep + d) % reps
                index = Place(dims, reps, other).at(da, du, dv)
                push(
                    partials[k].at[index, :, columns(width, other)],
                    from_rep[k].at[d - 1, index],
                    r_sem.at[k, da, du, dv, d - 1],
                    me,
                    other,
                )
            index = place.at(da, du, dv)
            copy = pltpu.make_async_copy(
                partials[k].at[index, :, columns(width, rep)],
                held[k].at[index],
                own_sem.at[k, da, du, dv],
            )
            copy.start()
            local[k, da, du, dv] = copy

    def handle(k, da, du, dv):
        index = place.at(da, du, dv)
        local[k, da, du, dv].wait()
        total = held[k][index].astype(f32)
        for d in range(1, reps):
            landed(from_rep[k].at[d - 1, index], r_sem.at[k, da, du, dv, d - 1])
            total = total + from_rep[k][d - 1, index].astype(f32)
        if dv == 0:
            for e in range(1, size_c):
                landed(from_v[k].at[e - 1, da, du], v_sem.at[k, da, du, e - 1])
                total = total + from_v[k][e - 1, da, du].astype(f32)
            if du == 0:
                for e in range(1, size_b):
                    landed(from_u[k].at[e - 1, da], u_sem.at[k, da, e - 1])
                    total = total + from_u[k][e - 1, da].astype(f32)
                if da == 0:
                    for e in range(1, size_a):
                        landed(from_a[k].at[e - 1], a_sem.at[k, e - 1])
                        total = total + from_a[k][e - 1].astype(f32)
        if (da, du, dv) == (0, 0, 0):
            share[k][rep] = total.astype(bf16)
            for d in range(1, reps):
                push(share[k].at[rep], share[k].at[rep], s_sem.at[k, d - 1], me, (rep + d) % reps)
            return
        held[k][index] = total.astype(bf16)
        if dv:
            push(held[k].at[index], from_v[k].at[dv - 1, da, du], v_sem.at[k, da, du, dv - 1], place.at(0, 0, dv), rep)
        elif du:
            push(held[k].at[index], from_u[k].at[du - 1, da], u_sem.at[k, da, du - 1], place.at(0, du, 0), rep)
        else:
            push(held[k].at[index], from_a[k].at[da - 1], a_sem.at[k, da - 1], place.at(da, 0, 0), rep)

    for step in range(count + 3):
        for lag in range(4):
            k = step - lag
            for da, du, dv in order() if 0 <= k < count else ():
                if lag == (0 if dv else 1 if du else 2 if da else 3):
                    handle(k, da, du, dv)
    for k in range(count):
        width = partials[k].shape[-1] // reps
        for d in range(1, reps):
            landed(share[k].at[(rep + reps - d) % reps], s_sem.at[k, d - 1])
        for which in range(reps):
            totals[k][:, which * width : (which + 1) * width] = share[k][which].astype(f32)
    for copy in waits:
        copy.wait_send()


def scatter_all(partials, fsdp, reps, collective_id, name):
    dims = factor_three(fsdp)
    size_a, size_b, size_c = dims
    stacked = [p.ndim == 4 for p in partials]
    shapes = []
    for p in partials:
        shapes += [(p.shape[-2], p.shape[-1] // reps)] * (p.shape[0] if p.ndim == 4 else 1)
    count = len(shapes)

    def buffers(*lead):
        return [pltpu.VMEM(lead + shape, bf16) for shape in shapes]

    return pl.pallas_call(
        functools.partial(scatter_kernel, dims, reps, stacked),
        out_shape=[
            jax.ShapeDtypeStruct(p.shape[:-3] + p.shape[-2:], f32) for p in partials
        ],
        in_specs=[ANY] * len(partials),
        out_specs=[IN_VMEM] * len(partials),
        scratch_shapes=buffers(fsdp)
        + buffers(max(reps - 1, 1), fsdp)
        + buffers(max(size_c - 1, 1), size_a, size_b)
        + buffers(max(size_b - 1, 1), size_a)
        + buffers(max(size_a - 1, 1))
        + buffers(reps)
        + [
            DMA((count, size_a, size_b, size_c)),
            DMA((count, size_a, size_b, size_c, max(reps - 1, 1), 2)),
            DMA((count, size_a, size_b, max(size_c - 1, 1), 2)),
            DMA((count, size_a, max(size_b - 1, 1), 2)),
            DMA((count, max(size_a - 1, 1), 2)),
            DMA((count, max(reps - 1, 1), 2)),
        ],
        compiler_params=pltpu.CompilerParams(
            collective_id=collective_id, has_side_effects=True, vmem_limit_bytes=VMEM_LIMIT
        ),
        name=name,
    )(*partials)


def stage_sizes(devices):
    sizes = []
    while devices > 1:
        size = next(s for s in (8, 4, 2, 7, 5, 3, devices) if devices % s == 0)
        sizes.append(size)
        devices //= size
    return sizes


class Exchange:
    def __init__(self, sizes, reps, buffers):
        self.sizes, self.reps = sizes, reps
        self.mine, self.slots, self.sems = buffers[0], buffers[1:-1], buffers[-1]
        place = lax.axis_index("fsdp") * reps + lax.axis_index("rep")
        self.stages = []
        stride = 1
        for size in sizes:
            position = (place // stride) % size
            peers = []
            for d in range(1, size):
                target = place + ((position + d) % size - position) * stride
                peers.append((target // reps, target % reps))
            self.stages.append((size, position, peers))
            stride *= size
        self.peers = [peer for stage in self.stages for peer in stage[2]]
        self.waits = []

    def total(self, round, current, moments):
        number = len(current)
        spans, start = [], 0
        for value in current:
            spans.append((start, value.shape[1]))
            start += value.shape[1]
        for index, (size, position, peers) in enumerate(self.stages):
            used = pl.ds(0, sum(length for _, length in spans))
            mine = self.mine.at[round, index, :, used]
            slots = self.slots[index].at[round, :, :, used]
            for (start, length), value in zip(spans, current):
                mine[:, start : start + length] = value
            for d, (target, rep) in enumerate(peers, 1):
                copy = remote(mine, slots.at[position], self.sems.at[round, index, d - 1], target, rep)
                copy.start()
                self.waits.append(copy)
            slots[position] = mine[...]
            for d, (target, rep) in enumerate(peers, 1):
                there = slots.at[(position + size - d) % size]
                remote(there, there, self.sems.at[round, index, d - 1], target, rep).wait_recv()
            parts = [
                [slots[j, :, start : start + length] for start, length in spans] for j in range(size)
            ]
            current = [functools.reduce(jnp.add, [part[row] for part in parts]) for row in range(number)]
            if moments:
                centre = current[0] / current[2][:, :1]
                squares = current[1]
                for part in parts:
                    count = part[2][:, :1]
                    off = part[0] / count - centre
                    squares = squares + count * off * off
                current[1] = squares
        return current

    def finish(self):
        for copy in self.waits:
            copy.wait_send()


def exchange_buffers(sizes, rounds, total):
    return (
        [pltpu.VMEM((rounds, len(sizes), 1, total), f32)]
        + [pltpu.VMEM((rounds, size, 1, total), f32) for size in sizes]
        + [DMA((rounds, len(sizes), max(max(sizes) - 1, 1), 2))]
    )


def exchange_kernel(sizes, reps, moments, *refs):
    number = 3 if moments else 2
    sources, results = refs[:number], refs[number : 2 * number]
    over = Exchange(sizes, reps, refs[2 * number :])
    greet(over.peers)
    current = over.total(0, [source[...] for source in sources], moments)
    for result, value in zip(results, current):
        result[...] = value
    over.finish()


def exchange(rows, fsdp, reps, moments, collective_id, name):
    sizes = stage_sizes(fsdp * reps)
    width = rows[0].shape[-1]
    padded = -(-width // LANES) * LANES
    rows = [jnp.pad(row.reshape(1, -1), ((0, 0), (0, padded - width))) for row in rows[:2]] + [
        jnp.broadcast_to(row.reshape(1, 1), (1, LANES)) for row in rows[2:]
    ]
    results = pl.pallas_call(
        functools.partial(exchange_kernel, sizes, reps, moments),
        out_shape=[jax.ShapeDtypeStruct(row.shape, f32) for row in rows],
        in_specs=[IN_VMEM] * len(rows),
        out_specs=[IN_VMEM] * len(rows),
        scratch_shapes=exchange_buffers(sizes, 1, sum(row.shape[1] for row in rows)),
        compiler_params=pltpu.CompilerParams(
            collective_id=collective_id, has_side_effects=True, vmem_limit_bytes=4 * 1024 * 1024
        ),
        name=name,
    )(*rows)
    return [result[0, :width] for result in results[:2]] + [result[0, 0] for result in results[2:]]


TANH_SCALE = 0.7978845608028654
CUBIC = 0.044715


def gelu_parts(x):
    square = x * x
    bend = jnp.tanh(TANH_SCALE * x * (1.0 + CUBIC * square))
    half = 0.5 * (1.0 + bend)
    slope = half + 0.5 * x * (1.0 - bend * bend) * (TANH_SCALE * (1.0 + 3.0 * CUBIC * square))
    return x * half, slope


def fold_rows(values):
    groups, slots, width = values.shape
    return jnp.sum(values.reshape(groups * slots // 8, 8, width), axis=0)


def whole_row(values):
    return jnp.sum(values, axis=0, keepdims=True)


def dot(left, right):
    return jnp.dot(left, right, preferred_element_type=f32)


def dot_t(left, right):
    return lax.dot_general(left, right, (((1,), (1,)), ((), ())), preferred_element_type=f32)


class Scatter:
    def __init__(self, dims, reps, terms, rows, buffers):
        count = len(terms)
        self.dims, self.reps, self.terms, self.rows = dims, reps, terms, rows
        self.from_rep, self.from_v, self.from_u, self.from_a, self.share = (
            buffers[i * count : (i + 1) * count] for i in range(5)
        )
        self.r_sem, self.v_sem, self.u_sem, self.a_sem, self.s_sem = buffers[5 * count :]
        self.place = Place(dims, reps)
        self.waits = []

    def push(self, source, there, sems, target, target_rep):
        copy = remote(source, there, sems, target, target_rep)
        copy.start()
        self.waits.append(copy)

    def landed(self, there, sems):
        remote(there, there, sems, self.place.me, self.place.rep).wait_recv()

    def part(self, k, index, which):
        rows = self.rows[k]
        start = pl.multiple_of(index * rows, rows)
        return self.terms[k].at[pl.ds(start, rows), columns(self.terms[k].shape[1] // self.reps, which)]

    def order(self):
        size_a, size_b, size_c = self.dims
        for dv in list(range(1, size_c)) + [0]:
            for du in list(range(1, size_b)) + [0]:
                for da in list(range(1, size_a)) + [0]:
                    yield da, du, dv

    def cores(self, k):
        place = self.place
        for da, du, dv in self.order():
            for d in range(1, self.reps):
                other = (place.rep + d) % self.reps
                index = Place(self.dims, self.reps, other).at(da, du, dv)
                self.push(
                    self.part(k, index, other), self.from_rep[k].at[d - 1, index],
                    self.r_sem.at[k, da, du, dv, d - 1], place.me, other,
                )

    def hop(self, k, lag):
        if 0 <= k < len(self.terms):
            for da, du, dv in self.order():
                if lag == (0 if dv else 1 if du else 2 if da else 3):
                    self.handle(k, da, du, dv)

    def handle(self, k, da, du, dv):
        size_a, size_b, size_c = self.dims
        place, reps, rep = self.place, self.reps, self.place.rep
        index = place.at(da, du, dv)
        mine = self.part(k, index, rep)
        total = mine[...].astype(f32)
        for d in range(1, reps):
            self.landed(self.from_rep[k].at[d - 1, index], self.r_sem.at[k, da, du, dv, d - 1])
            total = total + self.from_rep[k][d - 1, index].astype(f32)
        if dv == 0:
            for e in range(1, size_c):
                self.landed(self.from_v[k].at[e - 1, da, du], self.v_sem.at[k, da, du, e - 1])
                total = total + self.from_v[k][e - 1, da, du].astype(f32)
            if du == 0:
                for e in range(1, size_b):
                    self.landed(self.from_u[k].at[e - 1, da], self.u_sem.at[k, da, e - 1])
                    total = total + self.from_u[k][e - 1, da].astype(f32)
                if da == 0:
                    for e in range(1, size_a):
                        self.landed(self.from_a[k].at[e - 1], self.a_sem.at[k, e - 1])
                        total = total + self.from_a[k][e - 1].astype(f32)
        if (da, du, dv) == (0, 0, 0):
            self.share[k][rep] = total.astype(bf16)
            for d in range(1, reps):
                self.push(self.share[k].at[rep], self.share[k].at[rep], self.s_sem.at[k, d - 1], place.me, (rep + d) % reps)
            return
        mine[...] = total.astype(bf16)
        if dv:
            self.push(mine, self.from_v[k].at[dv - 1, da, du], self.v_sem.at[k, da, du, dv - 1], place.at(0, 0, dv), rep)
        elif du:
            self.push(mine, self.from_u[k].at[du - 1, da], self.u_sem.at[k, da, du - 1], place.at(0, du, 0), rep)
        else:
            self.push(mine, self.from_a[k].at[da - 1], self.a_sem.at[k, da - 1], place.at(da, 0, 0), rep)

    def finish(self, totals):
        for k, total in enumerate(totals):
            width = self.terms[k].shape[1] // self.reps
            for d in range(1, self.reps):
                self.landed(self.share[k].at[(self.place.rep + self.reps - d) % self.reps], self.s_sem.at[k, d - 1])
            for which in range(self.reps):
                total[:, which * width : (which + 1) * width] = self.share[k][which].astype(f32)
        for copy in self.waits:
            copy.wait_send()


def scatter_buffers(dims, reps, shapes):
    size_a, size_b, size_c = dims
    count = len(shapes)
    others = max(reps - 1, 1)

    def buffers(*lead):
        return [pltpu.VMEM(lead + (rows, width // reps), bf16) for rows, width in shapes]

    return (
        buffers(others, size_a * size_b * size_c)
        + buffers(max(size_c - 1, 1), size_a, size_b)
        + buffers(max(size_b - 1, 1), size_a)
        + buffers(max(size_a - 1, 1))
        + buffers(reps)
        + [
            DMA((count, size_a, size_b, size_c, others, 2)),
            DMA((count, size_a, size_b, max(size_c - 1, 1), 2)),
            DMA((count, size_a, max(size_b - 1, 1), 2)),
            DMA((count, max(size_a - 1, 1), 2)),
            DMA((count, others, 2)),
        ]
    )


def terms_kernel(dims, reps, rows, *refs):
    (small, block_low, grad_reduced, act_two, grad_expanded, modulated, grad_middle, change, grad_gate) = refs[:9]
    totals = refs[9:15]
    terms = refs[15:21]
    pads, line, turned, chunk, pad_sem, line_sem, chunk_sem, small_sem = refs[21:29]
    scatter = Scatter(dims, reps, terms, rows, refs[29:])
    slots, mid_width = modulated.shape[2:]
    lines = block_low.shape[0]
    width = block_low.shape[2]
    step = chunk.shape[-1]
    chunks = width // step
    ring = 2

    place = scatter.place
    small_copy = pltpu.make_async_copy(small, terms[0], small_sem)
    small_copy.start()
    sources = [(block_low, j) for j in range(chunks)] + [(grad_expanded, j) for j in range(chunks)]

    def load(number):
        source, j = sources[number]
        return pltpu.make_async_copy(
            source.at[:, :, j * step : (j + 1) * step], chunk.at[number % 2], chunk_sem.at[number % 2]
        )

    gradients = [grad_reduced, grad_middle, grad_gate, act_two]

    def turn(number):
        pltpu.make_async_copy(gradients[number], line, line_sem).wait()
        turned[...] = jnp.transpose(line[...].reshape(-1, mid_width))
        if number + 1 < len(gradients):
            pltpu.make_async_copy(gradients[number + 1], line, line_sem).start()

    load(0).start()
    pltpu.make_async_copy(gradients[0], line, line_sem).start()
    inner = pl.ds(ring, GRID)
    for index, source in enumerate((modulated, change)):
        for side in (slice(0, ring), slice(GRID + ring, GRID + 2 * ring)):
            pads[index, side] = jnp.zeros((ring, GRID + 2 * ring, slots, mid_width), bf16)
            pads[index, ring : GRID + ring, side] = jnp.zeros((GRID, ring, slots, mid_width), bf16)
        pltpu.make_async_copy(source, pads.at[index, inner, inner], pad_sem.at[index]).start()
    place.greet()

    def flow(*hops):
        for k, lag in hops:
            scatter.hop(k, lag)

    def piece(number):
        if number + 1 < len(sources):
            load(number + 1).start()
        load(number).wait()
        return dot(turned[...], chunk[number % 2].reshape(-1, step))

    def reduce_pieces(first, last):
        for j in range(first, last):
            terms[1][j * step : (j + 1) * step, :] = jnp.transpose(piece(j)).astype(bf16)

    def expand_pieces(first, last):
        for j in range(first, last):
            terms[2][:, j * step : (j + 1) * step] = piece(chunks + j).astype(bf16)

    def taps(k, pad, stride, first, last):
        def tap(t, _):
            top = ring + (t // 3 - 1) * stride
            left = ring + (t % 3 - 1) * stride
            source = pads[pad, pl.ds(top, GRID), pl.ds(left, GRID)].reshape(-1, mid_width)
            values = dot(turned[...], source)
            start = pl.multiple_of(t * mid_width, mid_width)
            terms[k][pl.ds(start, mid_width), :] = jnp.transpose(values).astype(bf16)
            return 0

        lax.fori_loop(first, last, tap, 0)

    def padded(pad):
        pltpu.make_async_copy((modulated, change)[pad], pads.at[pad, inner, inner], pad_sem.at[pad]).wait()

    half = chunks // 2
    small_copy.wait()
    scatter.cores(0)
    turn(0)
    reduce_pieces(0, half)
    flow((0, 0))
    reduce_pieces(half, chunks)
    scatter.cores(1)
    turn(1)
    padded(0)
    taps(3, 0, 1, 0, 3)
    flow((1, 0), (0, 1))
    taps(3, 0, 1, 3, 6)
    flow((1, 1), (0, 2))
    taps(3, 0, 1, 6, 9)
    scatter.cores(3)
    turn(2)
    padded(1)
    flow((1, 2), (0, 3))
    taps(4, 1, 1, 0, 3)
    flow((3, 0))
    taps(4, 1, 1, 3, 6)
    flow((1, 3))
    taps(4, 1, 1, 6, 9)
    scatter.cores(4)
    taps(5, 1, 2, 0, 3)
    flow((4, 0), (3, 1))
    taps(5, 1, 2, 3, 6)
    taps(5, 1, 2, 6, 9)
    scatter.cores(5)
    turn(3)
    flow((3, 2))
    expand_pieces(0, half)
    flow((5, 0), (4, 1))
    expand_pieces(half, chunks)
    scatter.cores(2)
    flow((3, 3), (4, 2), (2, 0), (5, 1), (2, 1), (4, 3), (5, 2), (2, 2), (5, 3), (2, 3))
    scatter.finish(totals)


def terms_all(small, block_low, grad_reduced, act_two, grad_expanded, modulated, grad_middle, change, grad_gate, rows, fsdp, reps, collective_id):
    dims = factor_three(fsdp)
    lines, line_rows, width = block_low.shape
    mid_width = act_two.shape[-1]
    slots = modulated.shape[2]
    shapes = [(rows[0], width), (rows[1], mid_width), (rows[2], width)] + [(rows[3], mid_width)] * 3
    rows = [rows[0], rows[1], rows[2], rows[3], rows[3], rows[3]]
    side = GRID + 4
    return pl.pallas_call(
        functools.partial(terms_kernel, dims, reps, rows),
        out_shape=[jax.ShapeDtypeStruct(shape, f32) for shape in shapes],
        in_specs=[ANY] * 9,
        out_specs=[IN_VMEM] * 6,
        scratch_shapes=[pltpu.VMEM((fsdp * a, b), bf16) for a, b in shapes]
        + [
            pltpu.VMEM((2, side, side, slots, mid_width), bf16),
            pltpu.VMEM((lines, line_rows, mid_width), bf16),
            pltpu.VMEM((mid_width, lines * line_rows), bf16),
            pltpu.VMEM((2, lines, line_rows, 256), bf16),
            DMA((2,)), DMA(()), DMA((2,)), DMA(()),
        ]
        + scatter_buffers(dims, reps, shapes),
        compiler_params=pltpu.CompilerParams(
            collective_id=collective_id, has_side_effects=True, vmem_limit_bytes=VMEM_LIMIT
        ),
        name="terms",
    )(small, block_low, grad_reduced, act_two, grad_expanded, modulated, grad_middle, change, grad_gate)


class Gather:
    def __init__(self, dims, reps, shards, fulls, buffers):
        self.dims, self.reps, self.shards, self.fulls = dims, reps, shards, fulls
        self.own_sem, self.a_sem, self.b_sem, self.c_sem, self.r_sem = buffers
        self.place = Place(dims, reps)
        self.waits, self.local = [], []

    def slot(self, k, index, which):
        full = self.fulls[k]
        return full.at[index, :, columns(full.shape[-1] // self.reps, which)]

    def push(self, k, da, du, dv, target, target_rep, sems):
        index, rep = self.place.at(-da, -du, -dv), self.place.rep
        if (da, du, dv) == (0, 0, 0):
            source = self.shards[k].at[:, columns(self.shards[k].shape[-1] // self.reps, rep)]
        else:
            source = self.slot(k, index, rep)
        copy = remote(source, self.slot(k, index, rep), sems, target, target_rep)
        copy.start()
        self.waits.append(copy)

    def landed(self, k, da, du, dv, which, sems):
        there = self.slot(k, self.place.at(-da, -du, -dv), which)
        remote(there, there, sems, self.place.me, self.place.rep).wait_recv()

    def forward(self, k, da, du, dv):
        size_a, size_b, size_c = self.dims
        place, rep = self.place, self.place.rep
        if dv == 0 and du == 0:
            for d in range(1, size_b):
                self.push(k, da, 0, 0, place.at(0, d, 0), rep, self.b_sem.at[k, da, d - 1])
        if dv == 0:
            for d in range(1, size_c):
                self.push(k, da, du, 0, place.at(0, 0, d), rep, self.c_sem.at[k, da, du, d - 1])
        if (da, du, dv) != (0, 0, 0):
            for d in range(1, self.reps):
                self.push(k, da, du, dv, place.me, (rep + d) % self.reps, self.r_sem.at[k, da, du, dv, d - 1])

    def begin(self, k):
        place = self.place
        copy = pltpu.make_async_copy(self.shards[k], self.fulls[k].at[place.me], self.own_sem.at[k])
        copy.start()
        self.local.append(copy)
        for d in range(1, self.dims[0]):
            self.push(k, 0, 0, 0, place.at(d, 0, 0), place.rep, self.a_sem.at[k, d - 1])
        self.forward(k, 0, 0, 0)

    def hop(self, k, lag):
        size_a, size_b, size_c = self.dims
        place, reps, rep = self.place, self.reps, self.place.rep
        if lag == 0:
            for da in range(1, size_a):
                self.landed(k, da, 0, 0, rep, self.a_sem.at[k, da - 1])
                self.forward(k, da, 0, 0)
        elif lag == 1:
            for du in range(1, size_b):
                for da in range(size_a):
                    self.landed(k, da, du, 0, rep, self.b_sem.at[k, da, du - 1])
                    self.forward(k, da, du, 0)
        elif lag == 2:
            for dv in range(1, size_c):
                for du in range(size_b):
                    for da in range(size_a):
                        self.landed(k, da, du, dv, rep, self.c_sem.at[k, da, du, dv - 1])
                        self.forward(k, da, du, dv)
        else:
            for dv in range(size_c):
                for du in range(size_b):
                    for da in range(size_a):
                        if (da, du, dv) != (0, 0, 0):
                            for d in range(1, reps):
                                self.landed(k, da, du, dv, (rep + reps - d) % reps, self.r_sem.at[k, da, du, dv, d - 1])
            self.local[k].wait()

    def finish(self):
        for copy in self.waits:
            copy.wait_send()


def gather_buffers(dims, reps, count):
    size_a, size_b, size_c = dims
    return [
        DMA((count,)),
        DMA((count, max(size_a - 1, 1), 2)),
        DMA((count, size_a, max(size_b - 1, 1), 2)),
        DMA((count, size_a, size_b, max(size_c - 1, 1), 2)),
        DMA((count, size_a, size_b, size_c, max(reps - 1, 1), 2)),
    ]


def head_kernel(dims, reps, sizes, stem_rows, *refs):
    stem_own, reduce_own, diff_own, mid_own, expand_own = refs[:5]
    lateral_own, wide_own, narrow_own, least_own, lhs, valid, pair, count, features = refs[5:14]
    (lateral_out, vector_out, reduce_out, diff_out, mid_out, expand_out, block_in, block_low, stem_normed, pool_low, stem_inverse,
     number_out, normed_one, inverse_one, act_one, change) = refs[14:30]
    (small_own, small, stem_taps, reduce_full, tap_rows, lateral, stem_values, stem_act, loaded, wide, low, reduced) = refs[30:42]
    load_sem, wide_sem, low_sem, out_sem = refs[42:46]
    gather = Gather(
        dims, reps, [small_own, stem_own, reduce_own, diff_own.at[0], diff_own.at[1], mid_own, expand_own],
        [small, stem_taps, reduce_full, diff_out.at[0], diff_out.at[1], mid_out, expand_out], refs[46:51],
    )
    over = Exchange(sizes, reps, refs[51:])
    fsdp = small.shape[0]
    me = gather.place.me
    stem_width = stem_rows * fsdp
    lines, rows, mid_width = reduced.shape
    clips, pixels, segs, width = features.shape
    slots = valid.shape[0]
    groups = rows // slots
    step = 256
    chunks = width // step
    mask = valid[:, :1].reshape(1, slots, 1)
    pairs = pair[:, :1].reshape(1, slots, 1)
    own = count[:, :1]

    def load(j):
        cols = slice(j * step, (j + 1) * step)
        return [
            pltpu.make_async_copy(
                features.at[clip, :, :, cols], loaded.at[j % 2, :, clip * segs : (clip + 1) * segs, :], load_sem.at[j % 2, clip]
            )
            for clip in range(clips)
        ]

    def grouped(values):
        return values.reshape(groups, slots, values.shape[-1])

    def moments(carry, origin):
        away, squares = whole_row(carry[0]), whole_row(carry[1])
        return [away + own * origin, jnp.maximum(squares - away * away / own, 0.0), count[...]]

    def add_moments(carry, values, origin):
        off = (grouped(values) - origin.reshape(1, 1, -1)) * mask
        return carry[0] + fold_rows(off), carry[1] + fold_rows(off * off)

    def blank(n):
        return jnp.zeros((8, n), f32), jnp.zeros((8, n), f32)

    for copy in load(0):
        copy.start()

    def placed(values, length):
        share = values.shape[1]
        one = lax.broadcasted_iota(jnp.int32, (share, length), 1) - me * share
        hot = (one == lax.broadcasted_iota(jnp.int32, (share, length), 0)).astype(f32).astype(bf16)
        return dot(values, hot)

    least = placed(least_own[...], LANES * -(-stem_width // LANES))
    narrow = placed(narrow_own[...], mid_width)
    pieces = [narrow[n : n + 1] for n in range(narrow.shape[0])] + [least[n : n + 1] for n in range(least.shape[0])]
    joined = jnp.concatenate(pieces, axis=1)
    joined = jnp.concatenate([joined, jnp.zeros((1, -joined.shape[1] % width), f32)], axis=1)
    small_rows = [lateral_own[...].astype(f32), placed(wide_own[...], width)]
    small_rows += [joined[:, n * width : (n + 1) * width] for n in range(joined.shape[1] // width)]
    taken = sum(row.shape[0] for row in small_rows)
    small_rows.append(jnp.zeros((small_own.shape[0] - taken, width), f32))
    small_own[...] = jnp.concatenate(small_rows, axis=0).astype(bf16)
    gather.place.greet(over.peers)
    gather.begin(0)
    gather.begin(1)
    gather.begin(2)
    gather.begin(3)
    gather.begin(4)
    gather.begin(5)
    gather.begin(6)
    stem_act[...] = jnp.zeros(stem_act.shape, f32)
    gather.hop(0, 0)
    gather.hop(1, 0)
    gather.hop(0, 1)
    gather.hop(1, 1)
    gather.hop(0, 2)
    gather.hop(1, 2)
    gather.hop(0, 3)
    gather.hop(1, 3)
    vectors = jnp.zeros((taken - stem_rows, width), f32)
    for device in range(fsdp):
        values = small[device].astype(f32)
        span = slice(device * stem_rows, (device + 1) * stem_rows)
        lateral[span, :] = values[:stem_rows]
        vectors = vectors + values[stem_rows:taken]
        taps = stem_taps[device].astype(f32)
        for x in range(GRID):
            tap_rows[x, span, :] = taps[x * stem_rows : (x + 1) * stem_rows]
    lateral_low = lateral[...].astype(bf16)
    vector_out[...] = vectors
    lateral_out[...] = lateral_low

    def vector(position, length):
        row, start = 2 + position // width, position % width
        return vectors[row : row + 1, start : start + length]

    gain_one, shift_one = vector(0, mid_width), vector(mid_width, mid_width)
    start = mid_width * narrow.shape[0]
    stem_gain, stem_shift = vector(start, stem_width), vector(start + least.shape[1], stem_width)
    gather.hop(2, 0)
    gather.hop(3, 0)
    gather.hop(2, 1)

    def stem_column(x, _):
        stem_values[x] = dot_t(lhs[...], tap_rows[x].astype(bf16))
        return 0

    lax.fori_loop(0, GRID, stem_column, 0)
    origin = stem_values[0, 0:1, :]
    carry = lax.fori_loop(0, GRID, lambda x, c: add_moments(c, stem_values[x], origin), blank(stem_width))
    gather.hop(4, 0)
    gather.hop(3, 1)
    total, squares, number = over.total(0, moments(carry, origin), True)
    number_out[...] = number
    number = number[:, :1]
    centre, inverse = total / number, lax.rsqrt(squares / number + epsilon)
    stem_inverse[...] = inverse
    gather.hop(5, 0)
    gather.hop(2, 2)
    gather.hop(4, 1)

    def stem_norm(x, _):
        normed = (stem_values[x] - centre) * inverse
        stem_normed[:, x] = grouped(normed)
        zeta = mask * (grouped(normed) * stem_gain.reshape(1, 1, -1) + stem_shift.reshape(1, 1, -1))
        stem_act[x + 1, 1 : GRID + 1] = gelu_parts(zeta)[0]
        return 0

    lax.fori_loop(0, GRID, stem_norm, 0)

    def stem_pool(x, _):
        total = stem_act[x] + stem_act[x + 1] + stem_act[x + 2]
        total = total[0:GRID] + total[1 : GRID + 1] + total[2 : GRID + 2]
        pool_low[:, x] = (total / 9.0).astype(bf16)
        return 0

    lax.fori_loop(0, GRID, stem_pool, 0)
    gather.hop(2, 3)

    later = [[], [(6, 0)], [(5, 1)], [], [(6, 1)], [(3, 2)], [], [(4, 2)]]
    for j in range(chunks):
        slot = j % 2
        cols = slice(j * step, (j + 1) * step)
        for copy in load(j + 1) if j + 1 < chunks else ():
            copy.start()
        for copy in load(j):
            copy.wait()
        out_wide = pltpu.make_async_copy(wide.at[slot], block_in.at[:, :, cols], wide_sem.at[slot])
        out_low = pltpu.make_async_copy(low.at[slot], block_low.at[:, :, cols], low_sem.at[slot])

        if j >= 2:
            out_wide.wait()
            out_low.wait()
        shares = step // reduce_full.shape[1]
        weight = reduce_full[j * shares : (j + 1) * shares].reshape(step, mid_width)

        def line(y, _):
            values = loaded[slot, pl.ds(y * groups, groups)].astype(f32).reshape(rows, step)
            values = values + dot(pool_low[y].reshape(rows, stem_width), lateral_low[:, cols])
            wide[slot, y] = values
            rounded = values.astype(bf16)
            low[slot, y] = rounded
            product = dot(rounded, weight)
            reduced[y] = product if j == 0 else reduced[y] + product
            return 0

        lax.fori_loop(0, lines, line, 0)
        out_wide.start()
        out_low.start()
        for k, lag in later[j] if j < len(later) else ():
            gather.hop(k, lag)
    pltpu.make_async_copy(reduce_full, reduce_out, out_sem).start()

    origin = reduced[0, 0:1, :]
    carry = lax.fori_loop(0, lines, lambda y, c: add_moments(c, reduced[y], origin), blank(mid_width))
    total, squares, _ = over.total(1, moments(carry, origin), True)
    centre, inverse = total / number, lax.rsqrt(squares / number + epsilon)
    inverse_one[...] = inverse
    gather.hop(5, 2)

    def first(y, _):
        normed = (reduced[y] - centre) * inverse
        normed_one[y] = normed
        zeta = mask * (grouped(normed) * gain_one.reshape(1, 1, -1) + shift_one.reshape(1, 1, -1))
        act = gelu_parts(zeta)[0].reshape(rows, mid_width)
        act_one[y] = act
        change[y] = (pairs * grouped(pltpu.roll(act, rows - 1, 0) - act)).astype(bf16).reshape(rows, mid_width)
        return 0

    lax.fori_loop(0, lines, first, 0)
    gather.hop(6, 2)
    for k in range(3, 7):
        gather.hop(k, 3)
    for j in (chunks - 2, chunks - 1):
        cols = slice(j * step, (j + 1) * step)
        pltpu.make_async_copy(wide.at[j % 2], block_in.at[:, :, cols], wide_sem.at[j % 2]).wait()
        pltpu.make_async_copy(low.at[j % 2], block_low.at[:, :, cols], low_sem.at[j % 2]).wait()
    pltpu.make_async_copy(reduce_full, reduce_out, out_sem).wait()
    gather.finish()
    over.finish()


def head(stem_taps, reduce_weight, diff_weight, mid_weight, expand_weight, lateral, wide, narrow, least, lhs, valid, pair, count, features, fsdp, reps, collective_id):
    dims, sizes = factor_three(fsdp), stage_sizes(fsdp * reps)
    shape = jax.ShapeDtypeStruct
    clips, pixels, segs, width = features.shape
    slots = clips * segs
    mid_width = reduce_weight.shape[1]
    stem_rows = lateral.shape[0]
    stem_width = stem_rows * fsdp
    rows = GRID * slots
    step = 256
    side = GRID + 2
    lengths = narrow.shape[0] * mid_width + least.shape[0] * (-(-stem_width // LANES) * LANES)
    vectors = 2 + -(-lengths // width)
    small = shape((-(-(stem_rows + vectors) // 16) * 16, width), bf16)

    def full(shard):
        return shape(shard.shape[:-2] + (fsdp,) + shard.shape[-2:], shard.dtype)

    def whole(shard):
        return pltpu.VMEM((fsdp,) + shard.shape, shard.dtype)

    return pl.pallas_call(
        functools.partial(head_kernel, dims, reps, sizes, stem_rows),
        out_shape=[
            shape((stem_width, width), bf16), shape((vectors, width), f32),
            full(reduce_weight), full(diff_weight), full(mid_weight), full(expand_weight),
            shape((GRID, rows, width), f32), shape((GRID, rows, width), bf16),
            shape((GRID, GRID, slots, stem_width), f32), shape((GRID, GRID, slots, stem_width), bf16),
            shape((1, stem_width), f32), shape((1, LANES), f32),
            shape((GRID, rows, mid_width), f32), shape((1, mid_width), f32), shape((GRID, rows, mid_width), f32),
            shape((GRID, rows, mid_width), bf16),
        ],
        in_specs=[ANY] * 5 + [IN_VMEM] * 8 + [ANY],
        out_specs=[IN_VMEM] * 2 + [ANY] * 6 + [IN_VMEM] * 8,
        scratch_shapes=[
            pltpu.VMEM(small.shape, bf16), whole(small), whole(stem_taps), whole(reduce_weight),
            pltpu.VMEM((GRID, stem_width, stem_taps.shape[1]), f32), pltpu.VMEM((stem_width, width), f32),
            pltpu.VMEM((GRID, rows, stem_width), f32), pltpu.VMEM((side, side, slots, stem_width), f32),
            pltpu.VMEM((2, pixels, slots, step), bf16),
            pltpu.VMEM((2, GRID, rows, step), f32), pltpu.VMEM((2, GRID, rows, step), bf16),
            pltpu.VMEM((GRID, rows, mid_width), f32),
            DMA((2, clips)), DMA((2,)), DMA((2,)), DMA(()),
        ] + gather_buffers(dims, reps, 7) + exchange_buffers(sizes, 2, 2 * mid_width + LANES),
        compiler_params=pltpu.CompilerParams(
            collective_id=collective_id, has_side_effects=True, vmem_limit_bytes=VMEM_LIMIT
        ),
        name="head",
    )(stem_taps, reduce_weight, diff_weight, mid_weight, expand_weight, lateral, wide, narrow, least, lhs, valid, pair, count, features)


def tail_kernel(sizes, reps, clip_count, *refs):
    (middle, expand, valid, spread, count, gain_two, shift_two, gain_three, shift_three, pooled_grad, block_in) = refs[:11]
    (pooled, grad_pre, grad_expanded, act_two, grad_middle, gain_three_sum, shift_three_sum, gain_two_sum, shift_two_sum) = refs[11:20]
    (wide, wide_grad, narrow, narrow_grad, block, low, totals, first, block_sem, pre_sem, low_sem) = refs[20:31]
    over = Exchange(sizes, reps, refs[31:])
    lines, rows, mid_width = middle.shape
    width = expand.shape[1]
    slots = valid.shape[0]
    segs = slots // clip_count
    groups = rows // slots
    step = 256
    chunks = width // step

    barrier = pltpu.get_barrier_semaphore()
    for target, rep in over.peers:
        pl.semaphore_signal(barrier, inc=1, device_id={"fsdp": target, "rep": rep}, device_id_type=MESH)

    def fetch(y, slot):
        return pltpu.make_async_copy(block_in.at[y], block.at[slot], block_sem.at[slot])

    fetch(0, 0).start()
    mask = valid[:, :1].reshape(1, slots, 1)
    own = count[:, :1]

    def grouped(values):
        return values.reshape(groups, slots, values.shape[-1])

    def moments(carry, origin):
        away, squares = whole_row(carry[0]), whole_row(carry[1])
        return away + own * origin, jnp.maximum(squares - away * away / own, 0.0)

    def gather_moments(carry, values, origin):
        off = (grouped(values) - origin.reshape(1, 1, -1)) * mask
        return carry[0] + fold_rows(off), carry[1] + fold_rows(off * off)

    def blank(n):
        return jnp.zeros((8, n), f32), jnp.zeros((8, n), f32)

    origin = middle[0, 0:1, :]
    carry = lax.fori_loop(0, lines, lambda y, c: gather_moments(c, middle[y], origin), blank(mid_width))
    pl.semaphore_wait(barrier, len(over.peers))
    total, squares, number = over.total(0, list(moments(carry, origin)) + [count[...]], True)
    number = number[:, :1]
    centre_two, inverse_two = total / number, lax.rsqrt(squares / number + epsilon)
    gain2, shift2 = gain_two[...], shift_two[...]

    def zeta_two(normed):
        return mask * (grouped(normed) * gain2.reshape(1, 1, -1) + shift2.reshape(1, 1, -1))

    def forward_two(y, _):
        normed = (middle[y] - centre_two) * inverse_two
        narrow[y] = normed
        act_two[y] = gelu_parts(zeta_two(normed))[0].astype(bf16).reshape(rows, mid_width)
        return 0

    lax.fori_loop(0, lines, forward_two, 0)

    def expand_chunk(j, _):
        cols = pl.ds(pl.multiple_of(j * step, step), step)
        weight = expand[:, cols]
        origin = dot(act_two[0, 0:16, :], weight)[0:1]

        def line(y, carry):
            values = dot(act_two[y], weight)
            wide[y, :, cols] = values
            return gather_moments(carry, values, origin)

        total, squares = moments(lax.fori_loop(0, lines, line, blank(step)), origin)
        totals[0, :, cols] = total
        totals[1, :, cols] = squares
        return 0

    lax.fori_loop(0, chunks, expand_chunk, 0)
    total, squares, _ = over.total(1, [totals[0], totals[1], count[...]], True)
    totals[0] = total / number
    totals[1] = lax.rsqrt(squares / number + epsilon)
    for index in range(2):
        first[index] = jnp.zeros((8, width), f32)

    def out_pre(y):
        return pltpu.make_async_copy(wide_grad.at[y], grad_pre.at[y], pre_sem.at[y])

    def forward_three(y, _):
        slot = y % 2
        fetch(y, slot).wait()

        @pl.when(y + 1 < lines)
        def _():
            fetch(y + 1, 1 - slot).start()

        def chunk(j, _):
            cols = pl.ds(pl.multiple_of(j * step, step), step)
            normed = (wide[y, :, cols] - totals[0, :, cols]) * totals[1, :, cols]
            wide[y, :, cols] = normed
            normed = grouped(normed)
            scaled = mask * (gain_three[:, cols].reshape(1, 1, step) * normed + shift_three[:, cols].reshape(1, 1, step))
            out, slope = gelu_parts(grouped(block[slot, :, cols]) + scaled)
            grads = []
            for clip in range(clip_count):
                span = slice(clip * segs, (clip + 1) * segs)
                share = spread[span, :1].reshape(1, segs, 1)
                pixels = pl.ds(y * groups, groups)
                pooled[clip, pixels, :, cols] = jnp.sum(out[:, span] * share, axis=1, keepdims=True)
                grads.append(slope[:, span] * (pooled_grad[clip, pixels, :, cols] * share))
            grad = jnp.concatenate(grads, axis=1)
            wide_grad[y, :, cols] = grad.reshape(rows, step)
            first[0, :, cols] += fold_rows(grad)
            first[1, :, cols] += fold_rows(grad * normed)
            return 0

        lax.fori_loop(0, chunks, chunk, 0)
        out_pre(y).start()
        return 0

    lax.fori_loop(0, lines, forward_three, 0)
    shift_sum, gain_sum = over.total(2, [whole_row(first[0]), whole_row(first[1])], False)
    shift_three_sum[...] = shift_sum
    gain_three_sum[...] = gain_sum
    totals[2] = shift_sum / number
    totals[3] = gain_sum / number
    totals[1] = totals[1] * gain_three[...]

    def out_low(y):
        return pltpu.make_async_copy(low.at[y % 2], grad_expanded.at[y], low_sem.at[y % 2])

    def back_three(y, carry):
        slot = y % 2

        @pl.when(y >= 2)
        def _():
            out_low(y - 2).wait()

        def chunk(j, _):
            cols = pl.ds(pl.multiple_of(j * step, step), step)
            grad = wide_grad[y, :, cols] - totals[2, :, cols] - wide[y, :, cols] * totals[3, :, cols]
            low[slot, :, cols] = (mask * grouped(grad * totals[1, :, cols])).astype(bf16).reshape(rows, step)
            return 0

        lax.fori_loop(0, chunks, chunk, 0)
        out_low(y).start()
        normed = narrow[y]
        grad = grouped(dot_t(low[slot], expand[...])) * gelu_parts(zeta_two(normed))[1] * mask
        narrow_grad[y] = grad.reshape(rows, mid_width)
        return carry[0] + fold_rows(grad), carry[1] + fold_rows(grad * grouped(normed))

    carry = lax.fori_loop(0, lines, back_three, blank(mid_width))
    shift_sum, gain_sum = over.total(3, [whole_row(carry[0]), whole_row(carry[1])], False)
    shift_two_sum[...] = shift_sum
    gain_two_sum[...] = gain_sum
    shift_mean, gain_mean, scale = shift_sum / number, gain_sum / number, inverse_two * gain2

    def back_two(y, _):
        grad = (narrow_grad[y] - shift_mean - narrow[y] * gain_mean) * scale
        grad_middle[y] = (mask * grouped(grad)).astype(bf16).reshape(rows, mid_width)
        return 0

    lax.fori_loop(0, lines, back_two, 0)
    lax.fori_loop(0, lines, lambda y, _: (out_pre(y).wait(), 0)[1], 0)
    for y in (lines - 2, lines - 1):
        out_low(y).wait()
    over.finish()


def tail(middle, expand, valid, spread, count, gain_two, shift_two, gain_three, shift_three, pooled_grad, block_in, clip_count, fsdp, reps, collective_id):
    sizes = stage_sizes(fsdp * reps)
    lines, rows, mid_width = middle.shape
    width = expand.shape[1]
    pixels = pooled_grad.shape[1]
    shape = jax.ShapeDtypeStruct
    return pl.pallas_call(
        functools.partial(tail_kernel, sizes, reps, clip_count),
        out_shape=[
            shape((clip_count, pixels, 1, width), f32), shape((lines, rows, width), f32), shape((lines, rows, width), bf16),
            shape((lines, rows, mid_width), bf16), shape((lines, rows, mid_width), bf16),
            shape((1, width), f32), shape((1, width), f32), shape((1, mid_width), f32), shape((1, mid_width), f32),
        ],
        in_specs=[IN_VMEM] * 10 + [ANY],
        out_specs=[IN_VMEM, ANY, ANY] + [IN_VMEM] * 6,
        scratch_shapes=[
            pltpu.VMEM((lines, rows, width), f32), pltpu.VMEM((lines, rows, width), f32),
            pltpu.VMEM((lines, rows, mid_width), f32), pltpu.VMEM((lines, rows, mid_width), f32),
            pltpu.VMEM((2, rows, width), f32), pltpu.VMEM((2, rows, width), bf16),
            pltpu.VMEM((4, 1, width), f32), pltpu.VMEM((2, 8, width), f32),
            DMA((2,)), DMA((lines,)), DMA((2,)),
        ] + exchange_buffers(sizes, 4, 2 * width + LANES),
        compiler_params=pltpu.CompilerParams(collective_id=collective_id, has_side_effects=True, vmem_limit_bytes=VMEM_LIMIT),
        name="tail",
    )(middle, expand, valid, spread, count, gain_two, shift_two, gain_three, shift_three, pooled_grad, block_in)


def back_kernel(clips, *refs):
    grad_reduced, reduce_full, pool_low, lateral, grad_pre = refs[:5]
    features_grad, lateral_terms, grad_act = refs[5:8]
    loaded, sums, low, total, load_sem, out_sem = refs[8:]
    lines, rows, mid_width = grad_reduced.shape
    width = reduce_full.shape[0]
    groups = GRID
    slots = rows // groups
    segs = slots // clips
    step = 512

    def load(y):
        return pltpu.make_async_copy(grad_pre.at[y], loaded.at[y % 2], load_sem.at[y % 2])

    def store(y):
        slot = y % 2
        return [
            pltpu.make_async_copy(
                sums.at[slot, :, clip * segs : (clip + 1) * segs, :],
                features_grad.at[clip, pl.ds(y * groups, groups)],
                out_sem.at[slot, clip],
            )
            for clip in range(clips)
        ]

    load(0).start()
    total[...] = jnp.zeros(total.shape, f32)

    def line(y, _):
        slot = y % 2
        load(y).wait()

        @pl.when(y + 1 < lines)
        def _():
            load(y + 1).start()

        @pl.when(y >= 2)
        def _():
            for copy in store(y - 2):
                copy.wait()

        for start in range(0, width, step):
            cols = slice(start, start + step)
            values = loaded[slot, :, cols] + dot_t(grad_reduced[y], reduce_full[cols, :])
            sums[slot, :, :, cols] = values.reshape(groups, slots, step)
            low[:, cols] = values.astype(bf16)
        for copy in store(y):
            copy.start()
        grad_act[y] = dot_t(low[...], lateral[...])
        turned = jnp.transpose(pool_low[y])
        for start in range(0, width, step):
            cols = slice(start, start + step)
            total[:, cols] += dot(turned, low[:, cols])
        return 0

    lax.fori_loop(0, lines, line, 0)
    lateral_terms[...] = total[...].astype(bf16)
    for y in (lines - 2, lines - 1):
        for copy in store(y):
            copy.wait()


def back(grad_reduced, reduce_full, pool_low, lateral, grad_pre, clips):
    lines, rows, mid_width = grad_reduced.shape
    width = reduce_full.shape[0]
    slots = rows // GRID
    stem_width = lateral.shape[0]
    shape = jax.ShapeDtypeStruct
    return pl.pallas_call(
        functools.partial(back_kernel, clips),
        out_shape=[
            shape((clips, lines * GRID, slots // clips, width), f32), shape((stem_width, width), bf16),
            shape((lines, rows, stem_width), f32),
        ],
        in_specs=[IN_VMEM] * 4 + [ANY],
        out_specs=[ANY, IN_VMEM, IN_VMEM],
        scratch_shapes=[
            pltpu.VMEM((2, rows, width), f32), pltpu.VMEM((2, GRID, slots, width), f32), pltpu.VMEM((rows, width), bf16),
            pltpu.VMEM((stem_width, width), f32), DMA((2,)), DMA((2, clips)),
        ],
        compiler_params=pltpu.CompilerParams(vmem_limit_bytes=VMEM_LIMIT),
        cost_estimate=pl.CostEstimate(flops=4 * lines * rows * width * mid_width, bytes_accessed=8 * lines * rows * width, transcendentals=0),
        name="back",
    )(grad_reduced, reduce_full, pool_low, lateral, grad_pre)


ORDER = ("HWNC", "HWIO", "HWNC")


def pad_of(span):
    return ((span, span), (span, span))


def convolve(source, weight, span, stride):
    side = 2 * span + 1
    kernel = weight.reshape(side, side, source.shape[-1], -1)
    return lax.conv_general_dilated(
        source, kernel, (1, 1), pad_of(span * stride), rhs_dilation=(stride, stride),
        dimension_numbers=ORDER, preferred_element_type=f32,
    )


def convolve_back(grads, weight, span, stride):
    side = 2 * span + 1
    kernel = weight.reshape(side, side, -1, grads.shape[-1])[::-1, ::-1]
    return lax.conv_general_dilated(
        grads, kernel, (1, 1), pad_of(span * stride), rhs_dilation=(stride, stride),
        dimension_numbers=("HWNC", "HWOI", "HWNC"), preferred_element_type=f32,
    )


def convolve_terms(source, grads, span, stride, kind):
    return lax.conv_general_dilated(
        source, grads, (stride, stride), pad_of(span * stride),
        dimension_numbers=("HWCN", "HWIO", "HWNC"), preferred_element_type=kind,
    )


def pool_mean(source):
    total = lax.reduce_window(source, 0.0, lax.add, (3, 3, 1, 1), (1, 1, 1, 1), "SAME")
    return total / 9.0


def project(source, weight):
    return jnp.einsum("yxnc,cd->yxnd", source, weight, preferred_element_type=f32)


def project_back(grads, weight):
    return jnp.einsum("yxnd,cd->yxnc", grads, weight, preferred_element_type=f32)


def project_terms(source, grads, kind):
    return jnp.einsum("yxnc,yxnd->cd", source, grads, preferred_element_type=kind)


def gelu_back(pre_act, grads):
    return jax.vjp(jax.nn.gelu, pre_act)[1](grads)[0]


def make_shards(fsdp, reps):
    def shards(
        frames, features, seg_counts, stem_weight, stem_gain, stem_shift, lateral, reduce_weight,
        gain_one, shift_one, diff_weight, gate_shift, mid_weight, gain_two, shift_two,
        expand_weight, gain_three, shift_three, pooled_grad,
    ):
        clip_count, seg_slots, pixels, feature_width = features.shape
        slots = clip_count * seg_slots
        mid_width = reduce_weight.shape[1]
        stem_rows, stem_depth = stem_weight.shape
        stem_width = stem_rows * fsdp

        seg_index = lax.broadcasted_iota(jnp.int32, (clip_count, seg_slots), 1)
        valid_seg = (seg_index < seg_counts[:, None]).astype(f32)
        pair_seg = valid_seg * jnp.concatenate(
            [valid_seg[:, 1:], jnp.zeros((clip_count, 1), f32)], axis=1
        )
        valid = valid_seg.reshape(1, 1, slots, 1)
        pair = pair_seg.reshape(1, 1, slots, 1)
        count_float = seg_counts.astype(f32)
        local_count = jnp.sum(count_float) * pixels

        taps = jnp.pad(stem_weight.reshape(stem_rows, GRID, GRID, -1), ((0, 0), (0, 0), (3, 3), (0, 0)))
        taps = jnp.stack([taps[:, :, 6 - x : 13 - x] for x in range(GRID)]).reshape(GRID * stem_rows, stem_depth)
        taps = jnp.pad(taps, ((0, -taps.shape[0] % 16), (0, -stem_depth % (LANES * reps))))
        moving = frames.astype(f32)
        motion = (moving[:, :, 1:] - moving[:, :, :-1]) * valid_seg[:, :, None, None, None]
        motion = jnp.transpose(motion.astype(bf16), (4, 0, 1, 2, 3)).reshape(GRID, GRID, slots, -1)
        strips = jnp.transpose(motion, (0, 2, 1, 3)).reshape(GRID, slots, -1)
        strips = jnp.pad(strips, ((3, 3), (0, 0), (0, 0)))
        strips = jnp.concatenate([strips[dy : dy + GRID] for dy in range(GRID)], axis=-1).reshape(GRID * slots, -1)
        strips = jnp.pad(strips, ((0, 0), (0, -stem_depth % (LANES * reps))))
        lanes = lambda column: jnp.broadcast_to(column.reshape(-1, 1), (column.size, LANES))
        (lateral_full, vectors, reduce_full, diff_full, mid_full, expand_full, block_in, block_low, stem_normed, pool_low,
         stem_inverse, number, normed_one, inverse_one, act_one, change) = head(
            taps, reduce_weight, diff_weight, mid_weight, expand_weight, lateral, jnp.stack([gain_three, shift_three]),
            jnp.stack([gain_one, shift_one, gate_shift, gain_two, shift_two]), jnp.stack([stem_gain, stem_shift]),
            strips, lanes(valid_seg), lanes(pair_seg), lanes(local_count), jnp.transpose(features, (0, 2, 1, 3)),
            fsdp, reps, 1,
        )
        row = vectors[2:].reshape(-1)
        gain_one_full, shift_one_full, gate_full, gain_two_full, shift_two_full = (
            row[n * mid_width : (n + 1) * mid_width] for n in range(5)
        )
        gain_three_full, shift_three_full = vectors[0], vectors[1]
        start = 5 * mid_width
        stem_gain_full = row[start : start + stem_width]
        start += -(-stem_width // LANES) * LANES
        stem_shift_full = row[start : start + stem_width]
        reduce_full = reduce_full.reshape(-1, mid_width)
        diff_full = diff_full.reshape(2, -1, mid_width)
        mid_full = mid_full.reshape(-1, mid_width)
        expand_full = expand_full.reshape(mid_width, -1)
        cube = (GRID, GRID, slots, -1)
        flat = (GRID, GRID * slots, -1)
        normed_one, act_one, change = normed_one.reshape(cube), act_one.reshape(cube), change.reshape(cube)
        stats_one = (None, inverse_one[0], number[0, 0])
        stem_stats = (None, stem_inverse[0], number[0, 0])
        zeta_one = valid * (gain_one_full * normed_one + shift_one_full)
        stem_norm = valid * (stem_gain_full * stem_normed + stem_shift_full)

        def norm_back(grad_out, normed, stats, gain, collective_id, name):
            masked = grad_out * valid
            shift_sum, gain_sum = exchange(
                [jnp.sum(masked, axis=(0, 1, 2)), jnp.sum(masked * normed, axis=(0, 1, 2))],
                fsdp, reps, False, collective_id, name,
            )
            grad_in = valid * stats[1] * gain * (masked - shift_sum / stats[2] - normed * gain_sum / stats[2])
            return grad_in.astype(bf16), gain_sum, shift_sum

        def earlier_of(values):
            grid = values.reshape(GRID, GRID, clip_count, seg_slots, -1)
            return jnp.pad(grid[:, :, :, :-1], ((0, 0), (0, 0), (0, 0), (1, 0), (0, 0))).reshape(values.shape)

        gate_pre = convolve(change, diff_full[0], 1, 1) + convolve(change, diff_full[1], 1, 2)
        gate = jax.nn.sigmoid(gate_pre + gate_full)
        modulated = (act_one * (1.0 + gate)).astype(bf16)
        middle = convolve(modulated, mid_full, 1, 1)
        (pooled, grad_pre, grad_expanded, act_two, grad_middle, gain_three_sum, shift_three_sum, gain_two_sum,
         shift_two_sum) = tail(
            middle.reshape(flat), expand_full, lanes(valid_seg), lanes(valid_seg / count_float[:, None]), lanes(local_count),
            gain_two_full[None], shift_two_full[None], gain_three_full[None], shift_three_full[None],
            pooled_grad.astype(f32)[:, :, None], block_in, clip_count, fsdp, reps, 4,
        )
        pooled = pooled.reshape(pooled_grad.shape).astype(bf16)
        gain_three_sum, shift_three_sum, gain_two_sum, shift_two_sum = (
            row[0] for row in (gain_three_sum, shift_three_sum, gain_two_sum, shift_two_sum)
        )
        grad_pre, grad_expanded, act_two, grad_middle = (
            block.reshape(cube) for block in (grad_pre, grad_expanded, act_two, grad_middle)
        )
        grad_modulated = convolve_back(grad_middle, mid_full, 1, 1)
        grad_gate_pre = grad_modulated * act_one * gate * (1.0 - gate)
        gate_terms = jnp.sum(grad_gate_pre, axis=(0, 1, 2))
        grad_gate = grad_gate_pre.astype(bf16)
        grad_change = convolve_back(grad_gate, diff_full[0], 1, 1) + convolve_back(grad_gate, diff_full[1], 1, 2)
        grad_change = grad_change * pair
        grad_act_one = grad_modulated * (1.0 + gate) + earlier_of(grad_change) - grad_change
        grad_reduced, gain_one_sum, shift_one_sum = norm_back(
            gelu_back(zeta_one, grad_act_one), normed_one, stats_one, gain_one_full, 8, "sums_one"
        )
        features_grad, lateral_terms, grad_act = back(
            grad_reduced.reshape(flat), reduce_full, pool_low.reshape(flat), lateral_full, grad_pre.reshape(flat), clip_count
        )
        grad_act = pool_mean(grad_act.reshape(cube))
        grad_stem, stem_gain_sum, stem_shift_sum = norm_back(
            gelu_back(stem_norm, grad_act), stem_normed, stem_stats, stem_gain_full, 9, "sums_stem"
        )
        stem_terms = convolve_terms(motion, grad_stem, 3, 1, bf16)
        stem_terms = jnp.transpose(stem_terms, (3, 0, 1, 2)).reshape(fsdp, stem_rows, stem_depth)
        gate_rows = gate_shift.shape[0]
        small_terms = jnp.concatenate(
            [
                lateral_terms.reshape(fsdp, stem_rows, feature_width),
                jnp.pad(stem_terms, ((0, 0), (0, 0), (0, feature_width - stem_depth))),
                jnp.pad(
                    gate_terms.astype(bf16).reshape(fsdp, 1, gate_rows),
                    ((0, 0), (0, 15 - 2 * stem_rows), (0, feature_width - gate_rows)),
                ),
            ],
            axis=1,
        )

        conv_rows = mid_weight.shape[0]
        if conv_rows % 32 == 0:
            small_part, reduce_part, expand_part, mid_part, diff_one, diff_two = terms_all(
                small_terms.reshape(-1, feature_width), block_low, grad_reduced.reshape(flat),
                act_two.reshape(flat), grad_expanded.reshape(flat), modulated, grad_middle.reshape(flat), change,
                grad_gate.reshape(flat),
                [small_terms.shape[1], reduce_weight.shape[0], expand_weight.shape[0], conv_rows], fsdp, reps, 10,
            )
        else:
            def owned(terms, shard):
                return terms.reshape((fsdp,) + shard.shape[-2:])

            small_part, reduce_part, expand_part, mid_part, diff_one, diff_two = scatter_all(
                [
                    small_terms,
                    owned(project_terms(block_low.reshape(cube), grad_reduced, bf16), reduce_weight),
                    owned(project_terms(act_two, grad_expanded, bf16), expand_weight),
                    owned(convolve_terms(modulated, grad_middle, 1, 1, bf16), mid_weight),
                    owned(convolve_terms(change, grad_gate, 1, 1, bf16), diff_weight),
                    owned(convolve_terms(change, grad_gate, 1, 2, bf16), diff_weight),
                ],
                fsdp, reps, 11, "scatter_terms",
            )

        def own_share(whole):
            share = whole.shape[0] // fsdp
            return lax.dynamic_slice_in_dim(whole, lax.axis_index("fsdp") * share, share)

        out = jnp.transpose(features_grad, (0, 2, 1, 3))
        return (
            pooled,
            out,
            small_part[stem_rows : 2 * stem_rows, :stem_depth],
            own_share(stem_gain_sum),
            own_share(stem_shift_sum),
            small_part[:stem_rows],
            reduce_part,
            own_share(gain_one_sum),
            own_share(shift_one_sum),
            jnp.stack([diff_one, diff_two]),
            small_part[2 * stem_rows, :gate_rows],
            mid_part,
            own_share(gain_two_sum),
            own_share(shift_two_sum),
            expand_part,
            own_share(gain_three_sum),
            own_share(shift_three_sum),
        )

    return shards


def solution(mesh):
    whole = ("fsdp", "rep")
    matrix, vector = P("fsdp", None), P("fsdp")
    in_specs = (
        P(whole, None, None, None, None), P(whole, None, None, None), P(whole),
        matrix, vector, vector, matrix, matrix, vector, vector, P(None, "fsdp", None), vector,
        matrix, vector, vector, matrix, vector, vector, P(whole, None, None),
    )
    out_specs = (
        P(whole, None, None), P(whole, None, None, None), matrix, vector, vector, matrix, matrix,
        vector, vector, P(None, "fsdp", None), vector, matrix, vector, vector, matrix, vector, vector,
    )
    body = make_shards(mesh.shape["fsdp"], mesh.shape["rep"])
    return jax.shard_map(body, mesh=mesh, in_specs=in_specs, out_specs=out_specs, check_vma=False)
```

```python
import functools

import jax
import jax.numpy as jnp
from jax import lax
from jax.experimental import pallas as pl
from jax.experimental.pallas import tpu as pltpu
from jax.sharding import PartitionSpec as P

GRID = 7
LANES = 128
PIXELS = GRID * GRID
epsilon = 1e-05
MESH = pl.DeviceIdType.MESH
ANY = pl.BlockSpec(memory_space=pl.ANY)
IN_VMEM = pl.BlockSpec(memory_space=pltpu.VMEM)
VMEM_LIMIT = 60 * 1024 * 1024
bf16 = jnp.bfloat16
f32 = jnp.float32
DMA = pltpu.SemaphoreType.DMA


def factor_three(size):
    best = None
    for b in range(1, size + 1):
        for c in range(1, b + 1):
            if size % (b * c) == 0 and size // (b * c) >= b:
                a = size // (b * c)
                if best is None or a + b + c < sum(best):
                    best = (a, b, c)
    return best


class Place:
    def __init__(self, dims, reps, rep=None):
        self.dims, self.reps = dims, reps
        size_a, size_b, size_c = dims
        self.me = lax.axis_index("fsdp")
        self.rep = lax.axis_index("rep") if rep is None else rep
        ib, ic = (self.me // size_c) % size_b, self.me % size_c
        self.ia = self.me // (size_b * size_c)
        odd = self.rep % 2 if size_b == size_c else 0
        self.stride_u = size_c * (1 - odd) + odd
        self.stride_v = (1 - odd) + size_c * odd
        self.iu = ib * (1 - odd) + ic * odd
        self.iv = ic * (1 - odd) + ib * odd

    def at(self, da, du, dv):
        size_a, size_b, size_c = self.dims
        a = (self.ia + da + size_a) % size_a
        u = (self.iu + du + size_b) % size_b
        v = (self.iv + dv + size_c) % size_c
        return a * (size_b * size_c) + u * self.stride_u + v * self.stride_v

    def greet(self, more=()):
        size_a, size_b, size_c = self.dims
        peers = [(self.at(d, 0, 0), self.rep) for d in range(1, size_a)]
        peers += [(self.at(0, d, 0), self.rep) for d in range(1, size_b)]
        peers += [(self.at(0, 0, d), self.rep) for d in range(1, size_c)]
        peers += [(self.me, (self.rep + d) % self.reps) for d in range(1, self.reps)]
        greet(peers + list(more))


def greet(peers):
    barrier = pltpu.get_barrier_semaphore()
    for target, rep in peers:
        pl.semaphore_signal(
            barrier, inc=1, device_id={"fsdp": target, "rep": rep}, device_id_type=MESH
        )
    pl.semaphore_wait(barrier, len(peers))


def remote(src, dst, sems, target, rep):
    return pltpu.make_async_remote_copy(
        src_ref=src,
        dst_ref=dst,
        send_sem=sems.at[0],
        recv_sem=sems.at[1],
        device_id={"fsdp": target, "rep": rep},
        device_id_type=MESH,
    )


def columns(width, which):
    start = which * width
    return pl.ds(start if isinstance(start, int) else pl.multiple_of(start, width), width)


def views(refs):
    out = []
    for ref, stacked in refs:
        out += [ref.at[j] for j in range(ref.shape[0])] if stacked else [ref]
    return out


def scatter_kernel(dims, reps, stacked, *refs):
    number = len(stacked)
    partials = views(zip(refs[:number], stacked))
    totals = views(zip(refs[number : 2 * number], stacked))
    count = len(partials)
    rest = refs[2 * number :]
    held, from_rep, from_v, from_u, from_a, share = (rest[i * count : (i + 1) * count] for i in range(6))
    own_sem, r_sem, v_sem, u_sem, a_sem, s_sem = rest[6 * count :]
    size_a, size_b, size_c = dims
    place = Place(dims, reps)
    me, rep = place.me, place.rep
    place.greet()
    waits = []

    def push(source, there, sems, target, target_rep):
        copy = remote(source, there, sems, target, target_rep)
        copy.start()
        waits.append(copy)

    def landed(there, sems):
        remote(there, there, sems, me, rep).wait_recv()

    def order():
        for dv in list(range(1, size_c)) + [0]:
            for du in list(range(1, size_b)) + [0]:
                for da in list(range(1, size_a)) + [0]:
                    yield da, du, dv

    local = {}
    for k in range(count):
        width = partials[k].shape[-1] // reps
        for da, du, dv in order():
            for d in range(1, reps):
                other = (rep + d) % reps
                index = Place(dims, reps, other).at(da, du, dv)
                push(
                    partials[k].at[index, :, columns(width, other)],
                    from_rep[k].at[d - 1, index],
                    r_sem.at[k, da, du, dv, d - 1],
                    me,
                    other,
                )
            index = place.at(da, du, dv)
            copy = pltpu.make_async_copy(
                partials[k].at[index, :, columns(width, rep)],
                held[k].at[index],
                own_sem.at[k, da, du, dv],
            )
            copy.start()
            local[k, da, du, dv] = copy

    def handle(k, da, du, dv):
        index = place.at(da, du, dv)
        local[k, da, du, dv].wait()
        total = held[k][index].astype(f32)
        for d in range(1, reps):
            landed(from_rep[k].at[d - 1, index], r_sem.at[k, da, du, dv, d - 1])
            total = total + from_rep[k][d - 1, index].astype(f32)
        if dv == 0:
            for e in range(1, size_c):
                landed(from_v[k].at[e - 1, da, du], v_sem.at[k, da, du, e - 1])
                total = total + from_v[k][e - 1, da, du].astype(f32)
            if du == 0:
                for e in range(1, size_b):
                    landed(from_u[k].at[e - 1, da], u_sem.at[k, da, e - 1])
                    total = total + from_u[k][e - 1, da].astype(f32)
                if da == 0:
                    for e in range(1, size_a):
                        landed(from_a[k].at[e - 1], a_sem.at[k, e - 1])
                        total = total + from_a[k][e - 1].astype(f32)
        if (da, du, dv) == (0, 0, 0):
            share[k][rep] = total.astype(bf16)
            for d in range(1, reps):
                push(share[k].at[rep], share[k].at[rep], s_sem.at[k, d - 1], me, (rep + d) % reps)
            return
        held[k][index] = total.astype(bf16)
        if dv:
            push(held[k].at[index], from_v[k].at[dv - 1, da, du], v_sem.at[k, da, du, dv - 1], place.at(0, 0, dv), rep)
        elif du:
            push(held[k].at[index], from_u[k].at[du - 1, da], u_sem.at[k, da, du - 1], place.at(0, du, 0), rep)
        else:
            push(held[k].at[index], from_a[k].at[da - 1], a_sem.at[k, da - 1], place.at(da, 0, 0), rep)

    for step in range(count + 3):
        for lag in range(4):
            k = step - lag
            for da, du, dv in order() if 0 <= k < count else ():
                if lag == (0 if dv else 1 if du else 2 if da else 3):
                    handle(k, da, du, dv)
    for k in range(count):
        width = partials[k].shape[-1] // reps
        for d in range(1, reps):
            landed(share[k].at[(rep + reps - d) % reps], s_sem.at[k, d - 1])
        for which in range(reps):
            totals[k][:, which * width : (which + 1) * width] = share[k][which].astype(f32)
    for copy in waits:
        copy.wait_send()


def scatter_all(partials, fsdp, reps, collective_id, name):
    dims = factor_three(fsdp)
    size_a, size_b, size_c = dims
    stacked = [p.ndim == 4 for p in partials]
    shapes = []
    for p in partials:
        shapes += [(p.shape[-2], p.shape[-1] // reps)] * (p.shape[0] if p.ndim == 4 else 1)
    count = len(shapes)

    def buffers(*lead):
        return [pltpu.VMEM(lead + shape, bf16) for shape in shapes]

    return pl.pallas_call(
        functools.partial(scatter_kernel, dims, reps, stacked),
        out_shape=[
            jax.ShapeDtypeStruct(p.shape[:-3] + p.shape[-2:], f32) for p in partials
        ],
        in_specs=[ANY] * len(partials),
        out_specs=[IN_VMEM] * len(partials),
        scratch_shapes=buffers(fsdp)
        + buffers(max(reps - 1, 1), fsdp)
        + buffers(max(size_c - 1, 1), size_a, size_b)
        + buffers(max(size_b - 1, 1), size_a)
        + buffers(max(size_a - 1, 1))
        + buffers(reps)
        + [
            DMA((count, size_a, size_b, size_c)),
            DMA((count, size_a, size_b, size_c, max(reps - 1, 1), 2)),
            DMA((count, size_a, size_b, max(size_c - 1, 1), 2)),
            DMA((count, size_a, max(size_b - 1, 1), 2)),
            DMA((count, max(size_a - 1, 1), 2)),
            DMA((count, max(reps - 1, 1), 2)),
        ],
        compiler_params=pltpu.CompilerParams(
            collective_id=collective_id, has_side_effects=True, vmem_limit_bytes=VMEM_LIMIT
        ),
        name=name,
    )(*partials)


def stage_sizes(devices):
    sizes = []
    while devices > 1:
        size = next(s for s in (8, 4, 2, 7, 5, 3, devices) if devices % s == 0)
        sizes.append(size)
        devices //= size
    return sizes


class Exchange:
    def __init__(self, sizes, reps, buffers):
        self.sizes, self.reps = sizes, reps
        self.mine, self.slots, self.sems = buffers[0], buffers[1:-1], buffers[-1]
        place = lax.axis_index("fsdp") * reps + lax.axis_index("rep")
        self.stages = []
        stride = 1
        for size in sizes:
            position = (place // stride) % size
            peers = []
            for d in range(1, size):
                target = place + ((position + d) % size - position) * stride
                peers.append((target // reps, target % reps))
            self.stages.append((size, position, peers))
            stride *= size
        self.peers = [peer for stage in self.stages for peer in stage[2]]
        self.waits = []

    def total(self, round, current, moments):
        number = len(current)
        spans, start = [], 0
        for value in current:
            spans.append((start, value.shape[1]))
            start += value.shape[1]
        for index, (size, position, peers) in enumerate(self.stages):
            used = pl.ds(0, sum(length for _, length in spans))
            mine = self.mine.at[round, index, :, used]
            slots = self.slots[index].at[round, :, :, used]
            for (start, length), value in zip(spans, current):
                mine[:, start : start + length] = value
            for d, (target, rep) in enumerate(peers, 1):
                copy = remote(mine, slots.at[position], self.sems.at[round, index, d - 1], target, rep)
                copy.start()
                self.waits.append(copy)
            slots[position] = mine[...]
            for d, (target, rep) in enumerate(peers, 1):
                there = slots.at[(position + size - d) % size]
                remote(there, there, self.sems.at[round, index, d - 1], target, rep).wait_recv()
            parts = [
                [slots[j, :, start : start + length] for start, length in spans] for j in range(size)
            ]
            current = [functools.reduce(jnp.add, [part[row] for part in parts]) for row in range(number)]
            if moments:
                centre = current[0] / current[2][:, :1]
                squares = current[1]
                for part in parts:
                    count = part[2][:, :1]
                    off = part[0] / count - centre
                    squares = squares + count * off * off
                current[1] = squares
        return current

    def finish(self):
        for copy in self.waits:
            copy.wait_send()


def exchange_buffers(sizes, rounds, total):
    return (
        [pltpu.VMEM((rounds, len(sizes), 1, total), f32)]
        + [pltpu.VMEM((rounds, size, 1, total), f32) for size in sizes]
        + [DMA((rounds, len(sizes), max(max(sizes) - 1, 1), 2))]
    )


def exchange_kernel(sizes, reps, moments, *refs):
    number = 3 if moments else 2
    sources, results = refs[:number], refs[number : 2 * number]
    over = Exchange(sizes, reps, refs[2 * number :])
    greet(over.peers)
    current = over.total(0, [source[...] for source in sources], moments)
    for result, value in zip(results, current):
        result[...] = value
    over.finish()


def exchange(rows, fsdp, reps, moments, collective_id, name):
    sizes = stage_sizes(fsdp * reps)
    width = rows[0].shape[-1]
    padded = -(-width // LANES) * LANES
    rows = [jnp.pad(row.reshape(1, -1), ((0, 0), (0, padded - width))) for row in rows[:2]] + [
        jnp.broadcast_to(row.reshape(1, 1), (1, LANES)) for row in rows[2:]
    ]
    results = pl.pallas_call(
        functools.partial(exchange_kernel, sizes, reps, moments),
        out_shape=[jax.ShapeDtypeStruct(row.shape, f32) for row in rows],
        in_specs=[IN_VMEM] * len(rows),
        out_specs=[IN_VMEM] * len(rows),
        scratch_shapes=exchange_buffers(sizes, 1, sum(row.shape[1] for row in rows)),
        compiler_params=pltpu.CompilerParams(
            collective_id=collective_id, has_side_effects=True, vmem_limit_bytes=4 * 1024 * 1024
        ),
        name=name,
    )(*rows)
    return [result[0, :width] for result in results[:2]] + [result[0, 0] for result in results[2:]]


TANH_SCALE = 0.7978845608028654
CUBIC = 0.044715


def gelu_parts(x):
    square = x * x
    bend = jnp.tanh(TANH_SCALE * x * (1.0 + CUBIC * square))
    half = 0.5 * (1.0 + bend)
    slope = half + 0.5 * x * (1.0 - bend * bend) * (TANH_SCALE * (1.0 + 3.0 * CUBIC * square))
    return x * half, slope


def fold_rows(values):
    groups, slots, width = values.shape
    return jnp.sum(values.reshape(groups * slots // 8, 8, width), axis=0)


def whole_row(values):
    return jnp.sum(values, axis=0, keepdims=True)


def dot(left, right):
    return jnp.dot(left, right, preferred_element_type=f32)


def dot_t(left, right):
    return lax.dot_general(left, right, (((1,), (1,)), ((), ())), preferred_element_type=f32)


class Scatter:
    def __init__(self, dims, reps, terms, rows, buffers):
        count = len(terms)
        self.dims, self.reps, self.terms, self.rows = dims, reps, terms, rows
        self.from_rep, self.from_v, self.from_u, self.from_a, self.share = (
            buffers[i * count : (i + 1) * count] for i in range(5)
        )
        self.r_sem, self.v_sem, self.u_sem, self.a_sem, self.s_sem = buffers[5 * count :]
        self.place = Place(dims, reps)
        self.waits = []

    def push(self, source, there, sems, target, target_rep):
        copy = remote(source, there, sems, target, target_rep)
        copy.start()
        self.waits.append(copy)

    def landed(self, there, sems):
        remote(there, there, sems, self.place.me, self.place.rep).wait_recv()

    def part(self, k, index, which):
        rows = self.rows[k]
        start = pl.multiple_of(index * rows, rows)
        return self.terms[k].at[pl.ds(start, rows), columns(self.terms[k].shape[1] // self.reps, which)]

    def order(self):
        size_a, size_b, size_c = self.dims
        for dv in list(range(1, size_c)) + [0]:
            for du in list(range(1, size_b)) + [0]:
                for da in list(range(1, size_a)) + [0]:
                    yield da, du, dv

    def cores(self, k):
        rep, reps = self.place.rep, self.reps
        for d in range(1, reps):
            other = (rep + d) % reps
            source = self.terms[k].at[:, columns(self.terms[k].shape[1] // reps, other)]
            self.push(source, self.from_rep[k].at[d - 1], self.r_sem.at[k, d - 1], self.place.me, other)

    def hop(self, k, lag):
        if lag == 0:
            for d in range(1, self.reps):
                self.landed(self.from_rep[k].at[d - 1], self.r_sem.at[k, d - 1])
        if 0 <= k < len(self.terms):
            for da, du, dv in self.order():
                if lag == (0 if dv else 1 if du else 2 if da else 3):
                    self.handle(k, da, du, dv)

    def handle(self, k, da, du, dv):
        size_a, size_b, size_c = self.dims
        place, reps, rep = self.place, self.reps, self.place.rep
        index = place.at(da, du, dv)
        mine = self.part(k, index, rep)
        rows = self.rows[k]
        span = pl.ds(pl.multiple_of(index * rows, rows), rows)
        if dv and reps == 2:
            total = mine[...] + self.from_rep[k][0, span]
        else:
            total = mine[...].astype(f32)
            for d in range(1, reps):
                total = total + self.from_rep[k][d - 1, span].astype(f32)
        if dv == 0:
            for e in range(1, size_c):
                self.landed(self.from_v[k].at[e - 1, da, du], self.v_sem.at[k, da, du, e - 1])
                total = total + self.from_v[k][e - 1, da, du].astype(f32)
            if du == 0:
                for e in range(1, size_b):
                    self.landed(self.from_u[k].at[e - 1, da], self.u_sem.at[k, da, e - 1])
                    total = total + self.from_u[k][e - 1, da].astype(f32)
                if da == 0:
                    for e in range(1, size_a):
                        self.landed(self.from_a[k].at[e - 1], self.a_sem.at[k, e - 1])
                        total = total + self.from_a[k][e - 1].astype(f32)
        if (da, du, dv) == (0, 0, 0):
            self.share[k][rep] = total.astype(bf16)
            for d in range(1, reps):
                self.push(self.share[k].at[rep], self.share[k].at[rep], self.s_sem.at[k, d - 1], place.me, (rep + d) % reps)
            return
        mine[...] = total.astype(bf16)
        if dv:
            self.push(mine, self.from_v[k].at[dv - 1, da, du], self.v_sem.at[k, da, du, dv - 1], place.at(0, 0, dv), rep)
        elif du:
            self.push(mine, self.from_u[k].at[du - 1, da], self.u_sem.at[k, da, du - 1], place.at(0, du, 0), rep)
        else:
            self.push(mine, self.from_a[k].at[da - 1], self.a_sem.at[k, da - 1], place.at(da, 0, 0), rep)

    def finish(self, totals):
        for k, total in enumerate(totals):
            width = self.terms[k].shape[1] // self.reps
            for d in range(1, self.reps):
                self.landed(self.share[k].at[(self.place.rep + self.reps - d) % self.reps], self.s_sem.at[k, d - 1])
            for which in range(self.reps):
                start = which * width
                for ref, row in total if isinstance(total, list) else [(total, 0)]:
                    height, length = ref.shape[0], min(ref.shape[1] - start, width)
                    if length > 0:
                        ref[:, start : start + length] = self.share[k][which, row : row + height, :length].astype(f32)
        for copy in self.waits:
            copy.wait_send()


def scatter_buffers(dims, reps, shapes):
    size_a, size_b, size_c = dims
    count = len(shapes)
    others = max(reps - 1, 1)

    def buffers(*lead):
        return [pltpu.VMEM(lead + (rows, width // reps), bf16) for rows, width in shapes]

    return (
        [pltpu.VMEM((others, size_a * size_b * size_c * rows, width // reps), bf16) for rows, width in shapes]
        + buffers(max(size_c - 1, 1), size_a, size_b)
        + buffers(max(size_b - 1, 1), size_a)
        + buffers(max(size_a - 1, 1))
        + buffers(reps)
        + [
            DMA((count, others, 2)),
            DMA((count, size_a, size_b, max(size_c - 1, 1), 2)),
            DMA((count, size_a, max(size_b - 1, 1), 2)),
            DMA((count, max(size_a - 1, 1), 2)),
            DMA((count, others, 2)),
        ]
    )


def terms_kernel(dims, reps, rows, *refs):
    (small, block_low, grad_reduced, act_two, grad_expanded, modulated, grad_middle, change, grad_gate) = refs[:9]
    lateral_total, stem_total, gate_total, reduce_total, expand_total, mid_total, diff_total = refs[9:16]
    stem_rows = stem_total.shape[0]
    totals = [
        [(lateral_total, 0), (stem_total, stem_rows), (gate_total, 2 * stem_rows)],
        reduce_total, expand_total, mid_total, diff_total.at[0], diff_total.at[1],
    ]
    terms = refs[16:22]
    pads, line, turned, chunk, pad_sem, line_sem, chunk_sem, small_sem = refs[22:30]
    scatter = Scatter(dims, reps, terms, rows, refs[30:])
    slots, mid_width = modulated.shape[2:]
    lines = block_low.shape[0]
    width = block_low.shape[2]
    step = chunk.shape[-1]
    chunks = width // step
    ring = 2

    place = scatter.place
    small_copy = pltpu.make_async_copy(small, terms[0], small_sem)
    small_copy.start()
    sources = [(block_low, j) for j in range(chunks)] + [(grad_expanded, j) for j in range(chunks)]

    def load(number):
        source, j = sources[number]
        return pltpu.make_async_copy(
            source.at[:, :, j * step : (j + 1) * step], chunk.at[number % 2], chunk_sem.at[number % 2]
        )

    gradients = [grad_middle, grad_gate, grad_reduced, act_two]

    def turn(number):
        pltpu.make_async_copy(gradients[number], line, line_sem).wait()
        turned[...] = jnp.transpose(line[...].reshape(-1, mid_width))
        if number + 1 < len(gradients):
            pltpu.make_async_copy(gradients[number + 1], line, line_sem).start()

    load(0).start()
    pltpu.make_async_copy(gradients[0], line, line_sem).start()
    inner = pl.ds(ring, GRID)
    for index, source in enumerate((modulated, change)):
        for side in (slice(0, ring), slice(GRID + ring, GRID + 2 * ring)):
            pads[index, side] = jnp.zeros((ring, GRID + 2 * ring, slots, mid_width), bf16)
            pads[index, ring : GRID + ring, side] = jnp.zeros((GRID, ring, slots, mid_width), bf16)
        pltpu.make_async_copy(source, pads.at[index, inner, inner], pad_sem.at[index]).start()
    place.greet()

    def flow(*hops):
        for k, lag in hops:
            scatter.hop(k, lag)

    def piece(number):
        if number + 1 < len(sources):
            load(number + 1).start()
        load(number).wait()
        return dot(turned[...], chunk[number % 2].reshape(-1, step))

    def reduce_pieces(first, last):
        for j in range(first, last):
            terms[1][j * step : (j + 1) * step, :] = jnp.transpose(piece(j)).astype(bf16)

    def expand_pieces(first, last):
        for j in range(first, last):
            terms[2][:, j * step : (j + 1) * step] = piece(chunks + j).astype(bf16)

    def taps(k, pad, stride, first, last):
        def tap(t, _):
            top = ring + (t // 3 - 1) * stride
            left = ring + (t % 3 - 1) * stride
            source = pads[pad, pl.ds(top, GRID), pl.ds(left, GRID)].reshape(-1, mid_width)
            values = dot(turned[...], source)
            start = pl.multiple_of(t * mid_width, mid_width)
            terms[k][pl.ds(start, mid_width), :] = jnp.transpose(values).astype(bf16)
            return 0

        lax.fori_loop(first, last, tap, 0)

    def padded(pad):
        pltpu.make_async_copy((modulated, change)[pad], pads.at[pad, inner, inner], pad_sem.at[pad]).wait()

    half = chunks // 2
    small_copy.wait()
    scatter.cores(0)
    turn(0)
    padded(0)
    taps(3, 0, 1, 0, 3)
    flow((0, 0))
    taps(3, 0, 1, 3, 6)
    flow((0, 1))
    taps(3, 0, 1, 6, 9)
    scatter.cores(3)
    turn(1)
    padded(1)
    taps(4, 1, 1, 0, 3)
    flow((3, 0), (0, 2))
    taps(4, 1, 1, 3, 6)
    flow((0, 3))
    taps(4, 1, 1, 6, 9)
    scatter.cores(4)
    taps(5, 1, 2, 0, 3)
    flow((4, 0), (3, 1))
    taps(5, 1, 2, 3, 6)
    taps(5, 1, 2, 6, 9)
    scatter.cores(5)
    turn(2)
    flow((3, 2))
    reduce_pieces(0, half)
    flow((5, 0), (4, 1))
    reduce_pieces(half, chunks)
    scatter.cores(1)
    turn(3)
    expand_pieces(0, half)
    flow((1, 0), (4, 2), (3, 3))
    expand_pieces(half, chunks)
    scatter.cores(2)
    flow((5, 1), (2, 0), (1, 1), (5, 2), (4, 3), (2, 1), (1, 2), (5, 3), (2, 2), (1, 3), (2, 3))
    scatter.finish(totals)


def terms_all(small, block_low, grad_reduced, act_two, grad_expanded, modulated, grad_middle, change, grad_gate, rows, stem_rows, stem_depth, fsdp, reps, collective_id):
    dims = factor_three(fsdp)
    lines, line_rows, width = block_low.shape
    mid_width = act_two.shape[-1]
    slots = modulated.shape[2]
    shapes = [(rows[0], width), (rows[1], mid_width), (rows[2], width)] + [(rows[3], mid_width)] * 3
    rows = [rows[0], rows[1], rows[2], rows[3], rows[3], rows[3]]
    side = GRID + 4
    return pl.pallas_call(
        functools.partial(terms_kernel, dims, reps, rows),
        out_shape=[
            jax.ShapeDtypeStruct(shape, f32)
            for shape in [(stem_rows, width), (stem_rows, stem_depth), (1, mid_width // fsdp)] + shapes[1:4] + [(2,) + shapes[4]]
        ],
        in_specs=[ANY] * 9,
        out_specs=[IN_VMEM] * 7,
        scratch_shapes=[pltpu.VMEM((fsdp * a, b), bf16) for a, b in shapes]
        + [
            pltpu.VMEM((2, side, side, slots, mid_width), bf16),
            pltpu.VMEM((lines, line_rows, mid_width), bf16),
            pltpu.VMEM((mid_width, lines * line_rows), bf16),
            pltpu.VMEM((2, lines, line_rows, 256), bf16),
            DMA((2,)), DMA(()), DMA((2,)), DMA(()),
        ]
        + scatter_buffers(dims, reps, shapes),
        compiler_params=pltpu.CompilerParams(
            collective_id=collective_id, has_side_effects=True, vmem_limit_bytes=VMEM_LIMIT
        ),
        name="terms",
    )(small, block_low, grad_reduced, act_two, grad_expanded, modulated, grad_middle, change, grad_gate)


class Gather:
    def __init__(self, dims, reps, shards, fulls, buffers):
        self.dims, self.reps, self.shards, self.fulls = dims, reps, shards, fulls
        self.own_sem, self.a_sem, self.b_sem, self.c_sem, self.r_sem = buffers
        self.place = Place(dims, reps)
        self.waits, self.local = [], []

    def slot(self, k, da, du, dv, which):
        full = self.fulls[k]
        index = self.place.at(-(da or 0), -du, -dv)
        others = self.dims[1] * self.dims[2]
        cols = columns(full.shape[-1] // self.reps, which)
        if da is None:
            return full.at[:, index % others, :, cols]
        return full.at[index // others, index % others, :, cols]

    def push(self, k, da, du, dv, target, target_rep, sems):
        there = self.slot(k, da, du, dv, self.place.rep)
        if (da, du, dv) == (0, 0, 0):
            source = self.shards[k].at[:, columns(self.shards[k].shape[-1] // self.reps, self.place.rep)]
        else:
            source = there
        copy = remote(source, there, sems, target, target_rep)
        copy.start()
        self.waits.append(copy)

    def landed(self, k, da, du, dv, which, sems):
        there = self.slot(k, da, du, dv, which)
        remote(there, there, sems, self.place.me, self.place.rep).wait_recv()

    def along_u(self, k, da):
        for d in range(1, self.dims[1]):
            self.push(k, da, 0, 0, self.place.at(0, d, 0), self.place.rep, self.b_sem.at[k, da, d - 1])

    def along_v(self, k, da, du):
        for d in range(1, self.dims[2]):
            self.push(k, da, du, 0, self.place.at(0, 0, d), self.place.rep, self.c_sem.at[k, da or 0, du, d - 1])

    def to_reps(self, k, da, du, dv):
        for d in range(1, self.reps):
            self.push(
                k, da, du, dv, self.place.me, (self.place.rep + d) % self.reps, self.r_sem.at[k, da or 0, du, dv, d - 1]
            )

    def begin(self, k):
        place = self.place
        others = self.dims[1] * self.dims[2]
        copy = pltpu.make_async_copy(self.shards[k], self.fulls[k].at[place.me // others, place.me % others], self.own_sem.at[k])
        copy.start()
        self.local.append(copy)
        for d in range(1, self.dims[0]):
            self.push(k, 0, 0, 0, place.at(d, 0, 0), place.rep, self.a_sem.at[k, d - 1])
        self.along_u(k, 0)
        self.along_v(k, 0, 0)

    def hop(self, k, lag):
        size_a, size_b, size_c = self.dims
        reps, rep = self.reps, self.place.rep
        if lag == 0:
            for da in range(1, size_a):
                self.landed(k, da, 0, 0, rep, self.a_sem.at[k, da - 1])
                self.along_u(k, da)
                self.along_v(k, da, 0)
                self.to_reps(k, da, 0, 0)
        elif lag == 1:
            for du in range(1, size_b):
                for da in range(size_a):
                    self.landed(k, da, du, 0, rep, self.b_sem.at[k, da, du - 1])
                self.along_v(k, None, du)
                self.to_reps(k, None, du, 0)
        elif lag == 2:
            for dv in range(1, size_c):
                for du in range(size_b):
                    for da in range(size_a) if du == 0 else (None,):
                        self.landed(k, da, du, dv, rep, self.c_sem.at[k, da or 0, du, dv - 1])
                    self.to_reps(k, None, du, dv)
        else:
            for dv in range(size_c):
                for du in range(size_b):
                    for da in range(1, size_a) if du == dv == 0 else (None,):
                        for d in range(1, reps):
                            self.landed(k, da, du, dv, (rep + reps - d) % reps, self.r_sem.at[k, da or 0, du, dv, d - 1])
            self.local[k].wait()

    def finish(self):
        for copy in self.waits:
            copy.wait_send()


def gather_buffers(dims, reps, count):
    size_a, size_b, size_c = dims
    return [
        DMA((count,)),
        DMA((count, max(size_a - 1, 1), 2)),
        DMA((count, size_a, max(size_b - 1, 1), 2)),
        DMA((count, size_a, size_b, max(size_c - 1, 1), 2)),
        DMA((count, size_a, size_b, size_c, max(reps - 1, 1), 2)),
    ]


def head_kernel(dims, reps, sizes, stem_rows, *refs):
    stem_own, reduce_own, diff_own, mid_own, expand_own = refs[:5]
    lateral_own, wide_own, narrow_own, least_own, lhs, valid, pair, count, features = refs[5:14]
    (lateral_out, vector_out, reduce_out, diff_out, mid_out, expand_out, block_in, block_low, stem_normed, pool_low, stem_inverse,
     number_out, normed_one, inverse_one, act_one, change) = refs[14:30]
    (small_own, small, stem_taps, reduce_full, tap_rows, lateral, stem_values, stem_act, loaded, wide, low, reduced) = refs[30:42]
    load_sem, wide_sem, low_sem, out_sem = refs[42:46]
    gather = Gather(
        dims, reps, [small_own, stem_own, reduce_own, diff_own.at[0], diff_own.at[1], mid_own, expand_own],
        [small, stem_taps, reduce_full, diff_out.at[0], diff_out.at[1], mid_out, expand_out], refs[46:51],
    )
    over = Exchange(sizes, reps, refs[51:])
    others = small.shape[1]
    fsdp = small.shape[0] * others
    me = gather.place.me
    stem_width = stem_rows * fsdp
    lines, rows, mid_width = reduced.shape
    clips, pixels, segs, width = features.shape
    slots = valid.shape[0]
    groups = rows // slots
    step = 256
    chunks = width // step
    mask = valid[:, :1].reshape(1, slots, 1)
    pairs = pair[:, :1].reshape(1, slots, 1)
    own = count[:, :1]

    def load(j):
        cols = slice(j * step, (j + 1) * step)
        return [
            pltpu.make_async_copy(
                features.at[clip, :, :, cols], loaded.at[j % 2, :, clip * segs : (clip + 1) * segs, :], load_sem.at[j % 2, clip]
            )
            for clip in range(clips)
        ]

    def grouped(values):
        return values.reshape(groups, slots, values.shape[-1])

    def moments(carry, origin):
        away, squares = whole_row(carry[0]), whole_row(carry[1])
        return [away + own * origin, jnp.maximum(squares - away * away / own, 0.0), count[...]]

    def add_moments(carry, values, origin):
        off = (grouped(values) - origin.reshape(1, 1, -1)) * mask
        return carry[0] + fold_rows(off), carry[1] + fold_rows(off * off)

    def blank(n):
        return jnp.zeros((8, n), f32), jnp.zeros((8, n), f32)

    for copy in load(0):
        copy.start()

    def placed(values, length):
        share = values.shape[1]
        one = lax.broadcasted_iota(jnp.int32, (share, length), 1) - me * share
        hot = (one == lax.broadcasted_iota(jnp.int32, (share, length), 0)).astype(f32).astype(bf16)
        return dot(values, hot)

    least = placed(least_own[...], LANES * -(-stem_width // LANES))
    narrow = placed(narrow_own[...], mid_width)
    pieces = [narrow[n : n + 1] for n in range(narrow.shape[0])] + [least[n : n + 1] for n in range(least.shape[0])]
    joined = jnp.concatenate(pieces, axis=1)
    joined = jnp.concatenate([joined, jnp.zeros((1, -joined.shape[1] % width), f32)], axis=1)
    small_rows = [lateral_own[...].astype(f32), placed(wide_own[...], width)]
    small_rows += [joined[:, n * width : (n + 1) * width] for n in range(joined.shape[1] // width)]
    taken = sum(row.shape[0] for row in small_rows)
    small_rows.append(jnp.zeros((small_own.shape[0] - taken, width), f32))
    small_own[...] = jnp.concatenate(small_rows, axis=0).astype(bf16)
    gather.place.greet(over.peers)
    gather.begin(0)
    gather.begin(1)
    gather.begin(2)
    gather.begin(3)
    gather.begin(4)
    gather.begin(5)
    gather.begin(6)
    stem_act[...] = jnp.zeros(stem_act.shape, f32)
    gather.hop(0, 0)
    gather.hop(1, 0)
    gather.hop(0, 1)
    gather.hop(1, 1)
    gather.hop(0, 2)
    gather.hop(1, 2)
    gather.hop(0, 3)
    gather.hop(1, 3)
    vectors = jnp.zeros((taken - stem_rows, width), f32)
    for device in range(fsdp):
        values = small[device // others, device % others].astype(f32)
        span = slice(device * stem_rows, (device + 1) * stem_rows)
        lateral[span, :] = values[:stem_rows]
        vectors = vectors + values[stem_rows:taken]
        taps = stem_taps[device // others, device % others].astype(f32)
        for x in range(GRID):
            tap_rows[x, span, :] = taps[x * stem_rows : (x + 1) * stem_rows]
    lateral_low = lateral[...].astype(bf16)
    vector_out[...] = vectors
    lateral_out[...] = lateral_low

    def vector(position, length):
        row, start = 2 + position // width, position % width
        return vectors[row : row + 1, start : start + length]

    gain_one, shift_one = vector(0, mid_width), vector(mid_width, mid_width)
    start = mid_width * narrow.shape[0]
    stem_gain, stem_shift = vector(start, stem_width), vector(start + least.shape[1], stem_width)
    gather.hop(2, 0)
    gather.hop(3, 0)
    gather.hop(2, 1)

    def stem_column(x, _):
        stem_values[x] = dot_t(lhs[...], tap_rows[x].astype(bf16))
        return 0

    lax.fori_loop(0, GRID, stem_column, 0)
    origin = stem_values[0, 0:1, :]
    carry = lax.fori_loop(0, GRID, lambda x, c: add_moments(c, stem_values[x], origin), blank(stem_width))
    gather.hop(4, 0)
    gather.hop(3, 1)
    total, squares, number = over.total(0, moments(carry, origin), True)
    number_out[...] = number
    number = number[:, :1]
    centre, inverse = total / number, lax.rsqrt(squares / number + epsilon)
    stem_inverse[...] = inverse
    gather.hop(5, 0)
    gather.hop(2, 2)
    gather.hop(4, 1)

    def stem_norm(x, _):
        normed = (stem_values[x] - centre) * inverse
        stem_normed[:, x] = grouped(normed)
        zeta = mask * (grouped(normed) * stem_gain.reshape(1, 1, -1) + stem_shift.reshape(1, 1, -1))
        stem_act[x + 1, 1 : GRID + 1] = gelu_parts(zeta)[0]
        return 0

    lax.fori_loop(0, GRID, stem_norm, 0)

    def stem_pool(x, _):
        total = stem_act[x] + stem_act[x + 1] + stem_act[x + 2]
        total = total[0:GRID] + total[1 : GRID + 1] + total[2 : GRID + 2]
        pool_low[:, x] = (total / 9.0).astype(bf16)
        return 0

    lax.fori_loop(0, GRID, stem_pool, 0)
    gather.hop(2, 3)

    later = [[], [(6, 0)], [(5, 1)], [], [(6, 1)], [(3, 2)], [], [(4, 2)]]
    for j in range(chunks):
        slot = j % 2
        cols = slice(j * step, (j + 1) * step)
        for copy in load(j + 1) if j + 1 < chunks else ():
            copy.start()
        for copy in load(j):
            copy.wait()
        out_wide = pltpu.make_async_copy(wide.at[slot], block_in.at[:, :, cols], wide_sem.at[slot])
        out_low = pltpu.make_async_copy(low.at[slot], block_low.at[:, :, cols], low_sem.at[slot])

        if j >= 2:
            out_wide.wait()
            out_low.wait()
        shares = step // reduce_full.shape[2]
        start = j * shares % others
        weight = reduce_full[j * shares // others, start : start + shares].reshape(step, mid_width)

        def line(y, _):
            values = loaded[slot, pl.ds(y * groups, groups)].astype(f32).reshape(rows, step)
            values = values + dot(pool_low[y].reshape(rows, stem_width), lateral_low[:, cols])
            wide[slot, y] = values
            rounded = values.astype(bf16)
            low[slot, y] = rounded
            product = dot(rounded, weight)
            reduced[y] = product if j == 0 else reduced[y] + product
            return 0

        lax.fori_loop(0, lines, line, 0)
        out_wide.start()
        out_low.start()
        for k, lag in later[j] if j < len(later) else ():
            gather.hop(k, lag)
    pltpu.make_async_copy(reduce_full, reduce_out, out_sem).start()

    origin = reduced[0, 0:1, :]
    carry = lax.fori_loop(0, lines, lambda y, c: add_moments(c, reduced[y], origin), blank(mid_width))
    total, squares, _ = over.total(1, moments(carry, origin), True)
    centre, inverse = total / number, lax.rsqrt(squares / number + epsilon)
    inverse_one[...] = inverse
    gather.hop(5, 2)

    def first(y, _):
        normed = (reduced[y] - centre) * inverse
        normed_one[y] = normed
        zeta = mask * (grouped(normed) * gain_one.reshape(1, 1, -1) + shift_one.reshape(1, 1, -1))
        act = gelu_parts(zeta)[0].reshape(rows, mid_width)
        act_one[y] = act
        change[y] = (pairs * grouped(pltpu.roll(act, rows - 1, 0) - act)).astype(bf16).reshape(rows, mid_width)
        return 0

    lax.fori_loop(0, lines, first, 0)
    gather.hop(6, 2)
    for k in range(3, 7):
        gather.hop(k, 3)
    for j in (chunks - 2, chunks - 1):
        cols = slice(j * step, (j + 1) * step)
        pltpu.make_async_copy(wide.at[j % 2], block_in.at[:, :, cols], wide_sem.at[j % 2]).wait()
        pltpu.make_async_copy(low.at[j % 2], block_low.at[:, :, cols], low_sem.at[j % 2]).wait()
    pltpu.make_async_copy(reduce_full, reduce_out, out_sem).wait()
    gather.finish()
    over.finish()


def head(stem_taps, reduce_weight, diff_weight, mid_weight, expand_weight, lateral, wide, narrow, least, lhs, valid, pair, count, features, fsdp, reps, collective_id):
    dims, sizes = factor_three(fsdp), stage_sizes(fsdp * reps)
    split = (dims[0], dims[1] * dims[2])
    shape = jax.ShapeDtypeStruct
    clips, pixels, segs, width = features.shape
    slots = clips * segs
    mid_width = reduce_weight.shape[1]
    stem_rows = lateral.shape[0]
    stem_width = stem_rows * fsdp
    rows = GRID * slots
    step = 256
    side = GRID + 2
    lengths = narrow.shape[0] * mid_width + least.shape[0] * (-(-stem_width // LANES) * LANES)
    vectors = 2 + -(-lengths // width)
    small = shape((-(-(stem_rows + vectors) // 16) * 16, width), bf16)

    def full(shard):
        return shape(shard.shape[:-2] + split + shard.shape[-2:], shard.dtype)

    def whole(shard):
        return pltpu.VMEM(split + shard.shape, shard.dtype)

    return pl.pallas_call(
        functools.partial(head_kernel, dims, reps, sizes, stem_rows),
        out_shape=[
            shape((stem_width, width), bf16), shape((vectors, width), f32),
            full(reduce_weight), full(diff_weight), full(mid_weight), full(expand_weight),
            shape((GRID, rows, width), f32), shape((GRID, rows, width), bf16),
            shape((GRID, GRID, slots, stem_width), f32), shape((GRID, GRID, slots, stem_width), bf16),
            shape((1, stem_width), f32), shape((1, LANES), f32),
            shape((GRID, rows, mid_width), f32), shape((1, mid_width), f32), shape((GRID, rows, mid_width), f32),
            shape((GRID, rows, mid_width), bf16),
        ],
        in_specs=[ANY] * 5 + [IN_VMEM] * 8 + [ANY],
        out_specs=[IN_VMEM] * 2 + [ANY] * 6 + [IN_VMEM] * 8,
        scratch_shapes=[
            pltpu.VMEM(small.shape, bf16), whole(small), whole(stem_taps), whole(reduce_weight),
            pltpu.VMEM((GRID, stem_width, stem_taps.shape[1]), f32), pltpu.VMEM((stem_width, width), f32),
            pltpu.VMEM((GRID, rows, stem_width), f32), pltpu.VMEM((side, side, slots, stem_width), f32),
            pltpu.VMEM((2, pixels, slots, step), bf16),
            pltpu.VMEM((2, GRID, rows, step), f32), pltpu.VMEM((2, GRID, rows, step), bf16),
            pltpu.VMEM((GRID, rows, mid_width), f32),
            DMA((2, clips)), DMA((2,)), DMA((2,)), DMA(()),
        ] + gather_buffers(dims, reps, 7) + exchange_buffers(sizes, 2, 2 * mid_width + LANES),
        compiler_params=pltpu.CompilerParams(
            collective_id=collective_id, has_side_effects=True, vmem_limit_bytes=VMEM_LIMIT
        ),
        name="head",
    )(stem_taps, reduce_weight, diff_weight, mid_weight, expand_weight, lateral, wide, narrow, least, lhs, valid, pair, count, features)


def tail_kernel(sizes, reps, clip_count, *refs):
    (middle, expand, valid, spread, count, gain_two, shift_two, gain_three, shift_three, pooled_grad, block_in) = refs[:11]
    (pooled, grad_pre, grad_expanded, act_two, grad_middle, gain_three_sum, shift_three_sum, gain_two_sum, shift_two_sum) = refs[11:20]
    (wide, wide_grad, narrow, narrow_grad, block, low, totals, first, block_sem, pre_sem, low_sem) = refs[20:31]
    over = Exchange(sizes, reps, refs[31:])
    lines, rows, mid_width = middle.shape
    width = expand.shape[1]
    slots = valid.shape[0]
    segs = slots // clip_count
    groups = rows // slots
    step = 256
    chunks = width // step

    barrier = pltpu.get_barrier_semaphore()
    for target, rep in over.peers:
        pl.semaphore_signal(barrier, inc=1, device_id={"fsdp": target, "rep": rep}, device_id_type=MESH)

    def fetch(y, slot):
        return pltpu.make_async_copy(block_in.at[y], block.at[slot], block_sem.at[slot])

    fetch(0, 0).start()
    mask = valid[:, :1].reshape(1, slots, 1)
    own = count[:, :1]

    def grouped(values):
        return values.reshape(groups, slots, values.shape[-1])

    def moments(carry, origin):
        away, squares = whole_row(carry[0]), whole_row(carry[1])
        return away + own * origin, jnp.maximum(squares - away * away / own, 0.0)

    def gather_moments(carry, values, origin):
        off = (grouped(values) - origin.reshape(1, 1, -1)) * mask
        return carry[0] + fold_rows(off), carry[1] + fold_rows(off * off)

    def blank(n):
        return jnp.zeros((8, n), f32), jnp.zeros((8, n), f32)

    origin = middle[0, 0:1, :]
    carry = lax.fori_loop(0, lines, lambda y, c: gather_moments(c, middle[y], origin), blank(mid_width))
    pl.semaphore_wait(barrier, len(over.peers))
    total, squares, number = over.total(0, list(moments(carry, origin)) + [count[...]], True)
    number = number[:, :1]
    centre_two, inverse_two = total / number, lax.rsqrt(squares / number + epsilon)
    gain2, shift2 = gain_two[...], shift_two[...]

    def zeta_two(normed):
        return mask * (grouped(normed) * gain2.reshape(1, 1, -1) + shift2.reshape(1, 1, -1))

    def forward_two(y, _):
        normed = (middle[y] - centre_two) * inverse_two
        narrow[y] = normed
        act_two[y] = gelu_parts(zeta_two(normed))[0].astype(bf16).reshape(rows, mid_width)
        return 0

    lax.fori_loop(0, lines, forward_two, 0)

    def expand_chunk(j, _):
        cols = pl.ds(pl.multiple_of(j * step, step), step)
        weight = expand[:, cols]
        wide[:, :, cols] = dot(act_two[...].reshape(lines * rows, mid_width), weight).reshape(lines, rows, step)
        origin = wide[0, 0:1, cols]

        def line(y, carry):
            return gather_moments(carry, wide[y, :, cols], origin)

        total, squares = moments(lax.fori_loop(0, lines, line, blank(step)), origin)
        totals[0, :, cols] = total
        totals[1, :, cols] = squares
        return 0

    lax.fori_loop(0, chunks, expand_chunk, 0)
    total, squares, _ = over.total(1, [totals[0], totals[1], count[...]], True)
    totals[0] = total / number
    totals[1] = lax.rsqrt(squares / number + epsilon)
    for index in range(2):
        first[index] = jnp.zeros((8, width), f32)

    def out_pre(y):
        return pltpu.make_async_copy(wide_grad.at[y], grad_pre.at[y], pre_sem.at[y])

    def forward_three(y, _):
        slot = y % 2
        fetch(y, slot).wait()

        @pl.when(y + 1 < lines)
        def _():
            fetch(y + 1, 1 - slot).start()

        def chunk(j, _):
            cols = pl.ds(pl.multiple_of(j * step, step), step)
            normed = (wide[y, :, cols] - totals[0, :, cols]) * totals[1, :, cols]
            wide[y, :, cols] = normed
            normed = grouped(normed)
            scaled = mask * (gain_three[:, cols].reshape(1, 1, step) * normed + shift_three[:, cols].reshape(1, 1, step))
            out, slope = gelu_parts(grouped(block[slot, :, cols]) + scaled)
            grads = []
            for clip in range(clip_count):
                span = slice(clip * segs, (clip + 1) * segs)
                share = spread[span, :1].reshape(1, segs, 1)
                pixels = pl.ds(y * groups, groups)
                pooled[clip, pixels, :, cols] = jnp.sum(out[:, span] * share, axis=1, keepdims=True)
                grads.append(slope[:, span] * (pooled_grad[clip, pixels, :, cols] * share))
            grad = jnp.concatenate(grads, axis=1)
            wide_grad[y, :, cols] = grad.reshape(rows, step)
            first[0, :, cols] += fold_rows(grad)
            first[1, :, cols] += fold_rows(grad * normed)
            return 0

        lax.fori_loop(0, chunks, chunk, 0)
        out_pre(y).start()
        return 0

    lax.fori_loop(0, lines, forward_three, 0)
    shift_sum, gain_sum = over.total(2, [whole_row(first[0]), whole_row(first[1])], False)
    shift_three_sum[...] = shift_sum
    gain_three_sum[...] = gain_sum
    totals[2] = shift_sum / number
    totals[3] = gain_sum / number
    totals[1] = totals[1] * gain_three[...]

    def out_low(y):
        return pltpu.make_async_copy(low.at[y], grad_expanded.at[y], low_sem.at[y])

    def back_three(y, _):
        def chunk(j, _):
            cols = pl.ds(pl.multiple_of(j * step, step), step)
            grad = wide_grad[y, :, cols] - totals[2, :, cols] - wide[y, :, cols] * totals[3, :, cols]
            low[y, :, cols] = (mask * grouped(grad * totals[1, :, cols])).astype(bf16).reshape(rows, step)
            return 0

        lax.fori_loop(0, chunks, chunk, 0)
        out_low(y).start()
        return 0

    lax.fori_loop(0, lines, back_three, 0)
    for start in range(0, mid_width, step):
        values = dot_t(low[...].reshape(lines * rows, width), expand[start : start + step, :])
        narrow_grad[:, :, start : start + step] = values.reshape(lines, rows, step)

    def slopes(y, carry):
        normed = narrow[y]
        grad = grouped(narrow_grad[y]) * gelu_parts(zeta_two(normed))[1] * mask
        narrow_grad[y] = grad.reshape(rows, mid_width)
        return carry[0] + fold_rows(grad), carry[1] + fold_rows(grad * grouped(normed))

    carry = lax.fori_loop(0, lines, slopes, blank(mid_width))
    shift_sum, gain_sum = over.total(3, [whole_row(carry[0]), whole_row(carry[1])], False)
    shift_two_sum[...] = shift_sum
    gain_two_sum[...] = gain_sum
    shift_mean, gain_mean, scale = shift_sum / number, gain_sum / number, inverse_two * gain2

    def back_two(y, _):
        grad = (narrow_grad[y] - shift_mean - narrow[y] * gain_mean) * scale
        grad_middle[y] = (mask * grouped(grad)).astype(bf16).reshape(rows, mid_width)
        return 0

    lax.fori_loop(0, lines, back_two, 0)
    lax.fori_loop(0, lines, lambda y, _: (out_pre(y).wait(), 0)[1], 0)
    lax.fori_loop(0, lines, lambda y, _: (out_low(y).wait(), 0)[1], 0)
    over.finish()


def tail(middle, expand, valid, spread, count, gain_two, shift_two, gain_three, shift_three, pooled_grad, block_in, clip_count, fsdp, reps, collective_id):
    sizes = stage_sizes(fsdp * reps)
    lines, rows, mid_width = middle.shape
    width = expand.shape[1]
    pixels = pooled_grad.shape[1]
    shape = jax.ShapeDtypeStruct
    return pl.pallas_call(
        functools.partial(tail_kernel, sizes, reps, clip_count),
        out_shape=[
            shape((clip_count, pixels, 1, width), f32), shape((lines, rows, width), f32), shape((lines, rows, width), bf16),
            shape((lines, rows, mid_width), bf16), shape((lines, rows, mid_width), bf16),
            shape((1, width), f32), shape((1, width), f32), shape((1, mid_width), f32), shape((1, mid_width), f32),
        ],
        in_specs=[IN_VMEM] * 10 + [ANY],
        out_specs=[IN_VMEM, ANY, ANY] + [IN_VMEM] * 6,
        scratch_shapes=[
            pltpu.VMEM((lines, rows, width), f32), pltpu.VMEM((lines, rows, width), f32),
            pltpu.VMEM((lines, rows, mid_width), f32), pltpu.VMEM((lines, rows, mid_width), f32),
            pltpu.VMEM((2, rows, width), f32), pltpu.VMEM((lines, rows, width), bf16),
            pltpu.VMEM((4, 1, width), f32), pltpu.VMEM((2, 8, width), f32),
            DMA((2,)), DMA((lines,)), DMA((lines,)),
        ] + exchange_buffers(sizes, 4, 2 * width + LANES),
        compiler_params=pltpu.CompilerParams(collective_id=collective_id, has_side_effects=True, vmem_limit_bytes=VMEM_LIMIT),
        name="tail",
    )(middle, expand, valid, spread, count, gain_two, shift_two, gain_three, shift_three, pooled_grad, block_in)


def back_kernel(clips, *refs):
    grad_reduced, reduce_full, pool_low, lateral, grad_pre = refs[:5]
    features_grad, lateral_terms, grad_act = refs[5:8]
    loaded, sums, low, total, load_sem, out_sem = refs[8:]
    lines, rows, mid_width = grad_reduced.shape
    width = reduce_full.shape[0]
    groups = GRID
    slots = rows // groups
    segs = slots // clips
    step = 512

    def load(y):
        return pltpu.make_async_copy(grad_pre.at[y], loaded.at[y % 2], load_sem.at[y % 2])

    def store(y):
        slot = y % 2
        return [
            pltpu.make_async_copy(
                sums.at[slot, :, clip * segs : (clip + 1) * segs, :],
                features_grad.at[clip, pl.ds(y * groups, groups)],
                out_sem.at[slot, clip],
            )
            for clip in range(clips)
        ]

    load(0).start()
    total[...] = jnp.zeros(total.shape, f32)

    def line(y, _):
        slot = y % 2
        load(y).wait()

        @pl.when(y + 1 < lines)
        def _():
            load(y + 1).start()

        @pl.when(y >= 2)
        def _():
            for copy in store(y - 2):
                copy.wait()

        for start in range(0, width, step):
            cols = slice(start, start + step)
            values = loaded[slot, :, cols] + dot_t(grad_reduced[y], reduce_full[cols, :])
            sums[slot, :, :, cols] = values.reshape(groups, slots, step)
            low[:, cols] = values.astype(bf16)
        for copy in store(y):
            copy.start()
        grad_act[y] = dot_t(low[...], lateral[...])
        turned = jnp.transpose(pool_low[y])
        for start in range(0, width, step):
            cols = slice(start, start + step)
            total[:, cols] += dot(turned, low[:, cols])
        return 0

    lax.fori_loop(0, lines, line, 0)
    lateral_terms[...] = total[...].astype(bf16)
    for y in (lines - 2, lines - 1):
        for copy in store(y):
            copy.wait()


def back(grad_reduced, reduce_full, pool_low, lateral, grad_pre, clips):
    lines, rows, mid_width = grad_reduced.shape
    width = reduce_full.shape[0]
    slots = rows // GRID
    stem_width = lateral.shape[0]
    shape = jax.ShapeDtypeStruct
    return pl.pallas_call(
        functools.partial(back_kernel, clips),
        out_shape=[
            shape((clips, lines * GRID, slots // clips, width), f32), shape((stem_width, width), bf16),
            shape((lines, rows, stem_width), f32),
        ],
        in_specs=[IN_VMEM] * 4 + [ANY],
        out_specs=[ANY, IN_VMEM, IN_VMEM],
        scratch_shapes=[
            pltpu.VMEM((2, rows, width), f32), pltpu.VMEM((2, GRID, slots, width), f32), pltpu.VMEM((rows, width), bf16),
            pltpu.VMEM((stem_width, width), f32), DMA((2,)), DMA((2, clips)),
        ],
        compiler_params=pltpu.CompilerParams(vmem_limit_bytes=VMEM_LIMIT),
        cost_estimate=pl.CostEstimate(flops=4 * lines * rows * width * mid_width, bytes_accessed=8 * lines * rows * width, transcendentals=0),
        name="back",
    )(grad_reduced, reduce_full, pool_low, lateral, grad_pre)


ORDER = ("HWNC", "HWIO", "HWNC")


def pad_of(span):
    return ((span, span), (span, span))


def convolve(source, weight, span, stride):
    side = 2 * span + 1
    kernel = weight.reshape(side, side, source.shape[-1], -1)
    return lax.conv_general_dilated(
        source, kernel, (1, 1), pad_of(span * stride), rhs_dilation=(stride, stride),
        dimension_numbers=ORDER, preferred_element_type=f32,
    )


def convolve_back(grads, weight, span, stride):
    side = 2 * span + 1
    kernel = weight.reshape(side, side, -1, grads.shape[-1])[::-1, ::-1]
    return lax.conv_general_dilated(
        grads, kernel, (1, 1), pad_of(span * stride), rhs_dilation=(stride, stride),
        dimension_numbers=("HWNC", "HWOI", "HWNC"), preferred_element_type=f32,
    )


def convolve_terms(source, grads, span, stride, kind):
    return lax.conv_general_dilated(
        source, grads, (stride, stride), pad_of(span * stride),
        dimension_numbers=("HWCN", "HWIO", "HWNC"), preferred_element_type=kind,
    )


def pool_mean(source):
    total = lax.reduce_window(source, 0.0, lax.add, (3, 3, 1, 1), (1, 1, 1, 1), "SAME")
    return total / 9.0


def project(source, weight):
    return jnp.einsum("yxnc,cd->yxnd", source, weight, preferred_element_type=f32)


def project_back(grads, weight):
    return jnp.einsum("yxnd,cd->yxnc", grads, weight, preferred_element_type=f32)


def project_terms(source, grads, kind):
    return jnp.einsum("yxnc,yxnd->cd", source, grads, preferred_element_type=kind)


def gelu_back(pre_act, grads):
    return jax.vjp(jax.nn.gelu, pre_act)[1](grads)[0]


def make_shards(fsdp, reps):
    def shards(
        frames, features, seg_counts, stem_weight, stem_gain, stem_shift, lateral, reduce_weight,
        gain_one, shift_one, diff_weight, gate_shift, mid_weight, gain_two, shift_two,
        expand_weight, gain_three, shift_three, pooled_grad,
    ):
        clip_count, seg_slots, pixels, feature_width = features.shape
        slots = clip_count * seg_slots
        mid_width = reduce_weight.shape[1]
        stem_rows, stem_depth = stem_weight.shape
        stem_width = stem_rows * fsdp

        seg_index = lax.broadcasted_iota(jnp.int32, (clip_count, seg_slots), 1)
        valid_seg = (seg_index < seg_counts[:, None]).astype(f32)
        pair_seg = valid_seg * jnp.concatenate(
            [valid_seg[:, 1:], jnp.zeros((clip_count, 1), f32)], axis=1
        )
        valid = valid_seg.reshape(1, 1, slots, 1)
        pair = pair_seg.reshape(1, 1, slots, 1)
        count_float = seg_counts.astype(f32)
        local_count = jnp.sum(count_float) * pixels

        taps = jnp.pad(stem_weight.reshape(stem_rows, GRID, GRID, -1), ((0, 0), (0, 0), (3, 3), (0, 0)))
        taps = jnp.stack([taps[:, :, 6 - x : 13 - x] for x in range(GRID)]).reshape(GRID * stem_rows, stem_depth)
        taps = jnp.pad(taps, ((0, -taps.shape[0] % 16), (0, -stem_depth % (LANES * reps))))
        moving = frames.astype(f32)
        motion = (moving[:, :, 1:] - moving[:, :, :-1]) * valid_seg[:, :, None, None, None]
        motion = jnp.transpose(motion.astype(bf16), (4, 0, 1, 2, 3)).reshape(GRID, GRID, slots, -1)
        strips = jnp.transpose(motion, (0, 2, 1, 3)).reshape(GRID, slots, -1)
        strips = jnp.pad(strips, ((3, 3), (0, 0), (0, 0)))
        strips = jnp.concatenate([strips[dy : dy + GRID] for dy in range(GRID)], axis=-1).reshape(GRID * slots, -1)
        strips = jnp.pad(strips, ((0, 0), (0, -stem_depth % (LANES * reps))))
        lanes = lambda column: jnp.broadcast_to(column.reshape(-1, 1), (column.size, LANES))
        (lateral_full, vectors, reduce_full, diff_full, mid_full, expand_full, block_in, block_low, stem_normed, pool_low,
         stem_inverse, number, normed_one, inverse_one, act_one, change) = head(
            taps, reduce_weight, diff_weight, mid_weight, expand_weight, lateral, jnp.stack([gain_three, shift_three]),
            jnp.stack([gain_one, shift_one, gate_shift, gain_two, shift_two]), jnp.stack([stem_gain, stem_shift]),
            strips, lanes(valid_seg), lanes(pair_seg), lanes(local_count), jnp.transpose(features, (0, 2, 1, 3)),
            fsdp, reps, 1,
        )
        row = vectors[2:].reshape(-1)
        gain_one_full, shift_one_full, gate_full, gain_two_full, shift_two_full = (
            row[n * mid_width : (n + 1) * mid_width] for n in range(5)
        )
        gain_three_full, shift_three_full = vectors[0], vectors[1]
        start = 5 * mid_width
        stem_gain_full = row[start : start + stem_width]
        start += -(-stem_width // LANES) * LANES
        stem_shift_full = row[start : start + stem_width]
        reduce_full = reduce_full.reshape(-1, mid_width)
        diff_full = diff_full.reshape(2, -1, mid_width)
        mid_full = mid_full.reshape(-1, mid_width)
        expand_full = expand_full.reshape(mid_width, -1)
        cube = (GRID, GRID, slots, -1)
        flat = (GRID, GRID * slots, -1)
        normed_one, act_one, change = normed_one.reshape(cube), act_one.reshape(cube), change.reshape(cube)
        stats_one = (None, inverse_one[0], number[0, 0])
        stem_stats = (None, stem_inverse[0], number[0, 0])
        zeta_one = valid * (gain_one_full * normed_one + shift_one_full)
        stem_norm = valid * (stem_gain_full * stem_normed + stem_shift_full)

        def norm_back(grad_out, normed, stats, gain, collective_id, name):
            masked = grad_out * valid
            shift_sum, gain_sum = exchange(
                [jnp.sum(masked, axis=(0, 1, 2)), jnp.sum(masked * normed, axis=(0, 1, 2))],
                fsdp, reps, False, collective_id, name,
            )
            grad_in = valid * stats[1] * gain * (masked - shift_sum / stats[2] - normed * gain_sum / stats[2])
            return grad_in.astype(bf16), gain_sum, shift_sum

        def earlier_of(values):
            grid = values.reshape(GRID, GRID, clip_count, seg_slots, -1)
            return jnp.pad(grid[:, :, :, :-1], ((0, 0), (0, 0), (0, 0), (1, 0), (0, 0))).reshape(values.shape)

        gate_pre = convolve(change, diff_full[0], 1, 1) + convolve(change, diff_full[1], 1, 2)
        gate = jax.nn.sigmoid(gate_pre + gate_full)
        modulated = (act_one * (1.0 + gate)).astype(bf16)
        middle = convolve(modulated, mid_full, 1, 1)
        (pooled, grad_pre, grad_expanded, act_two, grad_middle, gain_three_sum, shift_three_sum, gain_two_sum,
         shift_two_sum) = tail(
            middle.reshape(flat), expand_full, lanes(valid_seg), lanes(valid_seg / count_float[:, None]), lanes(local_count),
            gain_two_full[None], shift_two_full[None], gain_three_full[None], shift_three_full[None],
            pooled_grad.astype(f32)[:, :, None], block_in, clip_count, fsdp, reps, 4,
        )
        pooled = pooled.reshape(pooled_grad.shape).astype(bf16)
        gain_three_sum, shift_three_sum, gain_two_sum, shift_two_sum = (
            row[0] for row in (gain_three_sum, shift_three_sum, gain_two_sum, shift_two_sum)
        )
        grad_pre, grad_expanded, act_two, grad_middle = (
            block.reshape(cube) for block in (grad_pre, grad_expanded, act_two, grad_middle)
        )
        grad_modulated = convolve_back(grad_middle, mid_full, 1, 1)
        grad_gate_pre = grad_modulated * act_one * gate * (1.0 - gate)
        gate_terms = jnp.sum(grad_gate_pre, axis=(0, 1, 2))
        grad_gate = grad_gate_pre.astype(bf16)
        grad_change = convolve_back(grad_gate, diff_full[0], 1, 1) + convolve_back(grad_gate, diff_full[1], 1, 2)
        grad_change = grad_change * pair
        grad_act_one = grad_modulated * (1.0 + gate) + earlier_of(grad_change) - grad_change
        grad_reduced, gain_one_sum, shift_one_sum = norm_back(
            gelu_back(zeta_one, grad_act_one), normed_one, stats_one, gain_one_full, 8, "sums_one"
        )
        features_grad, lateral_terms, grad_act = back(
            grad_reduced.reshape(flat), reduce_full, pool_low.reshape(flat), lateral_full, grad_pre.reshape(flat), clip_count
        )
        grad_act = pool_mean(grad_act.reshape(cube))
        grad_stem, stem_gain_sum, stem_shift_sum = norm_back(
            gelu_back(stem_norm, grad_act), stem_normed, stem_stats, stem_gain_full, 9, "sums_stem"
        )
        stem_terms = convolve_terms(motion, grad_stem, 3, 1, bf16)
        stem_terms = jnp.transpose(stem_terms, (3, 0, 1, 2)).reshape(fsdp, stem_rows, stem_depth)
        gate_rows = gate_shift.shape[0]
        small_terms = jnp.concatenate(
            [
                lateral_terms.reshape(fsdp, stem_rows, feature_width),
                jnp.pad(stem_terms, ((0, 0), (0, 0), (0, feature_width - stem_depth))),
                jnp.pad(
                    gate_terms.astype(bf16).reshape(fsdp, 1, gate_rows),
                    ((0, 0), (0, 15 - 2 * stem_rows), (0, feature_width - gate_rows)),
                ),
            ],
            axis=1,
        )

        conv_rows = mid_weight.shape[0]
        if conv_rows % 32 == 0:
            lateral_part, stem_part, gate_part, reduce_part, expand_part, mid_part, diff_part = terms_all(
                small_terms.reshape(-1, feature_width), block_low, grad_reduced.reshape(flat),
                act_two.reshape(flat), grad_expanded.reshape(flat), modulated, grad_middle.reshape(flat), change,
                grad_gate.reshape(flat),
                [small_terms.shape[1], reduce_weight.shape[0], expand_weight.shape[0], conv_rows], stem_rows, stem_depth,
                fsdp, reps, 10,
            )
        else:
            def owned(terms, shard):
                return terms.reshape((fsdp,) + shard.shape[-2:])

            small_part, reduce_part, expand_part, mid_part, diff_one, diff_two = scatter_all(
                [
                    small_terms,
                    owned(project_terms(block_low.reshape(cube), grad_reduced, bf16), reduce_weight),
                    owned(project_terms(act_two, grad_expanded, bf16), expand_weight),
                    owned(convolve_terms(modulated, grad_middle, 1, 1, bf16), mid_weight),
                    owned(convolve_terms(change, grad_gate, 1, 1, bf16), diff_weight),
                    owned(convolve_terms(change, grad_gate, 1, 2, bf16), diff_weight),
                ],
                fsdp, reps, 11, "scatter_terms",
            )
            lateral_part, gate_part = small_part[:stem_rows], small_part[2 * stem_rows, :gate_rows]
            stem_part = small_part[stem_rows : 2 * stem_rows, :stem_depth]
            diff_part = jnp.stack([diff_one, diff_two])

        def own_share(whole):
            share = whole.shape[0] // fsdp
            return lax.dynamic_slice_in_dim(whole, lax.axis_index("fsdp") * share, share)

        out = jnp.transpose(features_grad, (0, 2, 1, 3))
        return (
            pooled,
            out,
            stem_part,
            own_share(stem_gain_sum),
            own_share(stem_shift_sum),
            lateral_part,
            reduce_part,
            own_share(gain_one_sum),
            own_share(shift_one_sum),
            diff_part,
            gate_part.reshape(-1),
            mid_part,
            own_share(gain_two_sum),
            own_share(shift_two_sum),
            expand_part,
            own_share(gain_three_sum),
            own_share(shift_three_sum),
        )

    return shards


def solution(mesh):
    whole = ("fsdp", "rep")
    matrix, vector = P("fsdp", None), P("fsdp")
    in_specs = (
        P(whole, None, None, None, None), P(whole, None, None, None), P(whole),
        matrix, vector, vector, matrix, matrix, vector, vector, P(None, "fsdp", None), vector,
        matrix, vector, vector, matrix, vector, vector, P(whole, None, None),
    )
    out_specs = (
        P(whole, None, None), P(whole, None, None, None), matrix, vector, vector, matrix, matrix,
        vector, vector, P(None, "fsdp", None), vector, matrix, vector, vector, matrix, vector, vector,
    )
    body = make_shards(mesh.shape["fsdp"], mesh.shape["rep"])
    return jax.shard_map(body, mesh=mesh, in_specs=in_specs, out_specs=out_specs, check_vma=False)
```

```python
import functools

import jax
import jax.numpy as jnp
from jax import lax
from jax.experimental import pallas as pl
from jax.experimental.pallas import tpu as pltpu
from jax.sharding import PartitionSpec as P

GRID = 7
LANES = 128
PIXELS = GRID * GRID
epsilon = 1e-05
MESH = pl.DeviceIdType.MESH
ANY = pl.BlockSpec(memory_space=pl.ANY)
IN_VMEM = pl.BlockSpec(memory_space=pltpu.VMEM)
VMEM_LIMIT = 60 * 1024 * 1024
bf16 = jnp.bfloat16
f32 = jnp.float32
DMA = pltpu.SemaphoreType.DMA


def factor_three(size):
    best = None
    for b in range(1, size + 1):
        for c in range(1, b + 1):
            if size % (b * c) == 0 and size // (b * c) >= b:
                a = size // (b * c)
                if best is None or a + b + c < sum(best):
                    best = (a, b, c)
    return best


class Place:
    def __init__(self, dims, reps, rep=None):
        self.dims, self.reps = dims, reps
        size_a, size_b, size_c = dims
        self.me = lax.axis_index("fsdp")
        self.rep = lax.axis_index("rep") if rep is None else rep
        ib, ic = (self.me // size_c) % size_b, self.me % size_c
        self.ia = self.me // (size_b * size_c)
        odd = self.rep % 2 if size_b == size_c else 0
        self.stride_u = size_c * (1 - odd) + odd
        self.stride_v = (1 - odd) + size_c * odd
        self.iu = ib * (1 - odd) + ic * odd
        self.iv = ic * (1 - odd) + ib * odd

    def at(self, da, du, dv):
        size_a, size_b, size_c = self.dims
        a = (self.ia + da + size_a) % size_a
        u = (self.iu + du + size_b) % size_b
        v = (self.iv + dv + size_c) % size_c
        return a * (size_b * size_c) + u * self.stride_u + v * self.stride_v

    def greet(self, more=()):
        size_a, size_b, size_c = self.dims
        peers = [(self.at(d, 0, 0), self.rep) for d in range(1, size_a)]
        peers += [(self.at(0, d, 0), self.rep) for d in range(1, size_b)]
        peers += [(self.at(0, 0, d), self.rep) for d in range(1, size_c)]
        peers += [(self.me, (self.rep + d) % self.reps) for d in range(1, self.reps)]
        greet(peers + list(more))


def greet(peers):
    barrier = pltpu.get_barrier_semaphore()
    for target, rep in peers:
        pl.semaphore_signal(
            barrier, inc=1, device_id={"fsdp": target, "rep": rep}, device_id_type=MESH
        )
    pl.semaphore_wait(barrier, len(peers))


def remote(src, dst, sems, target, rep):
    return pltpu.make_async_remote_copy(
        src_ref=src,
        dst_ref=dst,
        send_sem=sems.at[0],
        recv_sem=sems.at[1],
        device_id={"fsdp": target, "rep": rep},
        device_id_type=MESH,
    )


def columns(width, which):
    start = which * width
    return pl.ds(start if isinstance(start, int) else pl.multiple_of(start, width), width)


def views(refs):
    out = []
    for ref, stacked in refs:
        out += [ref.at[j] for j in range(ref.shape[0])] if stacked else [ref]
    return out


def scatter_kernel(dims, reps, stacked, *refs):
    number = len(stacked)
    partials = views(zip(refs[:number], stacked))
    totals = views(zip(refs[number : 2 * number], stacked))
    count = len(partials)
    rest = refs[2 * number :]
    held, from_rep, from_v, from_u, from_a, share = (rest[i * count : (i + 1) * count] for i in range(6))
    own_sem, r_sem, v_sem, u_sem, a_sem, s_sem = rest[6 * count :]
    size_a, size_b, size_c = dims
    place = Place(dims, reps)
    me, rep = place.me, place.rep
    place.greet()
    waits = []

    def push(source, there, sems, target, target_rep):
        copy = remote(source, there, sems, target, target_rep)
        copy.start()
        waits.append(copy)

    def landed(there, sems):
        remote(there, there, sems, me, rep).wait_recv()

    def order():
        for dv in list(range(1, size_c)) + [0]:
            for du in list(range(1, size_b)) + [0]:
                for da in list(range(1, size_a)) + [0]:
                    yield da, du, dv

    local = {}
    for k in range(count):
        width = partials[k].shape[-1] // reps
        for da, du, dv in order():
            for d in range(1, reps):
                other = (rep + d) % reps
                index = Place(dims, reps, other).at(da, du, dv)
                push(
                    partials[k].at[index, :, columns(width, other)],
                    from_rep[k].at[d - 1, index],
                    r_sem.at[k, da, du, dv, d - 1],
                    me,
                    other,
                )
            index = place.at(da, du, dv)
            copy = pltpu.make_async_copy(
                partials[k].at[index, :, columns(width, rep)],
                held[k].at[index],
                own_sem.at[k, da, du, dv],
            )
            copy.start()
            local[k, da, du, dv] = copy

    def handle(k, da, du, dv):
        index = place.at(da, du, dv)
        local[k, da, du, dv].wait()
        total = held[k][index].astype(f32)
        for d in range(1, reps):
            landed(from_rep[k].at[d - 1, index], r_sem.at[k, da, du, dv, d - 1])
            total = total + from_rep[k][d - 1, index].astype(f32)
        if dv == 0:
            for e in range(1, size_c):
                landed(from_v[k].at[e - 1, da, du], v_sem.at[k, da, du, e - 1])
                total = total + from_v[k][e - 1, da, du].astype(f32)
            if du == 0:
                for e in range(1, size_b):
                    landed(from_u[k].at[e - 1, da], u_sem.at[k, da, e - 1])
                    total = total + from_u[k][e - 1, da].astype(f32)
                if da == 0:
                    for e in range(1, size_a):
                        landed(from_a[k].at[e - 1], a_sem.at[k, e - 1])
                        total = total + from_a[k][e - 1].astype(f32)
        if (da, du, dv) == (0, 0, 0):
            share[k][rep] = total.astype(bf16)
            for d in range(1, reps):
                push(share[k].at[rep], share[k].at[rep], s_sem.at[k, d - 1], me, (rep + d) % reps)
            return
        held[k][index] = total.astype(bf16)
        if dv:
            push(held[k].at[index], from_v[k].at[dv - 1, da, du], v_sem.at[k, da, du, dv - 1], place.at(0, 0, dv), rep)
        elif du:
            push(held[k].at[index], from_u[k].at[du - 1, da], u_sem.at[k, da, du - 1], place.at(0, du, 0), rep)
        else:
            push(held[k].at[index], from_a[k].at[da - 1], a_sem.at[k, da - 1], place.at(da, 0, 0), rep)

    for step in range(count + 3):
        for lag in range(4):
            k = step - lag
            for da, du, dv in order() if 0 <= k < count else ():
                if lag == (0 if dv else 1 if du else 2 if da else 3):
                    handle(k, da, du, dv)
    for k in range(count):
        width = partials[k].shape[-1] // reps
        for d in range(1, reps):
            landed(share[k].at[(rep + reps - d) % reps], s_sem.at[k, d - 1])
        for which in range(reps):
            totals[k][:, which * width : (which + 1) * width] = share[k][which].astype(f32)
    for copy in waits:
        copy.wait_send()


def scatter_all(partials, fsdp, reps, collective_id, name):
    dims = factor_three(fsdp)
    size_a, size_b, size_c = dims
    stacked = [p.ndim == 4 for p in partials]
    shapes = []
    for p in partials:
        shapes += [(p.shape[-2], p.shape[-1] // reps)] * (p.shape[0] if p.ndim == 4 else 1)
    count = len(shapes)

    def buffers(*lead):
        return [pltpu.VMEM(lead + shape, bf16) for shape in shapes]

    return pl.pallas_call(
        functools.partial(scatter_kernel, dims, reps, stacked),
        out_shape=[
            jax.ShapeDtypeStruct(p.shape[:-3] + p.shape[-2:], f32) for p in partials
        ],
        in_specs=[ANY] * len(partials),
        out_specs=[IN_VMEM] * len(partials),
        scratch_shapes=buffers(fsdp)
        + buffers(max(reps - 1, 1), fsdp)
        + buffers(max(size_c - 1, 1), size_a, size_b)
        + buffers(max(size_b - 1, 1), size_a)
        + buffers(max(size_a - 1, 1))
        + buffers(reps)
        + [
            DMA((count, size_a, size_b, size_c)),
            DMA((count, size_a, size_b, size_c, max(reps - 1, 1), 2)),
            DMA((count, size_a, size_b, max(size_c - 1, 1), 2)),
            DMA((count, size_a, max(size_b - 1, 1), 2)),
            DMA((count, max(size_a - 1, 1), 2)),
            DMA((count, max(reps - 1, 1), 2)),
        ],
        compiler_params=pltpu.CompilerParams(
            collective_id=collective_id, has_side_effects=True, vmem_limit_bytes=VMEM_LIMIT
        ),
        name=name,
    )(*partials)


def stage_sizes(devices):
    sizes = []
    while devices > 1:
        size = next(s for s in (8, 4, 2, 7, 5, 3, devices) if devices % s == 0)
        sizes.append(size)
        devices //= size
    return sizes


class Exchange:
    def __init__(self, sizes, reps, buffers):
        self.sizes, self.reps = sizes, reps
        self.mine, self.slots, self.sems = buffers[0], buffers[1:-1], buffers[-1]
        place = lax.axis_index("fsdp") * reps + lax.axis_index("rep")
        self.stages = []
        stride = 1
        for size in sizes:
            position = (place // stride) % size
            peers = []
            for d in range(1, size):
                target = place + ((position + d) % size - position) * stride
                peers.append((target // reps, target % reps))
            self.stages.append((size, position, peers))
            stride *= size
        self.peers = [peer for stage in self.stages for peer in stage[2]]
        self.waits = []

    def total(self, round, current, moments):
        number = len(current)
        spans, start = [], 0
        for value in current:
            spans.append((start, value.shape[1]))
            start += value.shape[1]
        for index, (size, position, peers) in enumerate(self.stages):
            used = pl.ds(0, sum(length for _, length in spans))
            mine = self.mine.at[round, index, :, used]
            slots = self.slots[index].at[round, :, :, used]
            for (start, length), value in zip(spans, current):
                mine[:, start : start + length] = value
            for d, (target, rep) in enumerate(peers, 1):
                copy = remote(mine, slots.at[position], self.sems.at[round, index, d - 1], target, rep)
                copy.start()
                self.waits.append(copy)
            slots[position] = mine[...]
            for d, (target, rep) in enumerate(peers, 1):
                there = slots.at[(position + size - d) % size]
                remote(there, there, self.sems.at[round, index, d - 1], target, rep).wait_recv()
            parts = [
                [slots[j, :, start : start + length] for start, length in spans] for j in range(size)
            ]
            current = [functools.reduce(jnp.add, [part[row] for part in parts]) for row in range(number)]
            if moments:
                centre = current[0] / current[2][:, :1]
                squares = current[1]
                for part in parts:
                    count = part[2][:, :1]
                    off = part[0] / count - centre
                    squares = squares + count * off * off
                current[1] = squares
        return current

    def finish(self):
        for copy in self.waits:
            copy.wait_send()


def exchange_buffers(sizes, rounds, total):
    return (
        [pltpu.VMEM((rounds, len(sizes), 1, total), f32)]
        + [pltpu.VMEM((rounds, size, 1, total), f32) for size in sizes]
        + [DMA((rounds, len(sizes), max(max(sizes) - 1, 1), 2))]
    )


def exchange_kernel(sizes, reps, moments, *refs):
    number = 3 if moments else 2
    sources, results = refs[:number], refs[number : 2 * number]
    over = Exchange(sizes, reps, refs[2 * number :])
    greet(over.peers)
    current = over.total(0, [source[...] for source in sources], moments)
    for result, value in zip(results, current):
        result[...] = value
    over.finish()


def exchange(rows, fsdp, reps, moments, collective_id, name):
    sizes = stage_sizes(fsdp * reps)
    width = rows[0].shape[-1]
    padded = -(-width // LANES) * LANES
    rows = [jnp.pad(row.reshape(1, -1), ((0, 0), (0, padded - width))) for row in rows[:2]] + [
        jnp.broadcast_to(row.reshape(1, 1), (1, LANES)) for row in rows[2:]
    ]
    results = pl.pallas_call(
        functools.partial(exchange_kernel, sizes, reps, moments),
        out_shape=[jax.ShapeDtypeStruct(row.shape, f32) for row in rows],
        in_specs=[IN_VMEM] * len(rows),
        out_specs=[IN_VMEM] * len(rows),
        scratch_shapes=exchange_buffers(sizes, 1, sum(row.shape[1] for row in rows)),
        compiler_params=pltpu.CompilerParams(
            collective_id=collective_id, has_side_effects=True, vmem_limit_bytes=4 * 1024 * 1024
        ),
        name=name,
    )(*rows)
    return [result[0, :width] for result in results[:2]] + [result[0, 0] for result in results[2:]]


TANH_SCALE = 0.7978845608028654
CUBIC = 0.044715


def gelu_parts(x):
    square = x * x
    bend = jnp.tanh(TANH_SCALE * x * (1.0 + CUBIC * square))
    half = 0.5 * (1.0 + bend)
    slope = half + 0.5 * x * (1.0 - bend * bend) * (TANH_SCALE * (1.0 + 3.0 * CUBIC * square))
    return x * half, slope


def fold_rows(values):
    groups, slots, width = values.shape
    return jnp.sum(values.reshape(groups * slots // 8, 8, width), axis=0)


def whole_row(values):
    return jnp.sum(values, axis=0, keepdims=True)


def dot(left, right):
    return jnp.dot(left, right, preferred_element_type=f32)


def dot_t(left, right):
    return lax.dot_general(left, right, (((1,), (1,)), ((), ())), preferred_element_type=f32)


class Scatter:
    def __init__(self, dims, reps, terms, rows, buffers):
        count = len(terms)
        self.dims, self.reps, self.terms, self.rows = dims, reps, terms, rows
        self.from_rep, self.from_v, self.from_u, self.from_a, self.share = (
            buffers[i * count : (i + 1) * count] for i in range(5)
        )
        self.r_sem, self.v_sem, self.u_sem, self.a_sem, self.s_sem = buffers[5 * count :]
        self.place = Place(dims, reps)
        self.waits = []

    def push(self, source, there, sems, target, target_rep):
        copy = remote(source, there, sems, target, target_rep)
        copy.start()
        self.waits.append(copy)

    def landed(self, there, sems):
        remote(there, there, sems, self.place.me, self.place.rep).wait_recv()

    def part(self, k, index, which):
        rows = self.rows[k]
        start = pl.multiple_of(index * rows, rows)
        return self.terms[k].at[pl.ds(start, rows), columns(self.terms[k].shape[1] // self.reps, which)]

    def order(self):
        size_a, size_b, size_c = self.dims
        for dv in list(range(1, size_c)) + [0]:
            for du in list(range(1, size_b)) + [0]:
                for da in list(range(1, size_a)) + [0]:
                    yield da, du, dv

    def cores(self, k):
        rep, reps = self.place.rep, self.reps
        for d in range(1, reps):
            other = (rep + d) % reps
            source = self.terms[k].at[:, columns(self.terms[k].shape[1] // reps, other)]
            self.push(source, self.from_rep[k].at[d - 1], self.r_sem.at[k, d - 1], self.place.me, other)

    def hop(self, k, lag):
        if lag == 0:
            for d in range(1, self.reps):
                self.landed(self.from_rep[k].at[d - 1], self.r_sem.at[k, d - 1])
        if 0 <= k < len(self.terms):
            for da, du, dv in self.order():
                if lag == (0 if dv else 1 if du else 2 if da else 3):
                    self.handle(k, da, du, dv)

    def handle(self, k, da, du, dv):
        size_a, size_b, size_c = self.dims
        place, reps, rep = self.place, self.reps, self.place.rep
        index = place.at(da, du, dv)
        mine = self.part(k, index, rep)
        rows = self.rows[k]
        span = pl.ds(pl.multiple_of(index * rows, rows), rows)
        if dv and reps == 2:
            total = mine[...] + self.from_rep[k][0, span]
        else:
            total = mine[...].astype(f32)
            for d in range(1, reps):
                total = total + self.from_rep[k][d - 1, span].astype(f32)
        if dv == 0:
            for e in range(1, size_c):
                self.landed(self.from_v[k].at[e - 1, da, du], self.v_sem.at[k, da, du, e - 1])
                total = total + self.from_v[k][e - 1, da, du].astype(f32)
            if du == 0:
                for e in range(1, size_b):
                    self.landed(self.from_u[k].at[e - 1, da], self.u_sem.at[k, da, e - 1])
                    total = total + self.from_u[k][e - 1, da].astype(f32)
                if da == 0:
                    for e in range(1, size_a):
                        self.landed(self.from_a[k].at[e - 1], self.a_sem.at[k, e - 1])
                        total = total + self.from_a[k][e - 1].astype(f32)
        if (da, du, dv) == (0, 0, 0):
            self.share[k][rep] = total.astype(bf16)
            for d in range(1, reps):
                self.push(self.share[k].at[rep], self.share[k].at[rep], self.s_sem.at[k, d - 1], place.me, (rep + d) % reps)
            return
        mine[...] = total.astype(bf16)
        if dv:
            self.push(mine, self.from_v[k].at[dv - 1, da, du], self.v_sem.at[k, da, du, dv - 1], place.at(0, 0, dv), rep)
        elif du:
            self.push(mine, self.from_u[k].at[du - 1, da], self.u_sem.at[k, da, du - 1], place.at(0, du, 0), rep)
        else:
            self.push(mine, self.from_a[k].at[da - 1], self.a_sem.at[k, da - 1], place.at(da, 0, 0), rep)

    def finish(self, totals):
        for k, total in enumerate(totals):
            width = self.terms[k].shape[1] // self.reps
            for d in range(1, self.reps):
                self.landed(self.share[k].at[(self.place.rep + self.reps - d) % self.reps], self.s_sem.at[k, d - 1])
            for which in range(self.reps):
                start = which * width
                for ref, row in total if isinstance(total, list) else [(total, 0)]:
                    height, length = ref.shape[0], min(ref.shape[1] - start, width)
                    if length > 0:
                        ref[:, start : start + length] = self.share[k][which, row : row + height, :length].astype(f32)
        for copy in self.waits:
            copy.wait_send()


def scatter_buffers(dims, reps, shapes):
    size_a, size_b, size_c = dims
    count = len(shapes)
    others = max(reps - 1, 1)

    def buffers(*lead):
        return [pltpu.VMEM(lead + (rows, width // reps), bf16) for rows, width in shapes]

    return (
        [pltpu.VMEM((others, size_a * size_b * size_c * rows, width // reps), bf16) for rows, width in shapes]
        + buffers(max(size_c - 1, 1), size_a, size_b)
        + buffers(max(size_b - 1, 1), size_a)
        + buffers(max(size_a - 1, 1))
        + buffers(reps)
        + [
            DMA((count, others, 2)),
            DMA((count, size_a, size_b, max(size_c - 1, 1), 2)),
            DMA((count, size_a, max(size_b - 1, 1), 2)),
            DMA((count, max(size_a - 1, 1), 2)),
            DMA((count, others, 2)),
        ]
    )


def terms_kernel(dims, reps, rows, *refs):
    (small, block_low, grad_reduced, act_two, grad_expanded, modulated, grad_middle, change, grad_gate) = refs[:9]
    lateral_total, stem_total, gate_total, reduce_total, expand_total, mid_total, diff_total = refs[9:16]
    stem_rows = stem_total.shape[0]
    totals = [
        [(lateral_total, 0), (stem_total, stem_rows), (gate_total, 2 * stem_rows)],
        reduce_total, expand_total, mid_total, diff_total.at[0], diff_total.at[1],
    ]
    terms = refs[16:22]
    pads, line, turned, chunk, pad_sem, line_sem, chunk_sem, small_sem = refs[22:30]
    scatter = Scatter(dims, reps, terms, rows, refs[30:])
    slots, mid_width = modulated.shape[2:]
    lines = block_low.shape[0]
    width = block_low.shape[2]
    step = chunk.shape[-1]
    chunks = width // step
    ring = 2

    place = scatter.place
    small_copy = pltpu.make_async_copy(small, terms[0], small_sem)
    small_copy.start()
    sources = [(block_low, j) for j in range(chunks)] + [(grad_expanded, j) for j in range(chunks)]

    def load(number):
        source, j = sources[number]
        return pltpu.make_async_copy(
            source.at[:, :, j * step : (j + 1) * step], chunk.at[number % 2], chunk_sem.at[number % 2]
        )

    gradients = [grad_middle, grad_gate, grad_reduced, act_two]

    def turn(number):
        pltpu.make_async_copy(gradients[number], line, line_sem).wait()
        turned[...] = jnp.transpose(line[...].reshape(-1, mid_width))
        if number + 1 < len(gradients):
            pltpu.make_async_copy(gradients[number + 1], line, line_sem).start()

    load(0).start()
    pltpu.make_async_copy(gradients[0], line, line_sem).start()
    inner = pl.ds(ring, GRID)
    for index, source in enumerate((modulated, change)):
        for side in (slice(0, ring), slice(GRID + ring, GRID + 2 * ring)):
            pads[index, side] = jnp.zeros((ring, GRID + 2 * ring, slots, mid_width), bf16)
            pads[index, ring : GRID + ring, side] = jnp.zeros((GRID, ring, slots, mid_width), bf16)
        pltpu.make_async_copy(source, pads.at[index, inner, inner], pad_sem.at[index]).start()
    place.greet()

    def flow(*hops):
        for k, lag in hops:
            scatter.hop(k, lag)

    def piece(number):
        if number + 1 < len(sources):
            load(number + 1).start()
        load(number).wait()
        return dot(turned[...], chunk[number % 2].reshape(-1, step))

    def reduce_pieces(first, last):
        for j in range(first, last):
            terms[1][j * step : (j + 1) * step, :] = jnp.transpose(piece(j)).astype(bf16)

    def expand_pieces(first, last):
        for j in range(first, last):
            terms[2][:, j * step : (j + 1) * step] = piece(chunks + j).astype(bf16)

    def taps(k, pad, stride, first, last):
        def tap(t, _):
            top = ring + (t // 3 - 1) * stride
            left = ring + (t % 3 - 1) * stride
            source = pads[pad, pl.ds(top, GRID), pl.ds(left, GRID)].reshape(-1, mid_width)
            values = dot(turned[...], source)
            start = pl.multiple_of(t * mid_width, mid_width)
            terms[k][pl.ds(start, mid_width), :] = jnp.transpose(values).astype(bf16)
            return 0

        lax.fori_loop(first, last, tap, 0)

    def padded(pad):
        pltpu.make_async_copy((modulated, change)[pad], pads.at[pad, inner, inner], pad_sem.at[pad]).wait()

    half = chunks // 2
    small_copy.wait()
    scatter.cores(0)
    turn(0)
    padded(0)
    taps(3, 0, 1, 0, 3)
    flow((0, 0))
    taps(3, 0, 1, 3, 6)
    flow((0, 1))
    taps(3, 0, 1, 6, 9)
    scatter.cores(3)
    turn(1)
    padded(1)
    taps(4, 1, 1, 0, 2)
    flow((3, 0), (0, 2))
    taps(4, 1, 1, 2, 6)
    flow((0, 3))
    taps(4, 1, 1, 6, 9)
    scatter.cores(4)
    taps(5, 1, 2, 0, 2)
    flow((4, 0), (3, 1))
    taps(5, 1, 2, 2, 6)
    taps(5, 1, 2, 6, 9)
    scatter.cores(5)
    turn(2)
    reduce_pieces(0, 2)
    flow((5, 0), (3, 2), (4, 1))
    reduce_pieces(2, chunks)
    scatter.cores(1)
    turn(3)
    expand_pieces(0, half)
    flow((1, 0), (4, 2), (3, 3))
    expand_pieces(half, chunks)
    scatter.cores(2)
    flow((5, 1), (2, 0), (1, 1), (5, 2), (4, 3), (2, 1), (1, 2), (5, 3), (2, 2), (1, 3), (2, 3))
    scatter.finish(totals)


def terms_all(small, block_low, grad_reduced, act_two, grad_expanded, modulated, grad_middle, change, grad_gate, rows, stem_rows, stem_depth, fsdp, reps, collective_id):
    dims = factor_three(fsdp)
    lines, line_rows, width = block_low.shape
    mid_width = act_two.shape[-1]
    slots = modulated.shape[2]
    shapes = [(rows[0], width), (rows[1], mid_width), (rows[2], width)] + [(rows[3], mid_width)] * 3
    rows = [rows[0], rows[1], rows[2], rows[3], rows[3], rows[3]]
    side = GRID + 4
    return pl.pallas_call(
        functools.partial(terms_kernel, dims, reps, rows),
        out_shape=[
            jax.ShapeDtypeStruct(shape, f32)
            for shape in [(stem_rows, width), (stem_rows, stem_depth), (1, mid_width // fsdp)] + shapes[1:4] + [(2,) + shapes[4]]
        ],
        in_specs=[ANY] * 9,
        out_specs=[IN_VMEM] * 7,
        scratch_shapes=[pltpu.VMEM((fsdp * a, b), bf16) for a, b in shapes]
        + [
            pltpu.VMEM((2, side, side, slots, mid_width), bf16),
            pltpu.VMEM((lines, line_rows, mid_width), bf16),
            pltpu.VMEM((mid_width, lines * line_rows), bf16),
            pltpu.VMEM((2, lines, line_rows, 256), bf16),
            DMA((2,)), DMA(()), DMA((2,)), DMA(()),
        ]
        + scatter_buffers(dims, reps, shapes),
        compiler_params=pltpu.CompilerParams(
            collective_id=collective_id, has_side_effects=True, vmem_limit_bytes=VMEM_LIMIT
        ),
        name="terms",
    )(small, block_low, grad_reduced, act_two, grad_expanded, modulated, grad_middle, change, grad_gate)


class Gather:
    def __init__(self, dims, reps, shards, fulls, buffers):
        self.dims, self.reps, self.shards, self.fulls = dims, reps, shards, fulls
        self.own_sem, self.a_sem, self.b_sem, self.c_sem, self.r_sem = buffers
        self.place = Place(dims, reps)
        self.waits, self.local = [], []

    def slot(self, k, da, du, dv, which):
        full = self.fulls[k]
        index = self.place.at(-(da or 0), -du, -dv)
        others = self.dims[1] * self.dims[2]
        cols = columns(full.shape[-1] // self.reps, which)
        if da is None:
            return full.at[:, index % others, :, cols]
        return full.at[index // others, index % others, :, cols]

    def push(self, k, da, du, dv, target, target_rep, sems):
        there = self.slot(k, da, du, dv, self.place.rep)
        if (da, du, dv) == (0, 0, 0):
            source = self.shards[k].at[:, columns(self.shards[k].shape[-1] // self.reps, self.place.rep)]
        else:
            source = there
        copy = remote(source, there, sems, target, target_rep)
        copy.start()
        self.waits.append(copy)

    def landed(self, k, da, du, dv, which, sems):
        there = self.slot(k, da, du, dv, which)
        remote(there, there, sems, self.place.me, self.place.rep).wait_recv()

    def along_u(self, k, da):
        for d in range(1, self.dims[1]):
            self.push(k, da, 0, 0, self.place.at(0, d, 0), self.place.rep, self.b_sem.at[k, da, d - 1])

    def along_v(self, k, da, du):
        for d in range(1, self.dims[2]):
            self.push(k, da, du, 0, self.place.at(0, 0, d), self.place.rep, self.c_sem.at[k, da or 0, du, d - 1])

    def to_reps(self, k, da, du, dv):
        for d in range(1, self.reps):
            self.push(
                k, da, du, dv, self.place.me, (self.place.rep + d) % self.reps, self.r_sem.at[k, da or 0, du, dv, d - 1]
            )

    def begin(self, k):
        place = self.place
        others = self.dims[1] * self.dims[2]
        copy = pltpu.make_async_copy(self.shards[k], self.fulls[k].at[place.me // others, place.me % others], self.own_sem.at[k])
        copy.start()
        self.local.append(copy)
        for d in range(1, self.dims[0]):
            self.push(k, 0, 0, 0, place.at(d, 0, 0), place.rep, self.a_sem.at[k, d - 1])
        self.along_u(k, 0)
        self.along_v(k, 0, 0)

    def hop(self, k, lag):
        size_a, size_b, size_c = self.dims
        reps, rep = self.reps, self.place.rep
        if lag == 0:
            for da in range(1, size_a):
                self.landed(k, da, 0, 0, rep, self.a_sem.at[k, da - 1])
                self.along_u(k, da)
                self.along_v(k, da, 0)
                self.to_reps(k, da, 0, 0)
        elif lag == 1:
            for du in range(1, size_b):
                for da in range(size_a):
                    self.landed(k, da, du, 0, rep, self.b_sem.at[k, da, du - 1])
                self.along_v(k, None, du)
                self.to_reps(k, None, du, 0)
        elif lag == 2:
            for dv in range(1, size_c):
                for du in range(size_b):
                    for da in range(size_a) if du == 0 else (None,):
                        self.landed(k, da, du, dv, rep, self.c_sem.at[k, da or 0, du, dv - 1])
                    self.to_reps(k, None, du, dv)
        else:
            for dv in range(size_c):
                for du in range(size_b):
                    for da in range(1, size_a) if du == dv == 0 else (None,):
                        for d in range(1, reps):
                            self.landed(k, da, du, dv, (rep + reps - d) % reps, self.r_sem.at[k, da or 0, du, dv, d - 1])
            self.local[k].wait()

    def finish(self):
        for copy in self.waits:
            copy.wait_send()


def gather_buffers(dims, reps, count):
    size_a, size_b, size_c = dims
    return [
        DMA((count,)),
        DMA((count, max(size_a - 1, 1), 2)),
        DMA((count, size_a, max(size_b - 1, 1), 2)),
        DMA((count, size_a, size_b, max(size_c - 1, 1), 2)),
        DMA((count, size_a, size_b, size_c, max(reps - 1, 1), 2)),
    ]


def head_kernel(dims, reps, sizes, stem_rows, *refs):
    stem_own, reduce_own, diff_own, mid_own, expand_own = refs[:5]
    lateral_own, wide_own, narrow_own, least_own, lhs, valid, pair, count, features = refs[5:14]
    (lateral_out, vector_out, reduce_out, diff_first, diff_second, mid_out, expand_out, block_in, block_low, stem_normed, pool_low, stem_inverse,
     number_out, normed_one, inverse_one, act_one, change) = refs[14:31]
    (small_own, small, stem_taps, reduce_full, tap_rows, lateral, stem_values, stem_act, loaded, wide, low, reduced) = refs[31:43]
    load_sem, wide_sem, low_sem, out_sem = refs[43:47]
    gather = Gather(
        dims, reps, [small_own, stem_own, reduce_own, diff_own.at[0], diff_own.at[1], mid_own, expand_own],
        [small, stem_taps, reduce_full, diff_first, diff_second, mid_out, expand_out], refs[47:52],
    )
    over = Exchange(sizes, reps, refs[52:])
    others = small.shape[1]
    fsdp = small.shape[0] * others
    me = gather.place.me
    stem_width = stem_rows * fsdp
    lines, rows, mid_width = reduced.shape
    clips, pixels, segs, width = features.shape
    slots = valid.shape[0]
    groups = rows // slots
    step = 256
    chunks = width // step
    mask = valid[:, :1].reshape(1, slots, 1)
    pairs = pair[:, :1].reshape(1, slots, 1)
    own = count[:, :1]

    def load(j):
        cols = slice(j * step, (j + 1) * step)
        return [
            pltpu.make_async_copy(
                features.at[clip, :, :, cols], loaded.at[j % 2, :, clip * segs : (clip + 1) * segs, :], load_sem.at[j % 2, clip]
            )
            for clip in range(clips)
        ]

    def grouped(values):
        return values.reshape(groups, slots, values.shape[-1])

    def moments(carry, origin):
        away, squares = whole_row(carry[0]), whole_row(carry[1])
        return [away + own * origin, jnp.maximum(squares - away * away / own, 0.0), count[...]]

    def add_moments(carry, values, origin):
        off = (grouped(values) - origin.reshape(1, 1, -1)) * mask
        return carry[0] + fold_rows(off), carry[1] + fold_rows(off * off)

    def blank(n):
        return jnp.zeros((8, n), f32), jnp.zeros((8, n), f32)

    for copy in load(0):
        copy.start()

    def placed(values, length):
        share = values.shape[1]
        one = lax.broadcasted_iota(jnp.int32, (share, length), 1) - me * share
        hot = (one == lax.broadcasted_iota(jnp.int32, (share, length), 0)).astype(f32).astype(bf16)
        return dot(values, hot)

    least = placed(least_own[...], LANES * -(-stem_width // LANES))
    narrow = placed(narrow_own[...], mid_width)
    pieces = [narrow[n : n + 1] for n in range(narrow.shape[0])] + [least[n : n + 1] for n in range(least.shape[0])]
    joined = jnp.concatenate(pieces, axis=1)
    joined = jnp.concatenate([joined, jnp.zeros((1, -joined.shape[1] % width), f32)], axis=1)
    small_rows = [lateral_own[...].astype(f32), placed(wide_own[...], width)]
    small_rows += [joined[:, n * width : (n + 1) * width] for n in range(joined.shape[1] // width)]
    taken = sum(row.shape[0] for row in small_rows)
    small_rows.append(jnp.zeros((small_own.shape[0] - taken, width), f32))
    small_own[...] = jnp.concatenate(small_rows, axis=0).astype(bf16)
    gather.place.greet(over.peers)
    gather.begin(0)
    gather.begin(1)
    gather.begin(2)
    gather.begin(3)
    gather.begin(4)
    gather.begin(5)
    gather.begin(6)
    stem_act[...] = jnp.zeros(stem_act.shape, f32)
    gather.hop(0, 0)
    gather.hop(1, 0)
    gather.hop(0, 1)
    gather.hop(1, 1)
    gather.hop(0, 2)
    gather.hop(1, 2)
    gather.hop(0, 3)
    gather.hop(1, 3)
    vectors = jnp.zeros((taken - stem_rows, width), f32)
    for device in range(fsdp):
        values = small[device // others, device % others].astype(f32)
        span = slice(device * stem_rows, (device + 1) * stem_rows)
        lateral[span, :] = values[:stem_rows]
        vectors = vectors + values[stem_rows:taken]
        taps = stem_taps[device // others, device % others].astype(f32)
        for x in range(GRID):
            tap_rows[x, span, :] = taps[x * stem_rows : (x + 1) * stem_rows]
    lateral_low = lateral[...].astype(bf16)
    vector_out[...] = vectors
    lateral_out[...] = lateral_low

    def vector(position, length):
        row, start = 2 + position // width, position % width
        return vectors[row : row + 1, start : start + length]

    gain_one, shift_one = vector(0, mid_width), vector(mid_width, mid_width)
    start = mid_width * narrow.shape[0]
    stem_gain, stem_shift = vector(start, stem_width), vector(start + least.shape[1], stem_width)
    gather.hop(2, 0)
    gather.hop(3, 0)
    gather.hop(2, 1)

    def stem_column(x, _):
        stem_values[x] = dot_t(lhs[...], tap_rows[x].astype(bf16))
        return 0

    lax.fori_loop(0, GRID, stem_column, 0)
    origin = stem_values[0, 0:1, :]
    carry = lax.fori_loop(0, GRID, lambda x, c: add_moments(c, stem_values[x], origin), blank(stem_width))
    gather.hop(4, 0)
    gather.hop(3, 1)
    total, squares, number = over.total(0, moments(carry, origin), True)
    number_out[...] = number
    number = number[:, :1]
    centre, inverse = total / number, lax.rsqrt(squares / number + epsilon)
    stem_inverse[...] = inverse
    gather.hop(5, 0)
    gather.hop(2, 2)
    gather.hop(4, 1)

    def stem_norm(x, _):
        normed = (stem_values[x] - centre) * inverse
        stem_normed[:, x] = grouped(normed)
        zeta = mask * (grouped(normed) * stem_gain.reshape(1, 1, -1) + stem_shift.reshape(1, 1, -1))
        stem_act[x + 1, 1 : GRID + 1] = gelu_parts(zeta)[0]
        return 0

    lax.fori_loop(0, GRID, stem_norm, 0)

    def stem_pool(x, _):
        total = stem_act[x] + stem_act[x + 1] + stem_act[x + 2]
        total = total[0:GRID] + total[1 : GRID + 1] + total[2 : GRID + 2]
        pool_low[:, x] = (total / 9.0).astype(bf16)
        return 0

    lax.fori_loop(0, GRID, stem_pool, 0)
    gather.hop(2, 3)

    later = [[], [(6, 0)], [(5, 1)], [], [(6, 1)], [(3, 2)], [], [(4, 2)]]
    for j in range(chunks):
        slot = j % 2
        cols = slice(j * step, (j + 1) * step)
        for copy in load(j + 1) if j + 1 < chunks else ():
            copy.start()
        for copy in load(j):
            copy.wait()
        out_wide = pltpu.make_async_copy(wide.at[slot], block_in.at[:, :, cols], wide_sem.at[slot])
        out_low = pltpu.make_async_copy(low.at[slot], block_low.at[:, :, cols], low_sem.at[slot])

        if j >= 2:
            out_wide.wait()
            out_low.wait()
        shares = step // reduce_full.shape[2]
        start = j * shares % others
        weight = reduce_full[j * shares // others, start : start + shares].reshape(step, mid_width)

        def line(y, _):
            values = loaded[slot, pl.ds(y * groups, groups)].astype(f32).reshape(rows, step)
            values = values + dot(pool_low[y].reshape(rows, stem_width), lateral_low[:, cols])
            wide[slot, y] = values
            rounded = values.astype(bf16)
            low[slot, y] = rounded
            product = dot(rounded, weight)
            reduced[y] = product if j == 0 else reduced[y] + product
            return 0

        lax.fori_loop(0, lines, line, 0)
        out_wide.start()
        out_low.start()
        for k, lag in later[j] if j < len(later) else ():
            gather.hop(k, lag)
    pltpu.make_async_copy(reduce_full, reduce_out, out_sem).start()

    origin = reduced[0, 0:1, :]
    carry = lax.fori_loop(0, lines, lambda y, c: add_moments(c, reduced[y], origin), blank(mid_width))
    total, squares, _ = over.total(1, moments(carry, origin), True)
    centre, inverse = total / number, lax.rsqrt(squares / number + epsilon)
    inverse_one[...] = inverse
    gather.hop(5, 2)

    def first(y, _):
        normed = (reduced[y] - centre) * inverse
        normed_one[y] = normed
        zeta = mask * (grouped(normed) * gain_one.reshape(1, 1, -1) + shift_one.reshape(1, 1, -1))
        act = gelu_parts(zeta)[0].reshape(rows, mid_width)
        act_one[y] = act
        change[y] = (pairs * grouped(pltpu.roll(act, rows - 1, 0) - act)).astype(bf16).reshape(rows, mid_width)
        return 0

    lax.fori_loop(0, lines, first, 0)
    gather.hop(6, 2)
    for k in range(3, 7):
        gather.hop(k, 3)
    for j in (chunks - 2, chunks - 1):
        cols = slice(j * step, (j + 1) * step)
        pltpu.make_async_copy(wide.at[j % 2], block_in.at[:, :, cols], wide_sem.at[j % 2]).wait()
        pltpu.make_async_copy(low.at[j % 2], block_low.at[:, :, cols], low_sem.at[j % 2]).wait()
    pltpu.make_async_copy(reduce_full, reduce_out, out_sem).wait()
    gather.finish()
    over.finish()


def head(stem_taps, reduce_weight, diff_weight, mid_weight, expand_weight, lateral, wide, narrow, least, lhs, valid, pair, count, features, fsdp, reps, collective_id):
    dims, sizes = factor_three(fsdp), stage_sizes(fsdp * reps)
    split = (dims[0], dims[1] * dims[2])
    shape = jax.ShapeDtypeStruct
    clips, pixels, segs, width = features.shape
    slots = clips * segs
    mid_width = reduce_weight.shape[1]
    stem_rows = lateral.shape[0]
    stem_width = stem_rows * fsdp
    rows = GRID * slots
    step = 256
    side = GRID + 2
    lengths = narrow.shape[0] * mid_width + least.shape[0] * (-(-stem_width // LANES) * LANES)
    vectors = 2 + -(-lengths // width)
    small = shape((-(-(stem_rows + vectors) // 16) * 16, width), bf16)

    def full(shard):
        return shape(shard.shape[:-2] + split + shard.shape[-2:], shard.dtype)

    def whole(shard):
        return pltpu.VMEM(split + shard.shape, shard.dtype)

    return pl.pallas_call(
        functools.partial(head_kernel, dims, reps, sizes, stem_rows),
        out_shape=[
            shape((stem_width, width), bf16), shape((vectors, width), f32),
            full(reduce_weight), *[full(shape(diff_weight.shape[1:], diff_weight.dtype))] * 2, full(mid_weight), full(expand_weight),
            shape((GRID, rows, width), f32), shape((GRID, rows, width), bf16),
            shape((GRID, GRID, slots, stem_width), f32), shape((GRID, GRID, slots, stem_width), bf16),
            shape((1, stem_width), f32), shape((1, LANES), f32),
            shape((GRID, rows, mid_width), f32), shape((1, mid_width), f32), shape((GRID, rows, mid_width), f32),
            shape((GRID, rows, mid_width), bf16),
        ],
        in_specs=[ANY] * 5 + [IN_VMEM] * 8 + [ANY],
        out_specs=[IN_VMEM] * 2 + [ANY] * 7 + [IN_VMEM] * 8,
        scratch_shapes=[
            pltpu.VMEM(small.shape, bf16), whole(small), whole(stem_taps), whole(reduce_weight),
            pltpu.VMEM((GRID, stem_width, stem_taps.shape[1]), f32), pltpu.VMEM((stem_width, width), f32),
            pltpu.VMEM((GRID, rows, stem_width), f32), pltpu.VMEM((side, side, slots, stem_width), f32),
            pltpu.VMEM((2, pixels, slots, step), bf16),
            pltpu.VMEM((2, GRID, rows, step), f32), pltpu.VMEM((2, GRID, rows, step), bf16),
            pltpu.VMEM((GRID, rows, mid_width), f32),
            DMA((2, clips)), DMA((2,)), DMA((2,)), DMA(()),
        ] + gather_buffers(dims, reps, 7) + exchange_buffers(sizes, 2, 2 * mid_width + LANES),
        compiler_params=pltpu.CompilerParams(
            collective_id=collective_id, has_side_effects=True, vmem_limit_bytes=VMEM_LIMIT
        ),
        name="head",
    )(stem_taps, reduce_weight, diff_weight, mid_weight, expand_weight, lateral, wide, narrow, least, lhs, valid, pair, count, features)


def tail_kernel(sizes, reps, clip_count, *refs):
    (middle, expand, valid, spread, count, gain_two, shift_two, gain_three, shift_three, pooled_grad, block_in) = refs[:11]
    (pooled, grad_pre, grad_expanded, act_two, grad_middle, gain_three_sum, shift_three_sum, gain_two_sum, shift_two_sum) = refs[11:20]
    (wide, wide_grad, narrow, narrow_grad, block, low, totals, first, block_sem, pre_sem, low_sem) = refs[20:31]
    over = Exchange(sizes, reps, refs[31:])
    lines, rows, mid_width = middle.shape
    width = expand.shape[1]
    slots = valid.shape[0]
    segs = slots // clip_count
    groups = rows // slots
    step = 256
    chunks = width // step

    barrier = pltpu.get_barrier_semaphore()
    for target, rep in over.peers:
        pl.semaphore_signal(barrier, inc=1, device_id={"fsdp": target, "rep": rep}, device_id_type=MESH)

    def fetch(y, slot):
        return pltpu.make_async_copy(block_in.at[y], block.at[slot], block_sem.at[slot])

    fetch(0, 0).start()
    mask = valid[:, :1].reshape(1, slots, 1)
    own = count[:, :1]

    def grouped(values):
        return values.reshape(groups, slots, values.shape[-1])

    def moments(carry, origin):
        away, squares = whole_row(carry[0]), whole_row(carry[1])
        return away + own * origin, jnp.maximum(squares - away * away / own, 0.0)

    def gather_moments(carry, values, origin):
        off = (grouped(values) - origin.reshape(1, 1, -1)) * mask
        return carry[0] + fold_rows(off), carry[1] + fold_rows(off * off)

    def blank(n):
        return jnp.zeros((8, n), f32), jnp.zeros((8, n), f32)

    origin = middle[0, 0:1, :]
    carry = lax.fori_loop(0, lines, lambda y, c: gather_moments(c, middle[y], origin), blank(mid_width))
    pl.semaphore_wait(barrier, len(over.peers))
    total, squares, number = over.total(0, list(moments(carry, origin)) + [count[...]], True)
    number = number[:, :1]
    centre_two, inverse_two = total / number, lax.rsqrt(squares / number + epsilon)
    gain2, shift2 = gain_two[...], shift_two[...]

    def zeta_two(normed):
        return mask * (grouped(normed) * gain2.reshape(1, 1, -1) + shift2.reshape(1, 1, -1))

    def forward_two(y, _):
        normed = (middle[y] - centre_two) * inverse_two
        narrow[y] = normed
        act_two[y] = gelu_parts(zeta_two(normed))[0].astype(bf16).reshape(rows, mid_width)
        return 0

    lax.fori_loop(0, lines, forward_two, 0)

    def expand_chunk(j, _):
        cols = pl.ds(pl.multiple_of(j * step, step), step)
        weight = expand[:, cols]
        wide[:, :, cols] = dot(act_two[...].reshape(lines * rows, mid_width), weight).reshape(lines, rows, step)
        origin = wide[0, 0:1, cols]

        def line(y, carry):
            return gather_moments(carry, wide[y, :, cols], origin)

        total, squares = moments(lax.fori_loop(0, lines, line, blank(step)), origin)
        totals[0, :, cols] = total
        totals[1, :, cols] = squares
        return 0

    lax.fori_loop(0, chunks, expand_chunk, 0)
    total, squares, _ = over.total(1, [totals[0], totals[1], count[...]], True)
    totals[0] = total / number
    totals[1] = lax.rsqrt(squares / number + epsilon)
    for index in range(2):
        first[index] = jnp.zeros((8, width), f32)

    def out_pre(y):
        return pltpu.make_async_copy(wide_grad.at[y], grad_pre.at[y], pre_sem.at[y])

    def forward_three(y, _):
        slot = y % 2
        fetch(y, slot).wait()

        @pl.when(y + 1 < lines)
        def _():
            fetch(y + 1, 1 - slot).start()

        def chunk(j, _):
            cols = pl.ds(pl.multiple_of(j * step, step), step)
            normed = (wide[y, :, cols] - totals[0, :, cols]) * totals[1, :, cols]
            wide[y, :, cols] = normed
            normed = grouped(normed)
            scaled = mask * (gain_three[:, cols].reshape(1, 1, step) * normed + shift_three[:, cols].reshape(1, 1, step))
            out, slope = gelu_parts(grouped(block[slot, :, cols]) + scaled)
            grads = []
            for clip in range(clip_count):
                span = slice(clip * segs, (clip + 1) * segs)
                share = spread[span, :1].reshape(1, segs, 1)
                pixels = pl.ds(y * groups, groups)
                pooled[clip, pixels, :, cols] = jnp.sum(out[:, span] * share, axis=1, keepdims=True)
                grads.append(slope[:, span] * (pooled_grad[clip, pixels, :, cols] * share))
            grad = jnp.concatenate(grads, axis=1)
            wide_grad[y, :, cols] = grad.reshape(rows, step)
            first[0, :, cols] += fold_rows(grad)
            first[1, :, cols] += fold_rows(grad * normed)
            return 0

        lax.fori_loop(0, chunks, chunk, 0)
        out_pre(y).start()
        return 0

    lax.fori_loop(0, lines, forward_three, 0)
    shift_sum, gain_sum = over.total(2, [whole_row(first[0]), whole_row(first[1])], False)
    shift_three_sum[...] = shift_sum
    gain_three_sum[...] = gain_sum
    totals[2] = shift_sum / number
    totals[3] = gain_sum / number
    totals[1] = totals[1] * gain_three[...]

    def out_low(y):
        return pltpu.make_async_copy(low.at[y], grad_expanded.at[y], low_sem.at[y])

    def back_three(y, _):
        def chunk(j, _):
            cols = pl.ds(pl.multiple_of(j * step, step), step)
            grad = wide_grad[y, :, cols] - totals[2, :, cols] - wide[y, :, cols] * totals[3, :, cols]
            low[y, :, cols] = (mask * grouped(grad * totals[1, :, cols])).astype(bf16).reshape(rows, step)
            return 0

        lax.fori_loop(0, chunks, chunk, 0)
        out_low(y).start()
        return 0

    lax.fori_loop(0, lines, back_three, 0)
    for start in range(0, mid_width, step):
        values = dot_t(low[...].reshape(lines * rows, width), expand[start : start + step, :])
        narrow_grad[:, :, start : start + step] = values.reshape(lines, rows, step)

    def slopes(y, carry):
        normed = narrow[y]
        grad = grouped(narrow_grad[y]) * gelu_parts(zeta_two(normed))[1] * mask
        narrow_grad[y] = grad.reshape(rows, mid_width)
        return carry[0] + fold_rows(grad), carry[1] + fold_rows(grad * grouped(normed))

    carry = lax.fori_loop(0, lines, slopes, blank(mid_width))
    shift_sum, gain_sum = over.total(3, [whole_row(carry[0]), whole_row(carry[1])], False)
    shift_two_sum[...] = shift_sum
    gain_two_sum[...] = gain_sum
    shift_mean, gain_mean, scale = shift_sum / number, gain_sum / number, inverse_two * gain2

    def back_two(y, _):
        grad = (narrow_grad[y] - shift_mean - narrow[y] * gain_mean) * scale
        grad_middle[y] = (mask * grouped(grad)).astype(bf16).reshape(rows, mid_width)
        return 0

    lax.fori_loop(0, lines, back_two, 0)
    lax.fori_loop(0, lines, lambda y, _: (out_pre(y).wait(), 0)[1], 0)
    lax.fori_loop(0, lines, lambda y, _: (out_low(y).wait(), 0)[1], 0)
    over.finish()


def tail(middle, expand, valid, spread, count, gain_two, shift_two, gain_three, shift_three, pooled_grad, block_in, clip_count, fsdp, reps, collective_id):
    sizes = stage_sizes(fsdp * reps)
    lines, rows, mid_width = middle.shape
    width = expand.shape[1]
    pixels = pooled_grad.shape[1]
    shape = jax.ShapeDtypeStruct
    return pl.pallas_call(
        functools.partial(tail_kernel, sizes, reps, clip_count),
        out_shape=[
            shape((clip_count, pixels, 1, width), f32), shape((lines, rows, width), f32), shape((lines, rows, width), bf16),
            shape((lines, rows, mid_width), bf16), shape((lines, rows, mid_width), bf16),
            shape((1, width), f32), shape((1, width), f32), shape((1, mid_width), f32), shape((1, mid_width), f32),
        ],
        in_specs=[IN_VMEM] * 10 + [ANY],
        out_specs=[IN_VMEM, ANY, ANY] + [IN_VMEM] * 6,
        scratch_shapes=[
            pltpu.VMEM((lines, rows, width), f32), pltpu.VMEM((lines, rows, width), f32),
            pltpu.VMEM((lines, rows, mid_width), f32), pltpu.VMEM((lines, rows, mid_width), f32),
            pltpu.VMEM((2, rows, width), f32), pltpu.VMEM((lines, rows, width), bf16),
            pltpu.VMEM((4, 1, width), f32), pltpu.VMEM((2, 8, width), f32),
            DMA((2,)), DMA((lines,)), DMA((lines,)),
        ] + exchange_buffers(sizes, 4, 2 * width + LANES),
        compiler_params=pltpu.CompilerParams(collective_id=collective_id, has_side_effects=True, vmem_limit_bytes=VMEM_LIMIT),
        name="tail",
    )(middle, expand, valid, spread, count, gain_two, shift_two, gain_three, shift_three, pooled_grad, block_in)


def back_kernel(clips, *refs):
    grad_reduced, reduce_full, pool_low, lateral, grad_pre = refs[:5]
    features_grad, lateral_terms, grad_act = refs[5:8]
    loaded, sums, low, total, load_sem, out_sem = refs[8:]
    lines, rows, mid_width = grad_reduced.shape
    width = reduce_full.shape[0]
    groups = GRID
    slots = rows // groups
    segs = slots // clips
    step = 512

    def load(y):
        return pltpu.make_async_copy(grad_pre.at[y], loaded.at[y % 2], load_sem.at[y % 2])

    def store(y):
        slot = y % 2
        return [
            pltpu.make_async_copy(
                sums.at[slot, :, clip * segs : (clip + 1) * segs, :],
                features_grad.at[clip, pl.ds(y * groups, groups)],
                out_sem.at[slot, clip],
            )
            for clip in range(clips)
        ]

    load(0).start()
    total[...] = jnp.zeros(total.shape, f32)

    def line(y, _):
        slot = y % 2
        load(y).wait()

        @pl.when(y + 1 < lines)
        def _():
            load(y + 1).start()

        @pl.when(y >= 2)
        def _():
            for copy in store(y - 2):
                copy.wait()

        for start in range(0, width, step):
            cols = slice(start, start + step)
            values = loaded[slot, :, cols] + dot_t(grad_reduced[y], reduce_full[cols, :])
            sums[slot, :, :, cols] = values.reshape(groups, slots, step)
            low[:, cols] = values.astype(bf16)
        for copy in store(y):
            copy.start()
        grad_act[y] = dot_t(low[...], lateral[...])
        turned = jnp.transpose(pool_low[y])
        for start in range(0, width, step):
            cols = slice(start, start + step)
            total[:, cols] += dot(turned, low[:, cols])
        return 0

    lax.fori_loop(0, lines, line, 0)
    lateral_terms[...] = total[...].astype(bf16)
    for y in (lines - 2, lines - 1):
        for copy in store(y):
            copy.wait()


def back(grad_reduced, reduce_full, pool_low, lateral, grad_pre, clips):
    lines, rows, mid_width = grad_reduced.shape
    width = reduce_full.shape[0]
    slots = rows // GRID
    stem_width = lateral.shape[0]
    shape = jax.ShapeDtypeStruct
    return pl.pallas_call(
        functools.partial(back_kernel, clips),
        out_shape=[
            shape((clips, lines * GRID, slots // clips, width), f32), shape((stem_width, width), bf16),
            shape((lines, rows, stem_width), f32),
        ],
        in_specs=[IN_VMEM] * 4 + [ANY],
        out_specs=[ANY, IN_VMEM, IN_VMEM],
        scratch_shapes=[
            pltpu.VMEM((2, rows, width), f32), pltpu.VMEM((2, GRID, slots, width), f32), pltpu.VMEM((rows, width), bf16),
            pltpu.VMEM((stem_width, width), f32), DMA((2,)), DMA((2, clips)),
        ],
        compiler_params=pltpu.CompilerParams(vmem_limit_bytes=VMEM_LIMIT),
        cost_estimate=pl.CostEstimate(flops=4 * lines * rows * width * mid_width, bytes_accessed=8 * lines * rows * width, transcendentals=0),
        name="back",
    )(grad_reduced, reduce_full, pool_low, lateral, grad_pre)


ORDER = ("HWNC", "HWIO", "HWNC")


def pad_of(span):
    return ((span, span), (span, span))


def convolve(source, weight, span, stride):
    side = 2 * span + 1
    kernel = weight.reshape(side, side, source.shape[-1], -1)
    return lax.conv_general_dilated(
        source, kernel, (1, 1), pad_of(span * stride), rhs_dilation=(stride, stride),
        dimension_numbers=ORDER, preferred_element_type=f32,
    )


def convolve_back(grads, weight, span, stride):
    side = 2 * span + 1
    kernel = weight.reshape(side, side, -1, grads.shape[-1])[::-1, ::-1]
    return lax.conv_general_dilated(
        grads, kernel, (1, 1), pad_of(span * stride), rhs_dilation=(stride, stride),
        dimension_numbers=("HWNC", "HWOI", "HWNC"), preferred_element_type=f32,
    )


def convolve_terms(source, grads, span, stride, kind):
    return lax.conv_general_dilated(
        source, grads, (stride, stride), pad_of(span * stride),
        dimension_numbers=("HWCN", "HWIO", "HWNC"), preferred_element_type=kind,
    )


def pool_mean(source):
    total = lax.reduce_window(source, 0.0, lax.add, (3, 3, 1, 1), (1, 1, 1, 1), "SAME")
    return total / 9.0


def project(source, weight):
    return jnp.einsum("yxnc,cd->yxnd", source, weight, preferred_element_type=f32)


def project_back(grads, weight):
    return jnp.einsum("yxnd,cd->yxnc", grads, weight, preferred_element_type=f32)


def project_terms(source, grads, kind):
    return jnp.einsum("yxnc,yxnd->cd", source, grads, preferred_element_type=kind)


def gelu_back(pre_act, grads):
    return jax.vjp(jax.nn.gelu, pre_act)[1](grads)[0]


def make_shards(fsdp, reps):
    def shards(
        frames, features, seg_counts, stem_weight, stem_gain, stem_shift, lateral, reduce_weight,
        gain_one, shift_one, diff_weight, gate_shift, mid_weight, gain_two, shift_two,
        expand_weight, gain_three, shift_three, pooled_grad,
    ):
        clip_count, seg_slots, pixels, feature_width = features.shape
        slots = clip_count * seg_slots
        mid_width = reduce_weight.shape[1]
        stem_rows, stem_depth = stem_weight.shape
        stem_width = stem_rows * fsdp

        seg_index = lax.broadcasted_iota(jnp.int32, (clip_count, seg_slots), 1)
        valid_seg = (seg_index < seg_counts[:, None]).astype(f32)
        pair_seg = valid_seg * jnp.concatenate(
            [valid_seg[:, 1:], jnp.zeros((clip_count, 1), f32)], axis=1
        )
        valid = valid_seg.reshape(1, 1, slots, 1)
        pair = pair_seg.reshape(1, 1, slots, 1)
        count_float = seg_counts.astype(f32)
        local_count = jnp.sum(count_float) * pixels

        taps = jnp.pad(stem_weight.reshape(stem_rows, GRID, GRID, -1), ((0, 0), (0, 0), (3, 3), (0, 0)))
        taps = jnp.stack([taps[:, :, 6 - x : 13 - x] for x in range(GRID)]).reshape(GRID * stem_rows, stem_depth)
        taps = jnp.pad(taps, ((0, -taps.shape[0] % 16), (0, -stem_depth % (LANES * reps))))
        moving = frames.astype(f32)
        motion = (moving[:, :, 1:] - moving[:, :, :-1]) * valid_seg[:, :, None, None, None]
        motion = jnp.transpose(motion.astype(bf16), (4, 0, 1, 2, 3)).reshape(GRID, GRID, slots, -1)
        strips = jnp.transpose(motion, (0, 2, 1, 3)).reshape(GRID, slots, -1)
        strips = jnp.pad(strips, ((3, 3), (0, 0), (0, 0)))
        strips = jnp.concatenate([strips[dy : dy + GRID] for dy in range(GRID)], axis=-1).reshape(GRID * slots, -1)
        strips = jnp.pad(strips, ((0, 0), (0, -stem_depth % (LANES * reps))))
        lanes = lambda column: jnp.broadcast_to(column.reshape(-1, 1), (column.size, LANES))
        (lateral_full, vectors, reduce_full, diff_first, diff_second, mid_full, expand_full, block_in, block_low, stem_normed, pool_low,
         stem_inverse, number, normed_one, inverse_one, act_one, change) = head(
            taps, reduce_weight, diff_weight, mid_weight, expand_weight, lateral, jnp.stack([gain_three, shift_three]),
            jnp.stack([gain_one, shift_one, gate_shift, gain_two, shift_two]), jnp.stack([stem_gain, stem_shift]),
            strips, lanes(valid_seg), lanes(pair_seg), lanes(local_count), jnp.transpose(features, (0, 2, 1, 3)),
            fsdp, reps, 1,
        )
        row = vectors[2:].reshape(-1)
        gain_one_full, shift_one_full, gate_full, gain_two_full, shift_two_full = (
            row[n * mid_width : (n + 1) * mid_width] for n in range(5)
        )
        gain_three_full, shift_three_full = vectors[0], vectors[1]
        start = 5 * mid_width
        stem_gain_full = row[start : start + stem_width]
        start += -(-stem_width // LANES) * LANES
        stem_shift_full = row[start : start + stem_width]
        reduce_full = reduce_full.reshape(-1, mid_width)
        diff_full = [diff_first.reshape(-1, mid_width), diff_second.reshape(-1, mid_width)]
        mid_full = mid_full.reshape(-1, mid_width)
        expand_full = expand_full.reshape(mid_width, -1)
        cube = (GRID, GRID, slots, -1)
        flat = (GRID, GRID * slots, -1)
        normed_one, act_one, change = normed_one.reshape(cube), act_one.reshape(cube), change.reshape(cube)
        stats_one = (None, inverse_one[0], number[0, 0])
        stem_stats = (None, stem_inverse[0], number[0, 0])
        zeta_one = valid * (gain_one_full * normed_one + shift_one_full)
        stem_norm = valid * (stem_gain_full * stem_normed + stem_shift_full)

        def norm_back(grad_out, normed, stats, gain, collective_id, name):
            masked = grad_out * valid
            shift_sum, gain_sum = exchange(
                [jnp.sum(masked, axis=(0, 1, 2)), jnp.sum(masked * normed, axis=(0, 1, 2))],
                fsdp, reps, False, collective_id, name,
            )
            grad_in = valid * stats[1] * gain * (masked - shift_sum / stats[2] - normed * gain_sum / stats[2])
            return grad_in.astype(bf16), gain_sum, shift_sum

        def earlier_of(values):
            grid = values.reshape(GRID, GRID, clip_count, seg_slots, -1)
            return jnp.pad(grid[:, :, :, :-1], ((0, 0), (0, 0), (0, 0), (1, 0), (0, 0))).reshape(values.shape)

        gate_pre = convolve(change, diff_full[0], 1, 1) + convolve(change, diff_full[1], 1, 2)
        gate = jax.nn.sigmoid(gate_pre + gate_full)
        modulated = (act_one * (1.0 + gate)).astype(bf16)
        middle = convolve(modulated, mid_full, 1, 1)
        (pooled, grad_pre, grad_expanded, act_two, grad_middle, gain_three_sum, shift_three_sum, gain_two_sum,
         shift_two_sum) = tail(
            middle.reshape(flat), expand_full, lanes(valid_seg), lanes(valid_seg / count_float[:, None]), lanes(local_count),
            gain_two_full[None], shift_two_full[None], gain_three_full[None], shift_three_full[None],
            pooled_grad.astype(f32)[:, :, None], block_in, clip_count, fsdp, reps, 4,
        )
        pooled = pooled.reshape(pooled_grad.shape).astype(bf16)
        gain_three_sum, shift_three_sum, gain_two_sum, shift_two_sum = (
            row[0] for row in (gain_three_sum, shift_three_sum, gain_two_sum, shift_two_sum)
        )
        grad_pre, grad_expanded, act_two, grad_middle = (
            block.reshape(cube) for block in (grad_pre, grad_expanded, act_two, grad_middle)
        )
        grad_modulated = convolve_back(grad_middle, mid_full, 1, 1)
        grad_gate_pre = grad_modulated * act_one * gate * (1.0 - gate)
        gate_terms = jnp.sum(grad_gate_pre, axis=(0, 1, 2))
        grad_gate = grad_gate_pre.astype(bf16)
        grad_change = convolve_back(grad_gate, diff_full[0], 1, 1) + convolve_back(grad_gate, diff_full[1], 1, 2)
        grad_change = grad_change * pair
        grad_act_one = grad_modulated * (1.0 + gate) + earlier_of(grad_change) - grad_change
        grad_reduced, gain_one_sum, shift_one_sum = norm_back(
            gelu_back(zeta_one, grad_act_one), normed_one, stats_one, gain_one_full, 8, "sums_one"
        )
        features_grad, lateral_terms, grad_act = back(
            grad_reduced.reshape(flat), reduce_full, pool_low.reshape(flat), lateral_full, grad_pre.reshape(flat), clip_count
        )
        grad_act = pool_mean(grad_act.reshape(cube))
        grad_stem, stem_gain_sum, stem_shift_sum = norm_back(
            gelu_back(stem_norm, grad_act), stem_normed, stem_stats, stem_gain_full, 9, "sums_stem"
        )
        stem_terms = convolve_terms(motion, grad_stem, 3, 1, bf16)
        stem_terms = jnp.transpose(stem_terms, (3, 0, 1, 2)).reshape(fsdp, stem_rows, stem_depth)
        gate_rows = gate_shift.shape[0]
        small_terms = jnp.concatenate(
            [
                lateral_terms.reshape(fsdp, stem_rows, feature_width),
                jnp.pad(stem_terms, ((0, 0), (0, 0), (0, feature_width - stem_depth))),
                jnp.pad(
                    gate_terms.astype(bf16).reshape(fsdp, 1, gate_rows),
                    ((0, 0), (0, 15 - 2 * stem_rows), (0, feature_width - gate_rows)),
                ),
            ],
            axis=1,
        )

        conv_rows = mid_weight.shape[0]
        if conv_rows % 32 == 0:
            lateral_part, stem_part, gate_part, reduce_part, expand_part, mid_part, diff_part = terms_all(
                small_terms.reshape(-1, feature_width), block_low, grad_reduced.reshape(flat),
                act_two.reshape(flat), grad_expanded.reshape(flat), modulated, grad_middle.reshape(flat), change,
                grad_gate.reshape(flat),
                [small_terms.shape[1], reduce_weight.shape[0], expand_weight.shape[0], conv_rows], stem_rows, stem_depth,
                fsdp, reps, 10,
            )
        else:
            def owned(terms, shard):
                return terms.reshape((fsdp,) + shard.shape[-2:])

            small_part, reduce_part, expand_part, mid_part, diff_one, diff_two = scatter_all(
                [
                    small_terms,
                    owned(project_terms(block_low.reshape(cube), grad_reduced, bf16), reduce_weight),
                    owned(project_terms(act_two, grad_expanded, bf16), expand_weight),
                    owned(convolve_terms(modulated, grad_middle, 1, 1, bf16), mid_weight),
                    owned(convolve_terms(change, grad_gate, 1, 1, bf16), diff_weight),
                    owned(convolve_terms(change, grad_gate, 1, 2, bf16), diff_weight),
                ],
                fsdp, reps, 11, "scatter_terms",
            )
            lateral_part, gate_part = small_part[:stem_rows], small_part[2 * stem_rows, :gate_rows]
            stem_part = small_part[stem_rows : 2 * stem_rows, :stem_depth]
            diff_part = jnp.stack([diff_one, diff_two])

        def own_share(whole):
            share = whole.shape[0] // fsdp
            return lax.dynamic_slice_in_dim(whole, lax.axis_index("fsdp") * share, share)

        out = jnp.transpose(features_grad, (0, 2, 1, 3))
        return (
            pooled,
            out,
            stem_part,
            own_share(stem_gain_sum),
            own_share(stem_shift_sum),
            lateral_part,
            reduce_part,
            own_share(gain_one_sum),
            own_share(shift_one_sum),
            diff_part,
            gate_part.reshape(-1),
            mid_part,
            own_share(gain_two_sum),
            own_share(shift_two_sum),
            expand_part,
            own_share(gain_three_sum),
            own_share(shift_three_sum),
        )

    return shards


def solution(mesh):
    whole = ("fsdp", "rep")
    matrix, vector = P("fsdp", None), P("fsdp")
    in_specs = (
        P(whole, None, None, None, None), P(whole, None, None, None), P(whole),
        matrix, vector, vector, matrix, matrix, vector, vector, P(None, "fsdp", None), vector,
        matrix, vector, vector, matrix, vector, vector, P(whole, None, None),
    )
    out_specs = (
        P(whole, None, None), P(whole, None, None, None), matrix, vector, vector, matrix, matrix,
        vector, vector, P(None, "fsdp", None), vector, matrix, vector, vector, matrix, vector, vector,
    )
    body = make_shards(mesh.shape["fsdp"], mesh.shape["rep"])
    return jax.shard_map(body, mesh=mesh, in_specs=in_specs, out_specs=out_specs, check_vma=False)
```
